512 devices in a mesh: seq: 128 (over y, z, core), head: 4 (over x).
Axes of the slice: x: 4, y: 4, z: 16, core: 2. Of those that a mesh axis runs over, the one named last changes fastest.
Arguments:
- values: bfloat16 [32768, 4096], P('seq', 'head'), may hold values from -6 to 6
- keys: bfloat16 [32768, 4096], P('seq', 'head'), may hold values from -0.59765625 to 0.59765625
- queries: bfloat16 [32768, 4096], P('seq', 'head'), may hold values from -6 to 6
- gates: bfloat16 [32768, 4096], P('seq', 'head'), may hold values from -6 to 6
- log_decay: float32 [32, 32768], P('head', 'seq'), may hold values from -1 to 0, as said below
- level_mix: float32 [8, 32, 32768], P(None, 'head', 'seq'), may hold values from 0.25 to 2
- norm_gain: bfloat16 [4096], P('head'), may hold values from 0.25 to 1.75
- out_weight_t: bfloat16 [4096, 4096], P('seq', 'head'), may hold values from -0.09375 to 0.09375
Outputs:
- mixed: bfloat16 [32768, 4096], P('seq', 'head')
The draws below stay inside these ranges and needn't reach their ends.
Inputs may be any that keep to these rules, and one draw needn't show every extreme that they name: `log_decay`: log decays are never positive; rates differ strongly between heads.
All inputs are finite; a program needn't handle non-finite values.
Results may differ from the reference program's by a relative error of at most 0.015.
Values may be sent and summed in bfloat16 or wider, within the bound.
No kernel may reach another device: no remote copies, remote signals or barrier semaphores. Data moves between devices by JAX's collectives and lax.ppermute only.
A program may use at most 64 MiB of HBM per device.

```python
import math
import jax
import jax.numpy as jnp
from jax import lax

D = 4096
HEAD_NUMBER = 32
P_SIZE = 128
N = 128
TOK_DEV = 256
TOKEN_NUMBER = 32768
LEVELS = 8
N_SEQ = 128


def draw_log_decay(key, part):
    key = jax.random.fold_in(key, 11)
    key_matrix_full = jax.random.split(key, 7)
    slow_share = 0.5
    slow = jax.random.uniform(key_matrix_full[0], (HEAD_NUMBER, 1)) < slow_share
    slow_rate = jnp.exp(jax.random.uniform(key_matrix_full[1], (HEAD_NUMBER, 1), minval=jnp.log(0.3 / TOKEN_NUMBER), maxval=jnp.log(2.0 / TOKEN_NUMBER)))
    fast_rate = jnp.exp(jax.random.uniform(key_matrix_full[2], (HEAD_NUMBER, 1), minval=jnp.log(1.0 / 400.0), maxval=jnp.log(1.0 / 30.0)))
    decay_speed = jnp.where(slow, slow_rate, fast_rate)
    coarse_state = jax.random.uniform(key_matrix_full[3], (HEAD_NUMBER, TOKEN_NUMBER), minval=0.3, maxval=1.7)
    shard_multiplier = jnp.exp(jax.random.uniform(key_matrix_full[4], (HEAD_NUMBER, TOKEN_NUMBER // TOK_DEV, 1), minval=jnp.log(0.5), maxval=jnp.log(2.0)))
    shard_multiplier = jnp.broadcast_to(shard_multiplier, (HEAD_NUMBER, TOKEN_NUMBER // TOK_DEV, TOK_DEV)).reshape(HEAD_NUMBER, TOKEN_NUMBER)
    decay_spike = jax.random.uniform(key_matrix_full[5], (HEAD_NUMBER, TOKEN_NUMBER)) < 8.0 / TOKEN_NUMBER
    level_depth = jnp.log(jax.random.uniform(key_matrix_full[6], (HEAD_NUMBER, TOKEN_NUMBER), minval=0.5, maxval=0.8))
    layer_output = -(decay_speed * coarse_state * shard_multiplier) + jnp.where(decay_spike, level_depth, 0.0)
    return layer_output.astype(jnp.float32)


def shard_levels(key, extent, pieces, low, high):
    level = 1.0
    for axis_at, parts in pieces:
        steps = jax.random.uniform(jax.random.fold_in(jax.random.fold_in(key, 6), axis_at), (parts,), jnp.float32, low / len(pieces), high / len(pieces))
        level = level * jnp.repeat(jnp.exp(steps), extent[axis_at] // parts).reshape((-1,) + (1,) * (len(extent) - 1 - axis_at))
    return level


def centred(own_key, dims, deviation, most, cuts=(), held_as=jnp.bfloat16):
    factor_of = shard_levels(own_key, dims, cuts, -0.22, 0.18) if cuts else 1.0
    drawn = jax.random.normal(own_key, dims, jnp.float32) * deviation * factor_of
    return jnp.minimum(jnp.maximum(drawn, -most), most).astype(held_as)


def setup_inputs(seed: int = 0) -> dict:
    arg_keys = jax.random.split(jax.random.key(seed), 9)
    return {
        "values": centred(arg_keys[0], (TOKEN_NUMBER, HEAD_NUMBER * P_SIZE), 1.0, 6.0, ((0, 128), (1, 4))),
        "keys": centred(arg_keys[1], (TOKEN_NUMBER, HEAD_NUMBER * N), 0.09, 0.59765625, ((0, 128), (1, 4))),
        "queries": centred(arg_keys[2], (TOKEN_NUMBER, HEAD_NUMBER * N), 1.0, 6.0, ((0, 128), (1, 4))),
        "gates": centred(arg_keys[3], (TOKEN_NUMBER, HEAD_NUMBER * P_SIZE), 1.0, 6.0, ((0, 128), (1, 4))),
        "log_decay": draw_log_decay(jax.random.fold_in(arg_keys[8], 71), 0),
        "level_mix": jnp.clip(jnp.exp(math.log(2.0) - 2.0794415 * jax.random.uniform(arg_keys[5], (LEVELS, HEAD_NUMBER, TOKEN_NUMBER), jnp.float32) ** shard_levels(arg_keys[5], (LEVELS, HEAD_NUMBER, TOKEN_NUMBER), ((1, 4), (2, 128)), -0.2, 0.2)), 0.25, 2.0),
        "norm_gain": jnp.clip(1.0 + 0.15 * jax.random.normal(arg_keys[6], (HEAD_NUMBER * P_SIZE,), jnp.float32), 0.25, 1.75).astype(jnp.bfloat16),
        "out_weight_t": centred(arg_keys[7], (D, HEAD_NUMBER * P_SIZE), (HEAD_NUMBER * P_SIZE) ** -0.5, 0.09375, ((0, 128), (1, 4))),
    }


def head_mix(x, b, c, z, a, lam, gain):
    shards = N_SEQ
    rows = TOK_DEV
    xr = x.reshape(shards, rows, P_SIZE).astype(jnp.float32)
    br = b.reshape(shards, rows, N).astype(jnp.float32)
    cr = c.reshape(shards, rows, N).astype(jnp.float32)
    ar = a.reshape(shards, rows)
    local = jnp.cumsum(ar, axis=1)
    total = lax.optimization_barrier(jnp.sum(ar, axis=1))
    scores = jnp.einsum('sln,smn->slm', cr, br)
    lower = jnp.arange(rows)[:, None] >= jnp.arange(rows)[None, :]
    gap = jnp.where(lower[None], local[:, :, None] - local[:, None, :], -jnp.inf)
    weights = (scores * jnp.exp(gap)).astype(jnp.bfloat16)
    own = jnp.einsum('slm,smp->slp', weights.astype(jnp.float32), xr)
    lamr = lam.reshape(LEVELS, shards, rows)
    mixture = own * lamr[0][:, :, None]
    scaled = (br * jnp.exp(total[:, None] - local)[:, :, None]).astype(jnp.bfloat16)
    ends = jnp.einsum('sln,slp->snp', scaled.astype(jnp.float32), xr)
    start_scale = jnp.exp(local)
    index = jnp.arange(shards)
    for level in range(1, LEVELS):
        size = 2 ** (level - 1)
        blocks = shards // size
        tr = total.reshape(blocks, size)
        within = jnp.cumsum(tr, axis=1)
        wblock = jnp.exp(within[:, -1:] - within)
        agg = jnp.einsum('bj,bjnp->bnp', wblock, ends.reshape(blocks, size, N, P_SIZE))
        prev = jnp.concatenate([jnp.zeros((1, N, P_SIZE), jnp.float32), agg[:-1]], axis=0)
        prev = jnp.repeat(prev, size, axis=0)
        pre = (within - tr).reshape(shards)
        flag = index // size % 2 == 1
        bucket = jnp.where(flag[:, None, None], prev * jnp.exp(pre)[:, None, None], 0.0).astype(jnp.bfloat16)
        read = jnp.einsum('sln,snp->slp', cr, bucket.astype(jnp.float32))
        mixture = mixture + read * (start_scale * lamr[level])[:, :, None]
    mixture = mixture.reshape(TOKEN_NUMBER, P_SIZE)
    gated = mixture * jax.nn.silu(z.astype(jnp.float32))
    rms = jnp.sqrt(lax.optimization_barrier(jnp.mean(gated * gated, axis=1, keepdims=True)) + 1e-05)
    return (gated / rms * gain.astype(jnp.float32)).astype(jnp.bfloat16)

def reference(values, keys, queries, gates, log_decay, level_mix, norm_gain, out_weight_t):
    xs = values.reshape(TOKEN_NUMBER, HEAD_NUMBER, P_SIZE).transpose(1, 0, 2)
    bs = keys.reshape(TOKEN_NUMBER, HEAD_NUMBER, N).transpose(1, 0, 2)
    cs = queries.reshape(TOKEN_NUMBER, HEAD_NUMBER, N).transpose(1, 0, 2)
    zs = gates.reshape(TOKEN_NUMBER, HEAD_NUMBER, P_SIZE).transpose(1, 0, 2)
    lams = level_mix.transpose(1, 0, 2)
    gains = norm_gain.reshape(HEAD_NUMBER, P_SIZE)

    def one_head(items):
        return head_mix(*items)
    normed = lax.map(one_head, (xs, bs, cs, zs, log_decay, lams, gains))
    normed = normed.transpose(1, 0, 2).reshape(TOKEN_NUMBER, HEAD_NUMBER * P_SIZE)
    out = lax.dot_general(normed, out_weight_t, (((1,), (1,)), ((), ())), preferred_element_type=jnp.float32)
    return out.astype(jnp.bfloat16)
```

```python
import jax
import jax.numpy as jnp
from jax import lax
from jax.sharding import Mesh, PartitionSpec as P

BF = jnp.bfloat16
F32 = jnp.float32
SEQ = ("y", "a", "b", "c")


def swap(value):
    return lax.ppermute(value, "c", [(0, 1), (1, 0)])


def flip(value, axis, mask):
    return lax.ppermute(value, axis, [(i, i ^ mask) for i in range(4)])


def halves(value, axis, core):
    size = value.shape[axis] // 2
    kept = lax.dynamic_slice_in_dim(value, core * size, size, axis)
    sent = lax.dynamic_slice_in_dim(value, (1 - core) * size, size, axis)
    return kept, sent


def in_order(kept, got, core):
    first = core == 0
    return jnp.stack([jnp.where(first, kept, got), jnp.where(first, got, kept)])


def tail(log):
    high = lax.reduce_precision(log, 8, 7)
    middle = lax.reduce_precision(log - high, 8, 7)
    terms = jnp.stack([high, middle, log - high - middle], axis=-1)
    rows = jnp.pad(terms, [(0, 0)] * log.ndim + [(0, 13)])
    return jnp.broadcast_to(rows[..., None], rows.shape + (128,)).astype(BF)


def untail(rows):
    return jnp.sum(rows[..., :3, 0].astype(F32), axis=-1)


def with_tail(state, log):
    return jnp.concatenate([state.astype(BF), tail(log)], axis=-2)


def split_tail(block):
    return block[..., :128, :], untail(block[..., 128:, :])


def exchange(block, axis):
    return lax.all_to_all(
        jnp.broadcast_to(block[None], (4,) + block.shape), axis, 0, 0, tiled=True
    )


def merge(state, log):
    state = state.astype(F32)
    e = jnp.exp
    pair = state[0] * e(log[1]) + state[1]
    whole = pair * e(log[2] + log[3]) + state[2] * e(log[3]) + state[3]
    return pair, whole


def shards(values, keys, queries, gates, log_decay, level_mix, norm_gain, weight):
    y, a, b, c, x = (lax.axis_index(n) for n in ("y", "a", "b", "c", "x"))
    kept, sent = halves(weight, 1, c)
    both = in_order(kept, swap(sent), c).reshape(64, 512)
    spread = []
    for k in range(4):
        perm = [(s * 4 + f, ((f + k) % 4) * 4 + s) for s in range(4) for f in range(4)]
        spread.append(lax.ppermute(both, ("y", "x"), perm))
    ring = jnp.concatenate(spread + spread[:3], axis=1)
    mine = lax.dynamic_slice_in_dim(ring, ((y - x) % 4) * 512, 2048, 1)
    gathered = lax.all_gather(mine, ("a", "b"), axis=0, tiled=True)

    small = jnp.concatenate([log_decay[None], level_mix])
    kept, sent = halves(small, 1, c)
    small = in_order(kept, swap(sent), c)
    kv = jnp.stack([keys, values])
    kept, sent = halves(kv, 2, c)
    kv = in_order(kept, swap(sent), c)
    qg = jnp.stack([queries, gates])
    kept, sent = halves(qg, 2, c)
    qg = in_order(kept, swap(sent), c)
    kb = kv[:, 0].reshape(2, 256, 4, 128)
    xv = kv[:, 1].reshape(2, 256, 4, 128)
    qc = qg[:, 0].reshape(2, 256, 4, 128)
    z = qg[:, 1].reshape(2, 256, 4, 128)
    gain = lax.dynamic_slice_in_dim(norm_gain, c * 512, 512, 0).reshape(4, 128)
    decay = small[:, 0]
    mix = small[:, 1:]

    local = jnp.cumsum(decay, axis=2)
    total = local[:, :, -1]
    scaled = (
        kb.astype(F32) * jnp.exp(total[:, :, None] - local).transpose(0, 2, 1)[..., None]
    ).astype(BF)
    ends = jnp.einsum("slhn,slhp->shnp", scaled, xv, preferred_element_type=F32)
    chip = ends[0] * jnp.exp(total[1])[:, None, None] + ends[1]
    chip_log = total[0] + total[1]

    got = lax.all_to_all(with_tail(chip, chip_log), "b", 0, 0, tiled=True)
    near, near_log = split_tail(got)
    pair, group = merge(near, near_log)
    group_log = jnp.sum(near_log)

    def near_message(target):
        odd = target % 2 == 1
        upper = target >= 2
        e0 = jnp.where(upper, near[2], near[0])
        l2 = jnp.where(odd, e0, jnp.zeros_like(e0))
        step = jnp.where(odd, jnp.where(upper, near_log[2], near_log[0]), 0.0)
        l3 = jnp.where(upper, pair * jnp.exp(step), 0.0).astype(BF)
        before = jnp.sum(jnp.where(jnp.arange(4) < target, near_log, 0.0))
        return jnp.concatenate([l2, l3, tail(before)], axis=0)

    near_got = [near_message(b)] + [flip(near_message(b ^ k), "b", k) for k in (1, 2, 3)]

    def by_head(blocks):
        stacked = jnp.stack(blocks)
        return jnp.stack([lax.dynamic_index_in_dim(stacked, b ^ h, 0, False) for h in range(4)])

    got = exchange(with_tail(group, group_log[None][0]), "a")
    far, far_log = split_tail(got)
    far_pair, row = merge(far, far_log)
    row_log = jnp.sum(far_log)
    odd, upper = a % 2 == 1, a >= 2
    l4 = jnp.where(odd, jnp.where(upper, far[2], far[0]), jnp.zeros_like(far[0]))
    step = jnp.where(odd, jnp.where(upper, far_log[2], far_log[0]), 0.0)
    l5 = jnp.where(upper, far_pair * jnp.exp(step), 0.0).astype(BF)
    far_before = jnp.sum(jnp.where(jnp.arange(4) < a, far_log, 0.0))
    far_message = jnp.concatenate([l4, l5], axis=0)
    far_got = [far_message] + [flip(far_message, "b", k) for k in (1, 2, 3)]

    got = exchange(with_tail(row, row_log), "y")
    rows, rows_log = split_tail(got)
    rows_pair = rows[0].astype(F32) * jnp.exp(rows_log[1]) + rows[1].astype(F32)
    odd, upper = y % 2 == 1, y >= 2
    l6 = jnp.where(odd, jnp.where(upper, rows[2], rows[0]).astype(F32) * jnp.exp(far_before), 0.0)
    step = jnp.where(odd, jnp.where(upper, rows_log[2], rows_log[0]), 0.0)
    l7 = jnp.where(upper, rows_pair * jnp.exp(step + far_before), 0.0)
    last_message = jnp.concatenate([l6.astype(BF), l7.astype(BF)], axis=0)
    last_got = exchange(last_message, "b")

    lower = jnp.arange(256)[:, None] >= jnp.arange(256)[None, :]
    scores = jnp.einsum("slhn,smhn->shlm", qc, kb, preferred_element_type=F32)
    gap = jnp.where(lower, local[..., :, None] - local[..., None, :], -jnp.inf)
    weights = (scores * jnp.exp(gap)).astype(BF)
    own = jnp.einsum("shlm,smhp->shlp", weights, xv, preferred_element_type=F32)
    mixture = own * mix[:, 0][..., None]
    start = jnp.exp(local)
    read1 = jnp.einsum("lhn,hnp->hlp", qc[1], ends[0].astype(BF), preferred_element_type=F32)
    read1 = read1 * (start[1] * mix[1, 1])[..., None]
    mixture = mixture + jnp.stack([jnp.zeros_like(read1), read1])
    chip_start = jnp.stack([start[0], jnp.exp(local[1] + total[0][:, None])])

    near_all = by_head(near_got)
    far_all = by_head(far_got)
    b_start = chip_start * jnp.exp(untail(near_all[:, 256:]))[None, :, None]
    for level, block, scale in (
        (2, near_all[:, :128], chip_start),
        (3, near_all[:, 128:256], chip_start),
        (4, far_all[:, :128], b_start),
        (5, far_all[:, 128:], b_start),
        (6, last_got[:, :128], b_start),
        (7, last_got[:, 128:], b_start),
    ):
        read = jnp.einsum("slhn,hnp->shlp", qc, block, preferred_element_type=F32)
        mixture = mixture + read * (scale * mix[:, level])[..., None]

    gated = mixture * jax.nn.silu(z.transpose(0, 2, 1, 3).astype(F32))
    rms = jnp.sqrt(jnp.mean(gated * gated, axis=3, keepdims=True) + 1e-05)
    normed = (gated / rms * gain[None, :, None].astype(F32)).astype(BF)
    normed = normed.transpose(0, 2, 1, 3).reshape(512, 512)

    blocks = [normed] + [
        lax.ppermute(normed, "x", [(i, (i + j) % 4) for i in range(4)]) for j in (1, 2, 3)
    ]
    out = 0.0
    for j in range(4):
        out = out + lax.dot_general(
            blocks[j],
            gathered[:, j * 512 : (j + 1) * 512],
            (((1,), (1,)), ((), ())),
            preferred_element_type=F32,
        )
    kept, sent = halves(out, 0, c)
    return (kept + swap(sent.astype(BF)).astype(F32)).astype(BF)


def solution(mesh):
    fine = Mesh(mesh.devices.reshape(4, 4, 4, 2, 4), SEQ + ("x",))
    return jax.shard_map(
        shards,
        mesh=fine,
        in_specs=(
            P(SEQ, "x"),
            P(SEQ, "x"),
            P(SEQ, "x"),
            P(SEQ, "x"),
            P("x", SEQ),
            P(None, "x", SEQ),
            P("x"),
            P(SEQ, "x"),
        ),
        out_specs=P(SEQ, "x"),
        check_vma=False,
    )
```

```python
import jax
import jax.numpy as jnp
from jax import lax
from jax.experimental import pallas as pl
from jax.experimental.pallas import tpu as pltpu
from jax.sharding import Mesh, PartitionSpec as P

BF = jnp.bfloat16
F32 = jnp.float32
SEQ = ("y", "a", "b", "c")
NT = (((1,), (1,)), ((), ()))
TN = (((0,), (0,)), ((), ()))


def swap(value):
    return lax.ppermute(value, "c", [(0, 1), (1, 0)])


def flip(value, axis, mask):
    return lax.ppermute(value, axis, [(i, i ^ mask) for i in range(4)])


def halves(value, axis, core):
    size = value.shape[axis] // 2
    kept = lax.dynamic_slice_in_dim(value, core * size, size, axis)
    sent = lax.dynamic_slice_in_dim(value, (1 - core) * size, size, axis)
    return kept, sent


def dot(left, right, dims=(((1,), (0,)), ((), ()))):
    return lax.dot_general(left, right, dims, preferred_element_type=F32)


def exact(left, right, dims):
    return lax.dot_general(
        left, right, dims, precision=lax.Precision.HIGHEST, preferred_element_type=F32
    )


def tail(log):
    high = log.astype(BF).astype(F32)
    middle = (log - high).astype(BF).astype(F32)
    low = log - high - middle
    row = lax.broadcasted_iota(jnp.int32, (16, 128), 0)
    return jnp.where(
        row == 0, high, jnp.where(row == 1, middle, jnp.where(row == 2, low, 0.0))
    ).astype(BF)


def untail(tile):
    return jnp.sum(tile.astype(F32), axis=0, keepdims=True)


def call(body, outs, args, scratch=(), flops=10**6):
    specs = [pl.BlockSpec(memory_space=pltpu.SMEM)]
    specs += [pl.BlockSpec(memory_space=pltpu.VMEM)] * (len(args) - 1)
    return pl.pallas_call(
        body,
        out_shape=[jax.ShapeDtypeStruct(*o) for o in outs],
        in_specs=specs,
        out_specs=[pl.BlockSpec(memory_space=pltpu.VMEM)] * len(outs),
        scratch_shapes=list(scratch),
        compiler_params=pltpu.CompilerParams(vmem_limit_bytes=32 * 2**20),
        cost_estimate=pl.CostEstimate(flops=flops, bytes_accessed=10**6, transcendentals=0),
    )(*args)


def four(ref, core):
    return jnp.where(core == 0, ref[0:4], ref[4:8])


def ends_body(at, keys, values, got, decay, got_small, pay, first):
    core = at[0]
    base = core * 512
    logs = jnp.concatenate([four(decay, core), got_small[0]], axis=0)
    after = (
        lax.broadcasted_iota(jnp.int32, (256, 256), 1)
        > lax.broadcasted_iota(jnp.int32, (256, 256), 0)
    ).astype(F32)
    scale = jnp.exp(exact(after, logs, NT))
    total = jnp.sum(logs, axis=1, keepdims=True)
    for h in range(4):
        mine = pl.ds(pl.multiple_of(base + h * 128, 128), 128)
        cols = slice(h * 128, h * 128 + 128)
        scaled = (keys[:, mine].astype(F32) * scale[:, h : h + 1]).astype(BF)
        own_end = dot(scaled, values[:, mine], TN)
        scaled = (got[0:256, cols].astype(F32) * scale[:, 4 + h : 5 + h]).astype(BF)
        got_end = dot(scaled, got[256:512, cols], TN)
        own_log, got_log = total[h : h + 1], total[4 + h : 5 + h]
        own_later = jnp.exp(jnp.where(core == 0, got_log, 0.0))
        got_later = jnp.exp(jnp.where(core == 0, 0.0, own_log))
        pay[h, 0:128, :] = (own_end * own_later + got_end * got_later).astype(BF)
        pay[h, 128:144, :] = tail(own_log + got_log)
        first[h, :, :] = jnp.where(core == 0, own_end, got_end).astype(BF)


def merge(got):
    s = [got[i, 0:128, :].astype(F32) for i in range(4)]
    t = [untail(got[i, 128:144, :]) for i in range(4)]
    pair = s[0] * jnp.exp(t[1]) + s[1]
    return s, t, pair


def whole(s, t, pair):
    return pair * jnp.exp(t[2] + t[3]) + s[2] * jnp.exp(t[3]) + s[3]


def lower_states(s, t, pair, at):
    odd, upper = at % 2 == 1, at >= 2
    one = jnp.where(odd, jnp.where(upper, s[2], s[0]), 0.0)
    step = jnp.where(odd, jnp.where(upper, t[2], t[0]), 0.0)
    two = jnp.where(upper, pair * jnp.exp(step), 0.0)
    before = sum(jnp.where(at > i, t[i], 0.0) for i in range(3))
    return one, two, before


def near_body(at, got, pay, *messages):
    s, t, pair = merge(got)
    group = whole(s, t, pair).astype(BF)
    log = tail(t[0] + t[1] + t[2] + t[3])
    for i in range(4):
        pay[i, 0:128, :] = group
        pay[i, 128:144, :] = log
    for k in range(4):
        one, two, before = lower_states(s, t, pair, at[1] ^ k)
        messages[k][0:128, 0:128] = one.astype(BF)
        messages[k][0:128, 128:256] = two.astype(BF)
        messages[k][128:144, 0:128] = tail(before)
        messages[k][128:144, 128:256] = jnp.zeros((16, 128), BF)


def far_body(at, got, pay, message, before_out):
    s, t, pair = merge(got)
    row = whole(s, t, pair).astype(BF)
    log = tail(t[0] + t[1] + t[2] + t[3])
    for i in range(4):
        pay[i, 0:128, :] = row
        pay[i, 128:144, :] = log
    one, two, before = lower_states(s, t, pair, at[2])
    message[:, 0:128] = one.astype(BF)
    message[:, 128:256] = two.astype(BF)
    before_out[...] = jnp.broadcast_to(before, (8, 128))


def last_body(at, got, before, message):
    s, t, pair = merge(got)
    one, two, _ = lower_states(s, t, pair, at[3])
    earlier = jnp.exp(before[0:1, :])
    one, two = (one * earlier).astype(BF), (two * earlier).astype(BF)
    for i in range(4):
        message[i, :, 0:128] = one
        message[i, :, 128:256] = two


def mix_body(
    at, keys, values, queries, got_kv, got_qg, decay, mix, got_small, first,
    n0, n1, n2, n3, f0, f1, f2, f3, mixture, coef, near, far,
):
    core, place = at[0], at[1]
    base = core * 512
    for k, (n, f) in enumerate(((n0, f0), (n1, f1), (n2, f2), (n3, f3))):
        near[place ^ k] = n[...]
        far[place ^ k] = f[...]
    rows = lax.broadcasted_iota(jnp.int32, (256, 256), 0)
    cols = lax.broadcasted_iota(jnp.int32, (256, 256), 1)
    lower = rows >= cols
    upto = lower.astype(F32)
    own_mix = jnp.where(core == 0, mix[:, 0:4, :], mix[:, 4:8, :])
    for s in range(2):
        logs = four(decay, core) if s == 0 else got_small[0]
        logs = jnp.concatenate([logs, logs], axis=0)
        other = four(decay, core) if s == 1 else got_small[0]
        levels = own_mix if s == 0 else got_small[1:9]
        second = (core if s == 0 else 1 - core) == 1
        at_row = exact(logs, upto, NT)
        at_col = exact(upto, logs, NT)
        flat = [levels[l] for l in range(8)]
        flat = [jnp.concatenate(flat[l : l + 2], axis=0) for l in range(0, 8, 2)]
        level = [f.T for f in flat]
        first_log = jnp.where(second, jnp.sum(other, axis=1, keepdims=True), 0.0)
        here = slice(s * 256, s * 256 + 256)
        for h in range(4):
            mine = pl.ds(pl.multiple_of(base + h * 128, 128), 128)
            hc = slice(h * 128, h * 128 + 128)
            if s == 0:
                q, kb, v = queries[:, mine], keys[:, mine], values[:, mine]
            else:
                q, kb, v = got_qg[0:256, hc], got_kv[0:256, hc], got_kv[256:512, hc]
            local = at_col[:, h : h + 1]
            gap = jnp.where(lower, local - at_row[h : h + 1, :], -1e30)
            weights = (dot(q, kb, NT) * jnp.exp(gap)).astype(BF)
            m = [level[l // 2][:, 4 * (l % 2) + h : 4 * (l % 2) + h + 1] for l in range(8)]
            total = dot(weights, v) * m[0]
            start = jnp.exp(local)
            total += dot(q, first[h]) * jnp.where(second, start * m[1], 0.0)
            start = start * jnp.exp(first_log[h : h + 1])
            read = dot(q, near[h, 0:128, :])
            total += read[:, 0:128] * (start * m[2]) + read[:, 128:256] * (start * m[3])
            start = start * jnp.exp(untail(near[h, 128:144, 0:128])[:, 0:1])
            read = dot(q, far[h])
            total += read[:, 0:128] * (start * m[4]) + read[:, 128:256] * (start * m[5])
            mixture[here, hc] = total
            coef[here, 2 * h : 2 * h + 1] = start * m[6]
            coef[here, 2 * h + 1 : 2 * h + 2] = start * m[7]


def norm_body(at, queries, gates, got_qg, gain, mixture, coef, last, normed):
    base = at[0] * 512
    for s in range(2):
        here = slice(s * 256, s * 256 + 256)
        for h in range(4):
            mine = pl.ds(pl.multiple_of(base + h * 128, 128), 128)
            hc = slice(h * 128, h * 128 + 128)
            if s == 0:
                q, z = queries[:, mine], gates[:, mine]
            else:
                q, z = got_qg[0:256, hc], got_qg[256:512, hc]
            read = dot(q, last[h])
            total = mixture[here, hc]
            total += read[:, 0:128] * coef[here, 2 * h : 2 * h + 1]
            total += read[:, 128:256] * coef[here, 2 * h + 1 : 2 * h + 2]
            z = z.astype(F32)
            gated = total * (z / (1.0 + jnp.exp(-z)))
            scale = lax.rsqrt(jnp.mean(gated * gated, axis=1, keepdims=True) + 1e-05)
            normed[here, hc] = (gated * scale * gain[:, mine].astype(F32)).astype(BF)


def shards(values, keys, queries, gates, log_decay, level_mix, norm_gain, weight):
    y, a, b, c, x = (lax.axis_index(n) for n in ("y", "a", "b", "c", "x"))
    at = jnp.stack([c, b, a, y]).astype(jnp.int32)
    kept, sent = halves(weight, 1, c)
    got = swap(sent)
    both = jnp.concatenate([jnp.where(c == 0, kept, got), jnp.where(c == 0, got, kept)])
    spread = []
    for k in range(4):
        perm = [(s * 4 + f, ((f + k) % 4) * 4 + s) for s in range(4) for f in range(4)]
        spread.append(lax.ppermute(both, ("y", "x"), perm))
    ring = jnp.concatenate(spread + spread[:3], axis=1)
    mine = lax.dynamic_slice_in_dim(ring, ((y - x) % 4) * 512, 2048, 1)
    gathered = lax.all_gather(mine, ("a", "b"), axis=0, tiled=True)

    away = (1 - c) * 512
    half = lambda v: lax.dynamic_slice_in_dim(v, away, 512, 1)
    got_kv = swap(jnp.concatenate([half(keys), half(values)]))
    small = jnp.concatenate([log_decay[None], level_mix])
    got_small = swap(lax.dynamic_slice_in_dim(small, (1 - c) * 4, 4, 1))
    got_qg = swap(jnp.concatenate([half(queries), half(gates)]))

    pay, first = call(
        ends_body,
        [((4, 144, 128), BF), ((4, 128, 128), BF)],
        (at, keys, values, got_kv, log_decay, got_small),
    )
    got = lax.all_to_all(pay, "b", 0, 0, tiled=True)
    pay, *near = call(near_body, [((4, 144, 128), BF)] + [((144, 256), BF)] * 4, (at, got))
    near = near[:1] + [flip(near[k], "b", k) for k in (1, 2, 3)]
    got = lax.all_to_all(pay, "a", 0, 0, tiled=True)
    pay, far, before = call(
        far_body, [((4, 144, 128), BF), ((128, 256), BF), ((8, 128), F32)], (at, got)
    )
    far = [far] + [flip(far, "b", k) for k in (1, 2, 3)]
    got = lax.all_to_all(pay, "y", 0, 0, tiled=True)
    (last,) = call(last_body, [((4, 128, 256), BF)], (at, got, before))
    last = lax.all_to_all(last, "b", 0, 0, tiled=True)
    mixture, coef = call(
        mix_body,
        [((512, 512), F32), ((512, 8), F32)],
        (at, keys, values, queries, got_kv, got_qg, log_decay, level_mix, got_small, first)
        + tuple(near) + tuple(far),
        [pltpu.VMEM((4, 144, 256), BF), pltpu.VMEM((4, 128, 256), BF)],
    )
    (normed,) = call(
        norm_body,
        [((512, 512), BF)],
        (at, queries, gates, got_qg, norm_gain[None], mixture, coef, last),
    )

    blocks = [normed] + [
        lax.ppermute(normed, "x", [(i, (i + j) % 4) for i in range(4)]) for j in (1, 2, 3)
    ]
    out = 0.0
    for j in range(4):
        out = out + dot(blocks[j], gathered[:, j * 512 : (j + 1) * 512], NT)
    return (out[:256] + swap(out[256:].astype(BF)).astype(F32)).astype(BF)


def solution(mesh):
    fine = Mesh(mesh.devices.reshape(4, 4, 4, 2, 4), SEQ + ("x",))
    return jax.shard_map(
        shards,
        mesh=fine,
        in_specs=(
            P(SEQ, "x"),
            P(SEQ, "x"),
            P(SEQ, "x"),
            P(SEQ, "x"),
            P("x", SEQ),
            P(None, "x", SEQ),
            P("x"),
            P(SEQ, "x"),
        ),
        out_specs=P(SEQ, "x"),
        check_vma=False,
    )
```

```python
import jax
import jax.numpy as jnp
from jax import lax
from jax.experimental import pallas as pl
from jax.experimental.pallas import tpu as pltpu
from jax.sharding import Mesh, PartitionSpec as P

BF = jnp.bfloat16
F32 = jnp.float32
SEQ = ("y", "a", "b", "c")
NT = (((1,), (1,)), ((), ()))
TN = (((0,), (0,)), ((), ()))
LOGS = 1024


def swap(value):
    return lax.ppermute(value, "c", [(0, 1), (1, 0)])


def dot(left, right, dims=(((1,), (0,)), ((), ()))):
    return lax.dot_general(left, right, dims, preferred_element_type=F32)


def exact(left, right, dims):
    return lax.dot_general(
        left, right, dims, precision=lax.Precision.HIGHEST, preferred_element_type=F32
    )


def tail(log):
    high = log.astype(BF).astype(F32)
    middle = (log - high).astype(BF).astype(F32)
    low = log - high - middle
    row = lax.broadcasted_iota(jnp.int32, (16, 128), 0)
    return jnp.where(
        row == 0, high, jnp.where(row == 1, middle, jnp.where(row == 2, low, 0.0))
    ).astype(BF)


def untail(tile):
    return jnp.sum(tile.astype(F32), axis=0, keepdims=True)


def call(body, outs, args, unread=(), flops=10**6):
    specs = [pl.BlockSpec(memory_space=pltpu.SMEM)]
    specs += [pl.BlockSpec(memory_space=pltpu.VMEM)] * (len(args) - 1)
    specs += [pl.BlockSpec(memory_space=pl.ANY)] * len(unread)

    def run(*refs):
        body(*refs[: len(args)], *refs[len(args) + len(unread) :])

    return pl.pallas_call(
        run,
        out_shape=[jax.ShapeDtypeStruct(*o) for o in outs],
        in_specs=specs,
        out_specs=[pl.BlockSpec(memory_space=pltpu.VMEM)] * len(outs),
        compiler_params=pltpu.CompilerParams(vmem_limit_bytes=32 * 2**20),
        cost_estimate=pl.CostEstimate(flops=flops, bytes_accessed=10**6, transcendentals=0),
    )(*args, *unread)


def pack_body(at, keys, values, queries, gates, decay, mix, out):
    core = at[0]
    theirs = pl.ds(pl.multiple_of((1 - core) * 512, 512), 512)
    for i, ref in enumerate((keys, values, queries, gates)):
        out[i * 256 : i * 256 + 256, :] = ref[:, theirs]
    logs = [jnp.where(core == 0, decay[4:8], decay[0:4])]
    logs += [jnp.where(core == 0, mix[l, 4:8], mix[l, 0:4]) for l in range(8)]
    logs = jnp.concatenate(logs + [jnp.zeros((12, 256), F32)], axis=0)
    high = logs.astype(BF)
    out[LOGS:, 0:256] = high
    out[LOGS:, 256:512] = (logs - high.astype(F32)).astype(BF)


def own_half(ref, core):
    return jnp.where(core == 0, ref[0:4], ref[4:8])


def got_logs(got):
    tile = got[LOGS:, :].astype(F32)
    return tile[:, 0:256] + tile[:, 256:512]


def ends_body(at, keys, values, got, decay, pay, first):
    core = at[0]
    logs = jnp.concatenate([own_half(decay, core), got_logs(got)[0:4]], axis=0)
    after = (
        lax.broadcasted_iota(jnp.int32, (256, 256), 1)
        > lax.broadcasted_iota(jnp.int32, (256, 256), 0)
    ).astype(F32)
    scale = jnp.exp(exact(after, logs, NT))
    total = jnp.sum(logs, axis=1, keepdims=True)
    for h in range(4):
        mine = pl.ds(pl.multiple_of(core * 512 + h * 128, 128), 128)
        cols = slice(h * 128, h * 128 + 128)
        scaled = (keys[:, mine].astype(F32) * scale[:, h : h + 1]).astype(BF)
        own_end = dot(scaled, values[:, mine], TN)
        scaled = (got[0:256, cols].astype(F32) * scale[:, 4 + h : 5 + h]).astype(BF)
        got_end = dot(scaled, got[256:512, cols], TN)
        own_log, got_log = total[h : h + 1], total[4 + h : 5 + h]
        own_later = jnp.exp(jnp.where(core == 0, got_log, 0.0))
        got_later = jnp.exp(jnp.where(core == 0, 0.0, own_log))
        pay[h, 0:128, :] = (own_end * own_later + got_end * got_later).astype(BF)
        pay[h, 128:144, :] = tail(own_log + got_log)
        first[h, :, :] = jnp.where(core == 0, own_end, got_end).astype(BF)


def merge(got):
    s = [got[i, 0:128, :].astype(F32) for i in range(4)]
    t = [untail(got[i, 128:144, :]) for i in range(4)]
    pair = s[0] * jnp.exp(t[1]) + s[1]
    return s, t, pair


def send_whole(s, t, pair, pay):
    state = (pair * jnp.exp(t[2] + t[3]) + s[2] * jnp.exp(t[3]) + s[3]).astype(BF)
    log = tail(t[0] + t[1] + t[2] + t[3])
    for i in range(4):
        pay[i, 0:128, :] = state
        pay[i, 128:144, :] = log


def lower_states(s, t, pair, at):
    odd, upper = at % 2 == 1, at >= 2
    one = jnp.where(odd, jnp.where(upper, s[2], s[0]), 0.0)
    step = jnp.where(odd, jnp.where(upper, t[2], t[0]), 0.0)
    two = jnp.where(upper, pair * jnp.exp(step), 0.0)
    before = sum(jnp.where(at > i, t[i], 0.0) for i in range(3))
    return one, two, before


def near_body(at, got, pay, message):
    s, t, pair = merge(got)
    send_whole(s, t, pair, pay)
    for i in range(4):
        one, two, before = lower_states(s, t, pair, jnp.int32(i))
        message[i, 0:128, 0:128] = one.astype(BF)
        message[i, 0:128, 128:256] = two.astype(BF)
        message[i, 128:144, 0:128] = tail(before)
        message[i, 128:144, 128:256] = jnp.zeros((16, 128), BF)


def far_body(at, got, pay, message, before_out):
    s, t, pair = merge(got)
    send_whole(s, t, pair, pay)
    one, two, before = lower_states(s, t, pair, at[2])
    for i in range(4):
        message[i, :, 0:128] = one.astype(BF)
        message[i, :, 128:256] = two.astype(BF)
    before_out[...] = jnp.broadcast_to(before, (8, 128))


def last_body(at, got, before, message):
    s, t, pair = merge(got)
    one, two, _ = lower_states(s, t, pair, at[3])
    earlier = jnp.exp(before[0:1, :])
    one, two = (one * earlier).astype(BF), (two * earlier).astype(BF)
    for i in range(4):
        message[i, :, 0:128] = one
        message[i, :, 128:256] = two


def place(s, core):
    at = core if s == 0 else 1 - core
    return at, pl.ds(pl.multiple_of(at * 256, 256), 256)


def own_body(at, keys, values, queries, got, decay, mix, first, mixture, coef):
    core = at[0]
    rows = lax.broadcasted_iota(jnp.int32, (256, 256), 0)
    cols = lax.broadcasted_iota(jnp.int32, (256, 256), 1)
    lower = rows >= cols
    upto = lower.astype(F32)
    own_logs = [own_half(decay, core)]
    own_logs += [jnp.where(core == 0, mix[l, 0:4], mix[l, 4:8]) for l in range(8)]
    own_logs = jnp.concatenate(own_logs + [jnp.zeros((12, 256), F32)], axis=0)
    both = (own_logs, got_logs(got))
    for s in range(2):
        second, here = place(s, core)
        logs = both[s]
        at_row = exact(logs[0:8], upto, NT)
        at_col = exact(upto, logs[0:8], NT)
        level = logs.T
        first_log = jnp.sum(both[1 - s][0:4], axis=1, keepdims=True)
        first_log = jnp.where(second == 1, first_log, 0.0)
        for h in range(4):
            mine = pl.ds(pl.multiple_of(core * 512 + h * 128, 128), 128)
            hc = slice(h * 128, h * 128 + 128)
            if s == 0:
                q, kb, v = queries[:, mine], keys[:, mine], values[:, mine]
            else:
                q, kb, v = got[512:768, hc], got[0:256, hc], got[256:512, hc]
            local = at_col[:, h : h + 1]
            gap = jnp.where(lower, local - at_row[h : h + 1, :], -1e30)
            weights = (dot(q, kb, NT) * jnp.exp(gap)).astype(BF)
            m = [level[:, 4 + 4 * l + h : 5 + 4 * l + h] for l in range(8)]
            total = dot(weights, v) * m[0]
            start = jnp.exp(local)
            total += dot(q, first[h]) * jnp.where(second == 1, start * m[1], 0.0)
            start = start * jnp.exp(first_log[h : h + 1])
            mixture[here, hc] = total
            for l in range(2, 8):
                coef[here, 6 * h + l - 2 : 6 * h + l - 1] = start * m[l]


def norm_body(at, queries, gates, got, gain, mixture, coef, near, far, last, normed):
    core = at[0]
    for s in range(2):
        _, here = place(s, core)
        for h in range(4):
            mine = pl.ds(pl.multiple_of(core * 512 + h * 128, 128), 128)
            hc = slice(h * 128, h * 128 + 128)
            if s == 0:
                q, z = queries[:, mine], gates[:, mine]
            else:
                q, z = got[512:768, hc], got[768:1024, hc]
            scale = [coef[here, 6 * h + l : 6 * h + l + 1] for l in range(6)]
            later = jnp.exp(untail(near[h, 128:144, 0:128])[:, 0:1])
            total = mixture[here, hc]
            read = dot(q, near[h, 0:128, :])
            total += read[:, 0:128] * scale[0] + read[:, 128:256] * scale[1]
            read = dot(q, far[h])
            total += read[:, 0:128] * (scale[2] * later) + read[:, 128:256] * (scale[3] * later)
            read = dot(q, last[h])
            total += read[:, 0:128] * (scale[4] * later) + read[:, 128:256] * (scale[5] * later)
            z = z.astype(F32)
            gated = total * (z / (1.0 + jnp.exp(-z)))
            size = lax.rsqrt(jnp.mean(gated * gated, axis=1, keepdims=True) + 1e-05)
            normed[here, hc] = (gated * size * gain[:, mine].astype(F32)).astype(BF)


def project_body(at, left, right, out, total):
    step = pl.program_id(0)
    part = dot(left[...], right[...], NT)

    @pl.when(step == 0)
    def _():
        total[...] = part

    @pl.when(step > 0)
    def _():
        total[...] += part

    @pl.when(step == pl.num_programs(0) - 1)
    def _():
        out[...] = total[...].astype(BF)


def project(at, left, right, other):
    row = (lambda k, at: (1 - at[0], k)) if other else (lambda k, at: (at[0], k))
    return pl.pallas_call(
        project_body,
        out_shape=jax.ShapeDtypeStruct((256, 512), BF),
        grid_spec=pltpu.PrefetchScalarGridSpec(
            num_scalar_prefetch=1,
            grid=(4,),
            in_specs=[
                pl.BlockSpec((256, 1024), row),
                pl.BlockSpec((512, 1024), lambda k, at: (0, k)),
            ],
            out_specs=pl.BlockSpec((256, 512), lambda k, at: (0, 0)),
            scratch_shapes=[pltpu.VMEM((256, 512), F32)],
        ),
        compiler_params=pltpu.CompilerParams(vmem_limit_bytes=32 * 2**20),
        cost_estimate=pl.CostEstimate(
            flops=2**30, bytes_accessed=6 * 2**20, transcendentals=0
        ),
    )(at, left, right)


def weave_body(at, own, got, out):
    core = at[0]
    i = lax.broadcasted_iota(jnp.int32, (128, 256), 0)
    j = lax.broadcasted_iota(jnp.int32, (128, 256), 1)
    spot = (i >> 5) * 64 + (i & 31)
    mine = (j == spot + core * 32).astype(BF)
    theirs = (j == spot + (1 - core) * 32).astype(BF)
    for m in range(4):
        cols = slice(m * 128, m * 128 + 128)
        both = dot(own[:, cols], mine) + dot(got[:, cols], theirs)
        out[:, m * 256 : m * 256 + 256] = both.astype(BF)


def shards(values, keys, queries, gates, log_decay, level_mix, norm_gain, weight):
    y, a, b, c, x = (lax.axis_index(n) for n in ("y", "a", "b", "c", "x"))
    at = jnp.stack([c, b, a, y]).astype(jnp.int32)
    spread = []
    for k in range(4):
        perm = [(s * 4 + f, ((f + k) % 4) * 4 + s) for s in range(4) for f in range(4)]
        spread.append(lax.ppermute(weight, ("y", "x"), perm))
    ring = jnp.concatenate(spread + spread[:3], axis=1)
    mine = lax.dynamic_slice_in_dim(ring, ((y - x) % 4) * 1024, 4096, 1)
    (pack,) = call(
        pack_body,
        [((LOGS + 48, 512), BF)],
        (at, keys, values, queries, gates, log_decay, level_mix),
    )
    got = swap(pack)
    mine, got = lax.optimization_barrier((mine, got))
    gathered = lax.all_gather(mine, ("a", "b"), axis=0, tiled=True)

    pay, first = call(
        ends_body,
        [((4, 144, 128), BF), ((4, 128, 128), BF)],
        (at, keys, values, got, log_decay),
    )
    mixture, coef = call(
        own_body,
        [((512, 512), F32), ((512, 24), F32)],
        (at, keys, values, queries, got, log_decay, level_mix, first),
    )
    near = lax.all_to_all(pay, "b", 0, 0, tiled=True)
    pay, near = call(near_body, [((4, 144, 128), BF), ((4, 144, 256), BF)], (at, near))
    near = lax.all_to_all(near, "b", 0, 0, tiled=True)
    far = lax.all_to_all(pay, "a", 0, 0, tiled=True)
    pay, far, before = call(
        far_body,
        [((4, 144, 128), BF), ((4, 128, 256), BF), ((8, 128), F32)],
        (at, far),
        (near, mixture),
    )
    far = lax.all_to_all(far, "b", 0, 0, tiled=True)
    last = lax.all_to_all(pay, "y", 0, 0, tiled=True)
    (last,) = call(last_body, [((4, 128, 256), BF)], (at, last, before), (far,))
    last = lax.all_to_all(last, "b", 0, 0, tiled=True)
    (normed,) = call(
        norm_body,
        [((512, 512), BF)],
        (at, queries, gates, got, norm_gain[None], mixture, coef, near, far, last),
    )

    blocks = [normed] + [
        lax.ppermute(normed, "x", [(i, (i + j) % 4) for i in range(4)]) for j in (1, 2, 3)
    ]
    pairs = []
    for block in blocks:
        theirs = swap(block)
        pairs += [jnp.where(c == 0, block, theirs), jnp.where(c == 0, theirs, block)]
    left = jnp.concatenate(pairs, axis=1)
    theirs = swap(project(at, left, gathered, True))
    own = project(at, left, gathered, False)
    return call(weave_body, [((256, 1024), BF)], (at, own, theirs))[0]


def solution(mesh):
    fine = Mesh(mesh.devices.reshape(4, 4, 4, 2, 4), SEQ + ("x",))
    return jax.shard_map(
        shards,
        mesh=fine,
        in_specs=(
            P(SEQ, "x"),
            P(SEQ, "x"),
            P(SEQ, "x"),
            P(SEQ, "x"),
            P("x", SEQ),
            P(None, "x", SEQ),
            P("x"),
            P(SEQ, "x"),
        ),
        out_specs=P(SEQ, "x"),
        check_vma=False,
    )
```

```python
import functools

import jax
import jax.numpy as jnp
from jax import lax
from jax.experimental import pallas as pl
from jax.experimental.pallas import tpu as pltpu
from jax.sharding import Mesh, PartitionSpec as P

BF = jnp.bfloat16
F32 = jnp.float32
SEQ = ("y", "a", "b", "c")
NT = (((1,), (1,)), ((), ()))
TN = (((0,), (0,)), ((), ()))
LOGS = 1024


def swap(value):
    return lax.ppermute(value, "c", [(0, 1), (1, 0)])


def flip(value, axis, mask):
    return lax.ppermute(value, axis, [(i, i ^ mask) for i in range(4)])


def flat(place):
    y, x, core = place // 8, place // 2 % 4, place % 2
    return (y * 2 + core) * 4 + x


def dot(left, right, dims=(((1,), (0,)), ((), ()))):
    return lax.dot_general(left, right, dims, preferred_element_type=F32)


def exact(left, right, dims):
    return lax.dot_general(
        left, right, dims, precision=lax.Precision.HIGHEST, preferred_element_type=F32
    )


def tail(log):
    high = log.astype(BF).astype(F32)
    middle = (log - high).astype(BF).astype(F32)
    low = log - high - middle
    row = lax.broadcasted_iota(jnp.int32, (16, 128), 0)
    return jnp.where(
        row == 0, high, jnp.where(row == 1, middle, jnp.where(row == 2, low, 0.0))
    ).astype(BF)


def untail(tile):
    return jnp.sum(tile.astype(F32), axis=0, keepdims=True)


def call(body, outs, args, unread=(), scratch=(), hbm=()):
    specs = [pl.BlockSpec(memory_space=pltpu.SMEM)]
    specs += [
        pl.BlockSpec(memory_space=pl.ANY if i in hbm else pltpu.VMEM)
        for i in range(1, len(args))
    ]
    specs += [pl.BlockSpec(memory_space=pl.ANY)] * len(unread)

    def run(*refs):
        body(*refs[: len(args)], *refs[len(args) + len(unread) :])

    return pl.pallas_call(
        run,
        out_shape=[jax.ShapeDtypeStruct(*o) for o in outs],
        in_specs=specs,
        out_specs=[pl.BlockSpec(memory_space=pltpu.VMEM)] * len(outs),
        scratch_shapes=list(scratch),
        compiler_params=pltpu.CompilerParams(vmem_limit_bytes=32 * 2**20),
        cost_estimate=pl.CostEstimate(flops=10**6, bytes_accessed=10**6, transcendentals=0),
    )(*args, *unread)


def pack_body(
    at, keys, values, queries, gates, decay, mix, weight,
    keep, send, w_same, w_other, small, levels, wide, sems,
):
    core = at[0]
    mine = pl.ds(pl.multiple_of(core * 512, 512), 512)
    theirs = pl.ds(pl.multiple_of((1 - core) * 512, 512), 512)
    copies = [
        pltpu.make_async_copy(decay, small, sems.at[0]),
        pltpu.make_async_copy(mix, levels, sems.at[1]),
        pltpu.make_async_copy(weight, wide, sems.at[2]),
    ]
    for i, ref in enumerate((keys, values, queries, gates)):
        rows = pl.ds(i * 256, 256)
        for out, cols, n in ((send, theirs, 3), (keep, mine, 7)):
            copies.append(pltpu.make_async_copy(ref.at[:, cols], out.at[rows, :], sems.at[n + i]))
    for copy in copies:
        copy.start()
    for copy in copies[:3]:
        copy.wait()
    w_same[...] = wide[:, mine]
    w_other[...] = wide[:, theirs]
    for out, low in ((keep, core == 0), (send, core == 1)):
        logs = [jnp.where(low, small[0:4], small[4:8])]
        logs += [jnp.where(low, levels[l, 0:4], levels[l, 4:8]) for l in range(8)]
        logs = jnp.concatenate(logs + [jnp.zeros((12, 256), F32)], axis=0)
        high = logs.astype(BF)
        out[LOGS:, 0:256] = high
        out[LOGS:, 256:512] = (logs - high.astype(F32)).astype(BF)
    for copy in copies[3:]:
        copy.wait()


def logs_of(block):
    tile = block[LOGS:, :].astype(F32)
    return tile[:, 0:256] + tile[:, 256:512]


def ends_body(at, keep, got, pay, first):
    core = at[0]
    logs = jnp.concatenate([logs_of(keep)[0:4], logs_of(got)[0:4]], axis=0)
    after = (
        lax.broadcasted_iota(jnp.int32, (256, 256), 1)
        > lax.broadcasted_iota(jnp.int32, (256, 256), 0)
    ).astype(F32)
    scale = jnp.exp(exact(after, logs, NT))
    total = jnp.sum(logs, axis=1, keepdims=True)
    for h in range(4):
        cols = slice(h * 128, h * 128 + 128)
        end = []
        for i, ref in enumerate((keep, got)):
            scaled = ref[0:256, cols].astype(F32) * scale[:, 4 * i + h : 4 * i + h + 1]
            end.append(dot(scaled.astype(BF), ref[256:512, cols], TN))
        own_log, got_log = total[h : h + 1], total[4 + h : 5 + h]
        own_later = jnp.exp(jnp.where(core == 0, got_log, 0.0))
        got_later = jnp.exp(jnp.where(core == 0, 0.0, own_log))
        pay[h, 0:128, :] = (end[0] * own_later + end[1] * got_later).astype(BF)
        pay[h, 128:144, :] = tail(own_log + got_log)
        first[h, :, :] = jnp.where(core == 0, end[0], end[1]).astype(BF)


def merge(got):
    s = [got[i, 0:128, :].astype(F32) for i in range(4)]
    t = [untail(got[i, 128:144, :]) for i in range(4)]
    pair = s[0] * jnp.exp(t[1]) + s[1]
    return s, t, pair


def send_whole(s, t, pair, pay):
    state = (pair * jnp.exp(t[2] + t[3]) + s[2] * jnp.exp(t[3]) + s[3]).astype(BF)
    log = tail(t[0] + t[1] + t[2] + t[3])
    for i in range(4):
        pay[i, 0:128, :] = state
        pay[i, 128:144, :] = log


def lower_states(s, t, pair, at):
    odd, upper = at % 2 == 1, at >= 2
    one = jnp.where(odd, jnp.where(upper, s[2], s[0]), 0.0)
    step = jnp.where(odd, jnp.where(upper, t[2], t[0]), 0.0)
    two = jnp.where(upper, pair * jnp.exp(step), 0.0)
    before = sum(jnp.where(at > i, t[i], 0.0) for i in range(3))
    return one, two, before


def near_body(at, got, pay, *messages):
    s, t, pair = merge(got)
    send_whole(s, t, pair, pay)
    for k in range(4):
        one, two, before = lower_states(s, t, pair, at[1] ^ k)
        messages[k][0:128, 0:128] = one.astype(BF)
        messages[k][0:128, 128:256] = two.astype(BF)
        messages[k][128:144, 0:128] = tail(before)
        messages[k][128:144, 128:256] = jnp.zeros((16, 128), BF)


def far_body(at, got, pay, message, before_out):
    s, t, pair = merge(got)
    send_whole(s, t, pair, pay)
    one, two, before = lower_states(s, t, pair, at[2])
    message[:, 0:128] = one.astype(BF)
    message[:, 128:256] = two.astype(BF)
    before_out[...] = jnp.broadcast_to(before, (8, 128))


def last_body(at, got, far, before, message):
    s, t, pair = merge(got)
    one, two, _ = lower_states(s, t, pair, at[3])
    earlier = jnp.exp(before[0:1, :])
    one, two = (one * earlier).astype(BF), (two * earlier).astype(BF)
    for i in range(4):
        message[i, :, 0:256] = far[...]
        message[i, :, 256:384] = one
        message[i, :, 384:512] = two


def place(s, core):
    at = core if s == 0 else 1 - core
    return at, pl.ds(pl.multiple_of(at * 256, 256), 256)


def own_body(at, keep, got, first, n0, n1, n2, n3, mixture, coef, near):
    core = at[0]
    for k, n in enumerate((n0, n1, n2, n3)):
        near[at[1] ^ k] = n[...]
    rows = lax.broadcasted_iota(jnp.int32, (256, 256), 0)
    cols = lax.broadcasted_iota(jnp.int32, (256, 256), 1)
    lower = rows >= cols
    upto = lower.astype(F32)
    both = (logs_of(keep), logs_of(got))
    for s, ref in enumerate((keep, got)):
        second, here = place(s, core)
        logs = both[s]
        at_row = exact(logs[0:8], upto, NT)
        at_col = exact(upto, logs[0:8], NT)
        level = logs.T
        first_log = jnp.sum(both[1 - s][0:4], axis=1, keepdims=True)
        first_log = jnp.where(second == 1, first_log, 0.0)
        for h in range(4):
            hc = slice(h * 128, h * 128 + 128)
            q, kb, v = ref[512:768, hc], ref[0:256, hc], ref[256:512, hc]
            local = at_col[:, h : h + 1]
            gap = jnp.where(lower, local - at_row[h : h + 1, :], -1e30)
            weights = (dot(q, kb, NT) * jnp.exp(gap)).astype(BF)
            m = [level[:, 4 + 4 * l + h : 5 + 4 * l + h] for l in range(8)]
            total = dot(weights, v) * m[0]
            start = jnp.exp(local)
            total += dot(q, first[h]) * jnp.where(second == 1, start * m[1], 0.0)
            start = start * jnp.exp(first_log[h : h + 1])
            read = dot(q, near[h, 0:128, :])
            total += read[:, 0:128] * (start * m[2]) + read[:, 128:256] * (start * m[3])
            mixture[here, hc] = total
            start = start * jnp.exp(untail(near[h, 128:144, 0:128])[:, 0:1])
            for l in range(4, 8):
                coef[here, 4 * h + l - 4 : 4 * h + l - 3] = start * m[l]


def norm_body(at, keep, got, gain, mixture, coef, last, normed):
    core = at[0]
    for s, ref in enumerate((keep, got)):
        _, here = place(s, core)
        for h in range(4):
            mine = pl.ds(pl.multiple_of(core * 512 + h * 128, 128), 128)
            hc = slice(h * 128, h * 128 + 128)
            q, z = ref[512:768, hc], ref[768:1024, hc].astype(F32)
            total = mixture[here, hc]
            for l in range(0, 4, 2):
                read = dot(q, last[h, :, l * 128 : l * 128 + 256])
                total += read[:, 0:128] * coef[here, 4 * h + l : 4 * h + l + 1]
                total += read[:, 128:256] * coef[here, 4 * h + l + 1 : 4 * h + l + 2]
            gated = total * (z / (1.0 + jnp.exp(-z)))
            size = lax.rsqrt(jnp.mean(gated * gated, axis=1, keepdims=True) + 1e-05)
            normed[here, hc] = (gated * size * gain[:, mine].astype(F32)).astype(BF)


def project_body(other, at, b0, b1, b2, b3, right, out, total):
    step = pl.program_id(0)
    row = (1 - at[0]) if other else at[0]
    rows = pl.ds(pl.multiple_of(row * 256, 256), 256)
    for j, block in enumerate((b0, b1, b2, b3)):

        @pl.when(step == j)
        def _():
            part = dot(block[rows, :], right[...].reshape(1024, 512), NT)
            if j == 0:
                total[...] = part
            elif j < 3:
                total[...] += part
            else:
                out[...] = (total[...] + part).astype(out.dtype)


def project(at, blocks, right, other):
    whole_block = pl.BlockSpec((512, 512), lambda k, at: (0, 0))
    return pl.pallas_call(
        functools.partial(project_body, other),
        out_shape=jax.ShapeDtypeStruct((256, 1024), BF if other else F32),
        grid_spec=pltpu.PrefetchScalarGridSpec(
            num_scalar_prefetch=1,
            grid=(4,),
            in_specs=[whole_block] * 4
            + [pl.BlockSpec((16, 1, 64, 512), lambda k, at: (0, (at[4] + 4 - k) % 4, 0, 0))],
            out_specs=pl.BlockSpec((256, 1024), lambda k, at: (0, 0)),
            scratch_shapes=[pltpu.VMEM((256, 1024), F32)],
        ),
        compiler_params=pltpu.CompilerParams(vmem_limit_bytes=32 * 2**20),
        cost_estimate=pl.CostEstimate(
            flops=2**30, bytes_accessed=6 * 2**20, transcendentals=0
        ),
    )(at, *blocks, right)


def shards(values, keys, queries, gates, log_decay, level_mix, norm_gain, weight):
    y, a, b, c, x = (lax.axis_index(n) for n in ("y", "a", "b", "c", "x"))
    at = jnp.stack([c, b, a, y, x]).astype(jnp.int32)
    block = ((LOGS + 48, 512), BF)
    keep, send, w_same, w_other = call(
        pack_body,
        [block, block, ((32, 512), BF), ((32, 512), BF)],
        (at, keys, values, queries, gates, log_decay, level_mix, weight),
        scratch=[
            pltpu.VMEM((8, 256), F32),
            pltpu.VMEM((8, 8, 256), F32),
            pltpu.VMEM((32, 1024), BF),
            pltpu.SemaphoreType.DMA((11,)),
        ],
        hbm=range(1, 8),
    )
    turned = []
    for other, part in ((0, w_same), (1, w_other)):
        perm = [
            ((s * 4 + f) * 2 + k, (f * 4 + s) * 2 + (k ^ other))
            for s in range(4)
            for f in range(4)
            for k in range(2)
        ]
        perm = [(flat(p), flat(q)) for p, q in perm]
        turned.append(lax.ppermute(part, ("y", "c", "x"), perm))
    got = swap(send)
    first_rows = jnp.where(c == 0, turned[0], turned[1])
    later_rows = jnp.where(c == 0, turned[1], turned[0])
    mine = jnp.concatenate([first_rows, later_rows])
    mine = jnp.broadcast_to(mine[None], (4, 64, 512))
    mine = lax.all_to_all(mine, "y", 0, 0, tiled=True)
    gathered = lax.all_gather(mine, ("a", "b"))

    pay, first = call(
        ends_body, [((4, 144, 128), BF), ((4, 128, 128), BF)], (at, keep, got)
    )
    near = lax.all_to_all(pay, "b", 0, 0, tiled=True)
    pay, *near = call(near_body, [((4, 144, 128), BF)] + [((144, 256), BF)] * 4, (at, near))
    far = lax.all_to_all(pay, "a", 0, 0, tiled=True)
    near = near[:1] + [flip(near[k], "b", k) for k in (1, 2, 3)]
    mixture, coef = call(
        own_body,
        [((512, 512), F32), ((512, 16), F32)],
        (at, keep, got, first, *near),
        scratch=[pltpu.VMEM((4, 144, 256), BF)],
    )
    pay, far, before = call(
        far_body,
        [((4, 144, 128), BF), ((128, 256), BF), ((8, 128), F32)],
        (at, far),
        unread=(mixture,),
    )
    last = lax.all_to_all(pay, "y", 0, 0, tiled=True)
    (last,) = call(last_body, [((4, 128, 512), BF)], (at, last, far, before))
    last = lax.all_to_all(last, "b", 0, 0, tiled=True)
    (normed,) = call(
        norm_body,
        [((512, 512), BF)],
        (at, keep, got, norm_gain[None], mixture, coef, last),
    )

    blocks = [normed] + [
        lax.ppermute(normed, "x", [(i, (i + j) % 4) for i in range(4)]) for j in (1, 2, 3)
    ]
    theirs = swap(project(at, blocks, gathered, True))
    own = project(at, blocks, gathered, False)
    return (own + theirs.astype(F32)).astype(BF)


def solution(mesh):
    fine = Mesh(mesh.devices.reshape(4, 4, 4, 2, 4), SEQ + ("x",))
    return jax.shard_map(
        shards,
        mesh=fine,
        in_specs=(
            P(SEQ, "x"),
            P(SEQ, "x"),
            P(SEQ, "x"),
            P(SEQ, "x"),
            P("x", SEQ),
            P(None, "x", SEQ),
            P("x"),
            P(SEQ, "x"),
        ),
        out_specs=P(SEQ, "x"),
        check_vma=False,
    )
```

```python
import functools

import jax
import jax.numpy as jnp
from jax import lax
from jax.experimental import pallas as pl
from jax.experimental.pallas import tpu as pltpu
from jax.sharding import Mesh, PartitionSpec as P

BF = jnp.bfloat16
F32 = jnp.float32
SEQ = ("y", "a", "p", "q", "c")
NEAR = ("p", "q")
NT = (((1,), (1,)), ((), ()))
TN = (((0,), (0,)), ((), ()))
LOGS = 1024


def swap(value):
    return lax.ppermute(value, "c", [(0, 1), (1, 0)])


def flip(value, axis, mask):
    return lax.ppermute(value, axis, [(i, i ^ mask) for i in range(4)])


def flat(place):
    y, x, core = place // 8, place // 2 % 4, place % 2
    return (y * 2 + core) * 4 + x


def dot(left, right, dims=(((1,), (0,)), ((), ()))):
    return lax.dot_general(left, right, dims, preferred_element_type=F32)


def exact(left, right, dims):
    return lax.dot_general(
        left, right, dims, precision=lax.Precision.HIGHEST, preferred_element_type=F32
    )


def tail(log):
    high = log.astype(BF).astype(F32)
    middle = (log - high).astype(BF).astype(F32)
    low = log - high - middle
    row = lax.broadcasted_iota(jnp.int32, (16, 128), 0)
    return jnp.where(
        row == 0, high, jnp.where(row == 1, middle, jnp.where(row == 2, low, 0.0))
    ).astype(BF)


def untail(tile):
    return jnp.sum(tile.astype(F32), axis=0, keepdims=True)


def call(body, outs, args, unread=(), scratch=(), hbm=()):
    specs = [pl.BlockSpec(memory_space=pltpu.SMEM)]
    specs += [
        pl.BlockSpec(memory_space=pltpu.HBM if i in hbm else pltpu.VMEM)
        for i in range(1, len(args))
    ]
    specs += [pl.BlockSpec(memory_space=pl.ANY)] * len(unread)

    def run(*refs):
        body(*refs[: len(args)], *refs[len(args) + len(unread) :])

    return pl.pallas_call(
        run,
        out_shape=[jax.ShapeDtypeStruct(*o) for o in outs],
        in_specs=specs,
        out_specs=[pl.BlockSpec(memory_space=pltpu.VMEM)] * len(outs),
        scratch_shapes=list(scratch),
        compiler_params=pltpu.CompilerParams(vmem_limit_bytes=32 * 2**20),
        cost_estimate=pl.CostEstimate(flops=10**6, bytes_accessed=10**6, transcendentals=0),
    )(*args, *unread)


def pack_body(
    at, keys, values, queries, gates, decay, mix, weight,
    keep, send, w_same, w_other, small, levels, wide, sems,
):
    core = at[0]
    mine = pl.ds(pl.multiple_of(core * 512, 512), 512)
    theirs = pl.ds(pl.multiple_of((1 - core) * 512, 512), 512)
    copies = [
        pltpu.make_async_copy(decay, small, sems.at[0]),
        pltpu.make_async_copy(mix, levels, sems.at[1]),
        pltpu.make_async_copy(weight, wide, sems.at[2]),
    ]
    for i, ref in enumerate((keys, values, queries, gates)):
        rows = pl.ds(i * 256, 256)
        for out, cols, n in ((send, theirs, 3), (keep, mine, 7)):
            copies.append(pltpu.make_async_copy(ref.at[:, cols], out.at[rows, :], sems.at[n + i]))
    for copy in copies:
        copy.start()
    for copy in copies[:3]:
        copy.wait()
    w_same[...] = wide[:, mine]
    w_other[...] = wide[:, theirs]
    for out, low in ((keep, core == 0), (send, core == 1)):
        logs = [jnp.where(low, small[0:4], small[4:8])]
        logs += [jnp.where(low, levels[l, 0:4], levels[l, 4:8]) for l in range(8)]
        logs = jnp.concatenate(logs + [jnp.zeros((12, 256), F32)], axis=0)
        high = logs.astype(BF)
        out[LOGS:, 0:256] = high
        out[LOGS:, 256:512] = (logs - high.astype(F32)).astype(BF)
    for copy in copies[3:]:
        copy.wait()


def logs_of(block):
    tile = block[LOGS:, :].astype(F32)
    return tile[:, 0:256] + tile[:, 256:512]


def ends_body(at, keep, got, pay, first):
    core = at[0]
    logs = jnp.concatenate([logs_of(keep)[0:4], logs_of(got)[0:4]], axis=0)
    after = (
        lax.broadcasted_iota(jnp.int32, (256, 256), 1)
        > lax.broadcasted_iota(jnp.int32, (256, 256), 0)
    ).astype(F32)
    scale = jnp.exp(exact(after, logs, NT))
    total = jnp.sum(logs, axis=1, keepdims=True)
    for h in range(4):
        cols = slice(h * 128, h * 128 + 128)
        end = []
        for i, ref in enumerate((keep, got)):
            scaled = ref[0:256, cols].astype(F32) * scale[:, 4 * i + h : 4 * i + h + 1]
            end.append(dot(scaled.astype(BF), ref[256:512, cols], TN))
        own_log, got_log = total[h : h + 1], total[4 + h : 5 + h]
        own_later = jnp.exp(jnp.where(core == 0, got_log, 0.0))
        got_later = jnp.exp(jnp.where(core == 0, 0.0, own_log))
        pay[h, 0:128, :] = (end[0] * own_later + end[1] * got_later).astype(BF)
        pay[h, 128:144, :] = tail(own_log + got_log)
        first[h, :, :] = jnp.where(core == 0, end[0], end[1]).astype(BF)


def merge(got):
    s = [got[i, 0:128, :].astype(F32) for i in range(4)]
    t = [untail(got[i, 128:144, :]) for i in range(4)]
    pair = s[0] * jnp.exp(t[1]) + s[1]
    return s, t, pair


def send_whole(s, t, pair, pay):
    state = (pair * jnp.exp(t[2] + t[3]) + s[2] * jnp.exp(t[3]) + s[3]).astype(BF)
    log = tail(t[0] + t[1] + t[2] + t[3])
    for i in range(4):
        pay[i, 0:128, :] = state
        pay[i, 128:144, :] = log


def lower_states(s, t, pair, at):
    odd, upper = at % 2 == 1, at >= 2
    one = jnp.where(odd, jnp.where(upper, s[2], s[0]), 0.0)
    step = jnp.where(odd, jnp.where(upper, t[2], t[0]), 0.0)
    two = jnp.where(upper, pair * jnp.exp(step), 0.0)
    before = sum(jnp.where(at > i, t[i], 0.0) for i in range(3))
    return one, two, before


def near_body(at, got, pay, *messages):
    s, t, pair = merge(got)
    send_whole(s, t, pair, pay)
    for k in range(4):
        one, two, before = lower_states(s, t, pair, at[1] ^ k)
        messages[k][0:128, 0:128] = one.astype(BF)
        messages[k][0:128, 128:256] = two.astype(BF)
        messages[k][128:144, 0:128] = tail(before)
        messages[k][128:144, 128:256] = jnp.zeros((16, 128), BF)


def far_body(at, got, pay, message, before_out):
    s, t, pair = merge(got)
    send_whole(s, t, pair, pay)
    one, two, before = lower_states(s, t, pair, at[2])
    message[:, 0:128] = one.astype(BF)
    message[:, 128:256] = two.astype(BF)
    before_out[...] = jnp.broadcast_to(before, (8, 128))


def last_body(at, got, far, before, message):
    s, t, pair = merge(got)
    one, two, _ = lower_states(s, t, pair, at[3])
    earlier = jnp.exp(before[0:1, :])
    one, two = (one * earlier).astype(BF), (two * earlier).astype(BF)
    for i in range(4):
        message[i, :, 0:256] = far[...]
        message[i, :, 256:384] = one
        message[i, :, 384:512] = two


def place(s, core):
    at = core if s == 0 else 1 - core
    return at, pl.ds(pl.multiple_of(at * 256, 256), 256)


def own_body(at, keep, got, first, mixture, coef):
    core = at[0]
    rows = lax.broadcasted_iota(jnp.int32, (256, 256), 0)
    cols = lax.broadcasted_iota(jnp.int32, (256, 256), 1)
    lower = rows >= cols
    upto = lower.astype(F32)
    both = (logs_of(keep), logs_of(got))
    for s, ref in enumerate((keep, got)):
        second, here = place(s, core)
        logs = both[s]
        at_row = exact(logs[0:8], upto, NT)
        at_col = exact(upto, logs[0:8], NT)
        level = logs.T
        first_log = jnp.sum(both[1 - s][0:4], axis=1, keepdims=True)
        first_log = jnp.where(second == 1, first_log, 0.0)
        for h in range(4):
            hc = slice(h * 128, h * 128 + 128)
            q, kb, v = ref[512:768, hc], ref[0:256, hc], ref[256:512, hc]
            local = at_col[:, h : h + 1]
            gap = jnp.where(lower, local - at_row[h : h + 1, :], -1e30)
            weights = (dot(q, kb, NT) * jnp.exp(gap)).astype(BF)
            m = [level[:, 4 + 4 * l + h : 5 + 4 * l + h] for l in range(8)]
            total = dot(weights, v) * m[0]
            start = jnp.exp(local)
            total += dot(q, first[h]) * jnp.where(second == 1, start * m[1], 0.0)
            mixture[here, hc] = total
            start = start * jnp.exp(first_log[h : h + 1])
            for l in range(2, 8):
                coef[here, 6 * h + l - 2 : 6 * h + l - 1] = start * m[l]


def near_mix_body(at, keep, got, mixture, coef, n0, n1, n2, n3, mixed, later, near):
    for k, n in enumerate((n0, n1, n2, n3)):
        near[at[1] ^ k] = n[...]
    for s, ref in enumerate((keep, got)):
        _, here = place(s, at[0])
        for h in range(4):
            hc = slice(h * 128, h * 128 + 128)
            read = dot(ref[512:768, hc], near[h, 0:128, :])
            total = mixture[here, hc] + read[:, 0:128] * coef[here, 6 * h : 6 * h + 1]
            mixed[here, hc] = total + read[:, 128:256] * coef[here, 6 * h + 1 : 6 * h + 2]
            before = jnp.exp(untail(near[h, 128:144, 0:128])[:, 0:1])
            later[here, 4 * h : 4 * h + 4] = coef[here, 6 * h + 2 : 6 * h + 6] * before


def norm_body(at, keep, got, gain, mixture, coef, last, normed):
    core = at[0]
    for s, ref in enumerate((keep, got)):
        _, here = place(s, core)
        for h in range(4):
            mine = pl.ds(pl.multiple_of(core * 512 + h * 128, 128), 128)
            hc = slice(h * 128, h * 128 + 128)
            q, z = ref[512:768, hc], ref[768:1024, hc].astype(F32)
            total = mixture[here, hc]
            for l in range(0, 4, 2):
                read = dot(q, last[h, :, l * 128 : l * 128 + 256])
                total += read[:, 0:128] * coef[here, 4 * h + l : 4 * h + l + 1]
                total += read[:, 128:256] * coef[here, 4 * h + l + 1 : 4 * h + l + 2]
            gated = total * (z / (1.0 + jnp.exp(-z)))
            size = lax.rsqrt(jnp.mean(gated * gated, axis=1, keepdims=True) + 1e-05)
            normed[here, hc] = (gated * size * gain[:, mine].astype(F32)).astype(BF)


def project_body(other, at, b0, b1, b2, b3, w0, w1, w2, w3, out, left, right, sems):
    row = (1 - at[0]) if other else at[0]
    rows = pl.ds(pl.multiple_of(row * 256, 256), 256)
    copies = [
        pltpu.make_async_copy(w, right.at[k], sems.at[k]) for k, w in enumerate((w0, w1, w2, w3))
    ]
    for copy in copies:
        copy.start()
    for j, block in enumerate((b0, b1, b2, b3)):
        left[(at[4] + 4 - j) % 4] = block[rows, :]
    total = 0.0
    for k, turn in enumerate((0, 1, 3, 2)):
        copies[k].wait()
        total += dot(left[(at[3] + turn) % 4], right[k].reshape(1024, 512), NT)
    out[...] = total.astype(out.dtype)


def project(at, blocks, rights, other):
    return call(
        functools.partial(project_body, other),
        [((256, 1024), BF if other else F32)],
        (at, *blocks, *rights),
        scratch=[
            pltpu.VMEM((4, 256, 512), BF),
            pltpu.VMEM((4, 16, 64, 512), BF),
            pltpu.SemaphoreType.DMA((4,)),
        ],
        hbm=range(5, 9),
    )[0]


def shards(values, keys, queries, gates, log_decay, level_mix, norm_gain, weight):
    y, a, b, q, c, x = (lax.axis_index(n) for n in ("y", "a", NEAR, "q", "c", "x"))
    at = jnp.stack([c, b, a, y, x]).astype(jnp.int32)
    block = ((LOGS + 48, 512), BF)
    keep, send, w_same, w_other = call(
        pack_body,
        [block, block, ((32, 512), BF), ((32, 512), BF)],
        (at, keys, values, queries, gates, log_decay, level_mix, weight),
        scratch=[
            pltpu.VMEM((8, 256), F32),
            pltpu.VMEM((8, 8, 256), F32),
            pltpu.VMEM((32, 1024), BF),
            pltpu.SemaphoreType.DMA((11,)),
        ],
        hbm=range(1, 8),
    )
    turned = []
    for other, part in ((0, w_same), (1, w_other)):
        perm = [
            ((s * 4 + f) * 2 + k, (f * 4 + s) * 2 + (k ^ other))
            for s in range(4)
            for f in range(4)
            for k in range(2)
        ]
        perm = [(flat(p), flat(q)) for p, q in perm]
        turned.append(lax.ppermute(part, ("y", "c", "x"), perm))
    got = swap(send)
    first_rows = jnp.where(c == 0, turned[0], turned[1])
    later_rows = jnp.where(c == 0, turned[1], turned[0])
    mine = jnp.concatenate([first_rows, later_rows])
    next_z = lax.ppermute(mine, "q", [(0, 1), (1, 0)])
    mine = jnp.stack([jnp.where(q == 0, mine, next_z), jnp.where(q == 0, next_z, mine)])
    right = lax.all_gather(mine, ("a", "p"), axis=0, tiled=True)
    rights = [right] + [
        lax.ppermute(right, "y", [(i, (i - k) % 4) for i in range(4)]) for k in (1, 3, 2)
    ]

    pay, first = call(
        ends_body, [((4, 144, 128), BF), ((4, 128, 128), BF)], (at, keep, got)
    )
    near = lax.all_to_all(pay, NEAR, 0, 0, tiled=True)
    pay, *near = call(near_body, [((4, 144, 128), BF)] + [((144, 256), BF)] * 4, (at, near))
    far = lax.all_to_all(pay, "a", 0, 0, tiled=True)
    near = near[:1] + [flip(near[k], NEAR, k) for k in (1, 2, 3)]
    mixture, coef = call(
        own_body,
        [((512, 512), F32), ((512, 24), F32)],
        (at, keep, got, first),
    )
    pay, far, before = call(
        far_body,
        [((4, 144, 128), BF), ((128, 256), BF), ((8, 128), F32)],
        (at, far),
        unread=(mixture,),
    )
    mixture, coef = call(
        near_mix_body,
        [((512, 512), F32), ((512, 16), F32)],
        (at, keep, got, mixture, coef, *near),
        scratch=[pltpu.VMEM((4, 144, 256), BF)],
    )
    last = lax.all_to_all(pay, "y", 0, 0, tiled=True)
    (last,) = call(
        last_body, [((4, 128, 512), BF)], (at, last, far, before), unread=(mixture,)
    )
    last = lax.all_to_all(last, NEAR, 0, 0, tiled=True)
    (normed,) = call(
        norm_body,
        [((512, 512), BF)],
        (at, keep, got, norm_gain[None], mixture, coef, last),
    )

    blocks = [normed] + [
        lax.ppermute(normed, "x", [(i, (i + j) % 4) for i in range(4)]) for j in (1, 2, 3)
    ]
    theirs = swap(project(at, blocks, rights, True))
    own = project(at, blocks, rights, False)
    return (own + theirs.astype(F32)).astype(BF)


def solution(mesh):
    fine = Mesh(mesh.devices.reshape(4, 4, 2, 2, 2, 4), SEQ + ("x",))
    return jax.shard_map(
        shards,
        mesh=fine,
        in_specs=(
            P(SEQ, "x"),
            P(SEQ, "x"),
            P(SEQ, "x"),
            P(SEQ, "x"),
            P("x", SEQ),
            P(None, "x", SEQ),
            P("x"),
            P(SEQ, "x"),
        ),
        out_specs=P(SEQ, "x"),
        check_vma=False,
    )
```

```python
import functools

import jax
import jax.numpy as jnp
from jax import lax
from jax.experimental import pallas as pl
from jax.experimental.pallas import tpu as pltpu
from jax.sharding import Mesh, PartitionSpec as P

BF = jnp.bfloat16
F32 = jnp.float32
SEQ = ("y", "a", "p", "q", "c")
NEAR = ("p", "q")
NT = (((1,), (1,)), ((), ()))
TN = (((0,), (0,)), ((), ()))
LOGS = 1024


def swap(value):
    return lax.ppermute(value, "c", [(0, 1), (1, 0)])


def flat(place):
    y, x, core = place // 8, place // 2 % 4, place % 2
    return (y * 2 + core) * 4 + x


def dot(left, right, dims=(((1,), (0,)), ((), ()))):
    return lax.dot_general(left, right, dims, preferred_element_type=F32)


def exact(left, right, dims):
    return lax.dot_general(
        left, right, dims, precision=lax.Precision.HIGHEST, preferred_element_type=F32
    )


def tails(logs):
    row = lax.broadcasted_iota(jnp.int32, (16, 128), 0)
    tile = jnp.zeros((16, 128), F32)
    for h, log in enumerate(logs):
        high = log.astype(BF).astype(F32)
        middle = (log - high).astype(BF).astype(F32)
        for i, term in enumerate((high, middle, log - high - middle)):
            tile = jnp.where(row == 3 * h + i, term, tile)
    return tile.astype(BF)


def untail(tile, h):
    return jnp.sum(tile[3 * h : 3 * h + 3].astype(F32), axis=0, keepdims=True)


def call(body, outs, args, unread=(), scratch=(), hbm=(), vmem=12):
    specs = [pl.BlockSpec(memory_space=pltpu.SMEM)]
    specs += [
        pl.BlockSpec(memory_space=pltpu.HBM if i in hbm else pltpu.VMEM)
        for i in range(1, len(args))
    ]
    specs += [pl.BlockSpec(memory_space=pl.ANY)] * len(unread)

    def run(*refs):
        body(*refs[: len(args)], *refs[len(args) + len(unread) :])

    return pl.pallas_call(
        run,
        out_shape=[jax.ShapeDtypeStruct(*o) for o in outs],
        in_specs=specs,
        out_specs=[pl.BlockSpec(memory_space=pltpu.VMEM)] * len(outs),
        scratch_shapes=list(scratch),
        compiler_params=pltpu.CompilerParams(vmem_limit_bytes=vmem * 2**20),
        cost_estimate=pl.CostEstimate(flops=10**6, bytes_accessed=10**6, transcendentals=0),
    )(*args, *unread)


def pack_body(
    at, keys, values, queries, gates, decay, mix, weight,
    keep, send, w_same, w_other, small, levels, wide, sems,
):
    core = at[0]
    mine = pl.ds(pl.multiple_of(core * 512, 512), 512)
    theirs = pl.ds(pl.multiple_of((1 - core) * 512, 512), 512)
    copies = [
        pltpu.make_async_copy(decay, small, sems.at[0]),
        pltpu.make_async_copy(mix, levels, sems.at[1]),
        pltpu.make_async_copy(weight, wide, sems.at[2]),
    ]
    for i, ref in enumerate((keys, values, queries, gates)):
        rows = pl.ds(i * 256, 256)
        for out, cols, n in ((send, theirs, 3), (keep, mine, 7)):
            copies.append(pltpu.make_async_copy(ref.at[:, cols], out.at[rows, :], sems.at[n + i]))
    for copy in copies:
        copy.start()
    for copy in copies[:3]:
        copy.wait()
    w_same[...] = wide[:, mine]
    w_other[...] = wide[:, theirs]
    for out, low in ((keep, core == 0), (send, core == 1)):
        logs = [jnp.where(low, small[0:4], small[4:8])]
        logs += [jnp.where(low, levels[l, 0:4], levels[l, 4:8]) for l in range(8)]
        logs = jnp.concatenate(logs + [jnp.zeros((12, 256), F32)], axis=0)
        high = logs.astype(BF)
        out[LOGS:, 0:256] = high
        out[LOGS:, 256:512] = (logs - high.astype(F32)).astype(BF)
    for copy in copies[3:]:
        copy.wait()


def logs_of(block):
    tile = block[LOGS:, :].astype(F32)
    return tile[:, 0:256] + tile[:, 256:512]


def ends_body(at, keep, got, pay, first):
    core = at[0]
    logs = jnp.concatenate([logs_of(keep)[0:4], logs_of(got)[0:4]], axis=0)
    after = (
        lax.broadcasted_iota(jnp.int32, (256, 256), 1)
        > lax.broadcasted_iota(jnp.int32, (256, 256), 0)
    ).astype(F32)
    scale = jnp.exp(exact(after, logs, NT))
    total = jnp.sum(logs, axis=1, keepdims=True)
    for h in range(4):
        cols = slice(h * 128, h * 128 + 128)
        end = []
        for i, ref in enumerate((keep, got)):
            scaled = ref[0:256, cols].astype(F32) * scale[:, 4 * i + h : 4 * i + h + 1]
            end.append(dot(scaled.astype(BF), ref[256:512, cols], TN))
        own_later = jnp.exp(jnp.where(core == 0, total[4 + h : 5 + h], 0.0))
        got_later = jnp.exp(jnp.where(core == 0, 0.0, total[h : h + 1]))
        state = (end[0] * own_later + end[1] * got_later).astype(BF)
        for i in range(4):
            pay[i, h * 128 : h * 128 + 128, :] = state
        first[h, :, :] = jnp.where(core == 0, end[0], end[1]).astype(BF)
    tile = tails([total[h : h + 1] + total[4 + h : 5 + h] for h in range(4)])
    for i in range(4):
        pay[i, 512:528, :] = tile


def lower_states(got, h, at):
    s = [got[i, h * 128 : h * 128 + 128, :].astype(F32) for i in range(4)]
    tiles = [got[i, 512:528, :] for i in range(4)]
    t = [untail(tile, h) for tile in tiles]
    pair = s[0] * jnp.exp(t[1]) + s[1]
    whole = pair * jnp.exp(t[2] + t[3]) + s[2] * jnp.exp(t[3]) + s[3]
    odd, upper = at % 2 == 1, at >= 2
    one = jnp.where(odd, jnp.where(upper, s[2], s[0]), 0.0).astype(BF)
    step = jnp.where(odd, jnp.where(upper, t[2], t[0]), 0.0)
    two = jnp.where(upper, pair * jnp.exp(step), 0.0).astype(BF)
    before = sum(jnp.where(at > i, t[i], 0.0) for i in range(3))
    return whole.astype(BF), t[0] + t[1] + t[2] + t[3], one, two, before


def merge_body(which, at, got, pay, levels, before_out):
    logs = []
    for h in range(4):
        whole, log, one, two, before = lower_states(got, h, at[which])
        logs.append(log)
        for i in range(4):
            pay[i, h * 128 : h * 128 + 128, :] = whole
        levels[h, :, 0:128] = one
        levels[h, :, 128:256] = two
        before_out[h, :, :] = jnp.broadcast_to(before, (8, 128))
    tile = tails(logs)
    for i in range(4):
        pay[i, 512:528, :] = tile


def place(s, core):
    at = core if s == 0 else 1 - core
    return at, pl.ds(pl.multiple_of(at * 256, 256), 256)


def own_body(at, keep, got, first, near, before, mixture, coef):
    core = at[0]
    rows = lax.broadcasted_iota(jnp.int32, (256, 256), 0)
    cols = lax.broadcasted_iota(jnp.int32, (256, 256), 1)
    lower = rows >= cols
    upto = lower.astype(F32)
    both = (logs_of(keep), logs_of(got))
    for s, ref in enumerate((keep, got)):
        second, here = place(s, core)
        logs = both[s]
        at_row = exact(logs[0:8], upto, NT)
        at_col = exact(upto, logs[0:8], NT)
        level = logs.T
        first_log = jnp.sum(both[1 - s][0:4], axis=1, keepdims=True)
        first_log = jnp.where(second == 1, first_log, 0.0)
        for h in range(4):
            hc = slice(h * 128, h * 128 + 128)
            q, kb, v = ref[512:768, hc], ref[0:256, hc], ref[256:512, hc]
            local = at_col[:, h : h + 1]
            gap = jnp.where(lower, local - at_row[h : h + 1, :], -1e30)
            weights = (dot(q, kb, NT) * jnp.exp(gap)).astype(BF)
            m = [level[:, 4 + 4 * l + h : 5 + 4 * l + h] for l in range(8)]
            total = dot(weights, v) * m[0]
            start = jnp.exp(local)
            total += dot(q, first[h]) * jnp.where(second == 1, start * m[1], 0.0)
            start = start * jnp.exp(first_log[h : h + 1])
            read = dot(q, near[h])
            total += read[:, 0:128] * (start * m[2]) + read[:, 128:256] * (start * m[3])
            mixture[here, hc] = total
            start = start * jnp.exp(before[h, 0:1, 0:1])
            for l in range(4, 8):
                coef[here, 4 * h + l - 4 : 4 * h + l - 3] = start * m[l]


def far_mix_body(at, keep, got, mixture, coef, far, mixed):
    for s, ref in enumerate((keep, got)):
        _, here = place(s, at[0])
        for h in range(4):
            hc = slice(h * 128, h * 128 + 128)
            read = dot(ref[512:768, hc], far[h])
            total = mixture[here, hc] + read[:, 0:128] * coef[here, 4 * h : 4 * h + 1]
            mixed[here, hc] = total + read[:, 128:256] * coef[here, 4 * h + 1 : 4 * h + 2]


def norm_body(at, keep, got, gain, mixture, coef, last, before, normed):
    core = at[0]
    for h in range(4):
        _, _, one, two, _ = lower_states(last, h, at[3])
        earlier = jnp.exp(before[h, 0:1, 0:1])
        states = jnp.concatenate([one, two], axis=1)
        mine = pl.ds(pl.multiple_of(core * 512 + h * 128, 128), 128)
        hc = slice(h * 128, h * 128 + 128)
        for s, ref in enumerate((keep, got)):
            _, here = place(s, core)
            z = ref[768:1024, hc].astype(F32)
            read = dot(ref[512:768, hc], states)
            total = mixture[here, hc]
            total += read[:, 0:128] * (coef[here, 4 * h + 2 : 4 * h + 3] * earlier)
            total += read[:, 128:256] * (coef[here, 4 * h + 3 : 4 * h + 4] * earlier)
            gated = total * (z / (1.0 + jnp.exp(-z)))
            size = lax.rsqrt(jnp.mean(gated * gated, axis=1, keepdims=True) + 1e-05)
            normed[here, hc] = (gated * size * gain[:, mine].astype(F32)).astype(BF)


def project_body(other, at, b0, b1, b2, b3, gathered, out, left, right, sems):
    row = (1 - at[0]) if other else at[0]
    rows = pl.ds(pl.multiple_of(row * 256, 256), 256)
    copies = [
        pltpu.make_async_copy(gathered.at[:, k], right.at[k], sems.at[k]) for k in range(4)
    ]
    for copy in copies:
        copy.start()
    for j, block in enumerate((b0, b1, b2, b3)):
        left[(at[4] + 4 - j) % 4] = block[rows, :]
    total = 0.0
    for k, turn in enumerate((0, 1, 3, 2)):
        copies[k].wait()
        total += dot(left[(at[3] + turn) % 4], right[k].reshape(1024, 512), NT)
    out[...] = total.astype(out.dtype)


def project(at, blocks, gathered, other):
    return call(
        functools.partial(project_body, other),
        [((256, 1024), BF if other else F32)],
        (at, *blocks, gathered),
        scratch=[
            pltpu.VMEM((4, 256, 512), BF),
            pltpu.VMEM((4, 16, 64, 512), BF),
            pltpu.SemaphoreType.DMA((4,)),
        ],
        hbm=(5,),
        vmem=56,
    )[0]


def shards(values, keys, queries, gates, log_decay, level_mix, norm_gain, weight):
    y, a, b, c, x = (lax.axis_index(n) for n in ("y", "a", NEAR, "c", "x"))
    at = jnp.stack([c, b, a, y, x]).astype(jnp.int32)
    block = ((LOGS + 48, 512), BF)
    keep, send, w_same, w_other = call(
        pack_body,
        [block, block, ((32, 512), BF), ((32, 512), BF)],
        (at, keys, values, queries, gates, log_decay, level_mix, weight),
        scratch=[
            pltpu.VMEM((8, 256), F32),
            pltpu.VMEM((8, 8, 256), F32),
            pltpu.VMEM((32, 1024), BF),
            pltpu.SemaphoreType.DMA((11,)),
        ],
        hbm=range(1, 8),
        vmem=60,
    )
    turned = []
    for other, part in ((0, w_same), (1, w_other)):
        perm = [
            ((s * 4 + f) * 2 + k, (f * 4 + s) * 2 + (k ^ other))
            for s in range(4)
            for f in range(4)
            for k in range(2)
        ]
        perm = [(flat(p), flat(q)) for p, q in perm]
        turned.append(lax.ppermute(part, ("y", "c", "x"), perm))
    got = swap(send)
    first_rows = jnp.where(c == 0, turned[0], turned[1])
    later_rows = jnp.where(c == 0, turned[1], turned[0])
    mine = jnp.concatenate([first_rows, later_rows])
    mine = jnp.stack(
        [mine]
        + [lax.ppermute(mine, "y", [(i, (i - k) % 4) for i in range(4)]) for k in (1, 3, 2)]
    )
    gathered = lax.all_gather(mine, ("a", "p", "q"))

    pay = ((4, 528, 128), BF)
    merged = [pay, ((4, 128, 256), BF), ((4, 8, 128), F32)]
    pay_b, first = call(ends_body, [pay, ((4, 128, 128), BF)], (at, keep, got))
    near = lax.all_to_all(pay_b, NEAR, 0, 0, tiled=True)
    pay_a, near, before_b = call(functools.partial(merge_body, 1), merged, (at, near))
    far = lax.all_to_all(pay_a, "a", 0, 0, tiled=True)
    mixture, coef = call(
        own_body,
        [((512, 512), F32), ((512, 16), F32)],
        (at, keep, got, first, near, before_b),
    )
    pay_y, far, before_a = call(
        functools.partial(merge_body, 2), merged, (at, far), unread=(mixture,)
    )
    last = lax.all_to_all(pay_y, "y", 0, 0, tiled=True)
    (mixture,) = call(
        far_mix_body, [((512, 512), F32)], (at, keep, got, mixture, coef, far)
    )
    (normed,) = call(
        norm_body,
        [((512, 512), BF)],
        (at, keep, got, norm_gain[None], mixture, coef, last, before_a),
    )

    blocks = [normed] + [
        lax.ppermute(normed, "x", [(i, (i + j) % 4) for i in range(4)]) for j in (1, 2, 3)
    ]
    theirs = swap(project(at, blocks, gathered, True))
    own = project(at, blocks, gathered, False)
    return (own + theirs.astype(F32)).astype(BF)


def solution(mesh):
    fine = Mesh(mesh.devices.reshape(4, 4, 2, 2, 2, 4), SEQ + ("x",))
    return jax.shard_map(
        shards,
        mesh=fine,
        in_specs=(
            P(SEQ, "x"),
            P(SEQ, "x"),
            P(SEQ, "x"),
            P(SEQ, "x"),
            P("x", SEQ),
            P(None, "x", SEQ),
            P("x"),
            P(SEQ, "x"),
        ),
        out_specs=P(SEQ, "x"),
        check_vma=False,
    )
```

```python
import functools

import jax
import jax.numpy as jnp
from jax import lax
from jax.experimental import pallas as pl
from jax.experimental.pallas import tpu as pltpu
from jax.sharding import Mesh, PartitionSpec as P

BF = jnp.bfloat16
F32 = jnp.float32
SEQ = ("y", "a", "p", "q", "c")
NEAR = ("p", "q")
NT = (((1,), (1,)), ((), ()))
TN = (((0,), (0,)), ((), ()))
LOGS = 1024


def swap(value):
    return lax.ppermute(value, "c", [(0, 1), (1, 0)])


def dot(left, right, dims=(((1,), (0,)), ((), ()))):
    return lax.dot_general(left, right, dims, preferred_element_type=F32)


def exact(left, right, dims):
    return lax.dot_general(
        left, right, dims, precision=lax.Precision.HIGHEST, preferred_element_type=F32
    )


def tail(log):
    high = log.astype(BF).astype(F32)
    middle = (log - high).astype(BF).astype(F32)
    low = log - high - middle
    row = lax.broadcasted_iota(jnp.int32, (16, 128), 0)
    return jnp.where(
        row == 0, high, jnp.where(row == 1, middle, jnp.where(row == 2, low, 0.0))
    ).astype(BF)


def untail(tile):
    return jnp.sum(tile.astype(F32), axis=0, keepdims=True)


def call(body, outs, args, unread=(), scratch=(), hbm=(), vmem=12):
    specs = [pl.BlockSpec(memory_space=pltpu.SMEM)]
    specs += [
        pl.BlockSpec(memory_space=pltpu.HBM if i in hbm else pltpu.VMEM)
        for i in range(1, len(args))
    ]
    specs += [pl.BlockSpec(memory_space=pl.ANY)] * len(unread)

    def run(*refs):
        body(*refs[: len(args)], *refs[len(args) + len(unread) :])

    return pl.pallas_call(
        run,
        out_shape=[jax.ShapeDtypeStruct(*o) for o in outs],
        in_specs=specs,
        out_specs=[pl.BlockSpec(memory_space=pltpu.VMEM)] * len(outs),
        scratch_shapes=list(scratch),
        compiler_params=pltpu.CompilerParams(vmem_limit_bytes=vmem * 2**20),
        cost_estimate=pl.CostEstimate(flops=10**6, bytes_accessed=10**6, transcendentals=0),
    )(*args, *unread)


def pack_body(at, keys, values, queries, gates, decay, mix, keep, send, small, levels, sems):
    core = at[0]
    mine = pl.ds(pl.multiple_of(core * 512, 512), 512)
    theirs = pl.ds(pl.multiple_of((1 - core) * 512, 512), 512)
    copies = [
        pltpu.make_async_copy(decay, small, sems.at[0]),
        pltpu.make_async_copy(mix, levels, sems.at[1]),
    ]
    for i, ref in enumerate((keys, values, queries, gates)):
        rows = pl.ds(i * 256, 256)
        for out, cols, n in ((send, theirs, 2), (keep, mine, 6)):
            copies.append(pltpu.make_async_copy(ref.at[:, cols], out.at[rows, :], sems.at[n + i]))
    for copy in copies:
        copy.start()
    for copy in copies[:2]:
        copy.wait()
    for out, low in ((keep, core == 0), (send, core == 1)):
        logs = [jnp.where(low, small[0:4], small[4:8])]
        logs += [jnp.where(low, levels[l, 0:4], levels[l, 4:8]) for l in range(8)]
        logs = jnp.concatenate(logs + [jnp.zeros((12, 256), F32)], axis=0)
        high = logs.astype(BF)
        out[LOGS:, 0:256] = high
        out[LOGS:, 256:512] = (logs - high.astype(F32)).astype(BF)
    for copy in copies[2:]:
        copy.wait()


def logs_of(block):
    tile = block[LOGS:, :].astype(F32)
    return tile[:, 0:256] + tile[:, 256:512]


def ends_body(at, keep, got, pay, first):
    core = at[0]
    logs = jnp.concatenate([logs_of(keep)[0:4], logs_of(got)[0:4]], axis=0)
    after = (
        lax.broadcasted_iota(jnp.int32, (256, 256), 1)
        > lax.broadcasted_iota(jnp.int32, (256, 256), 0)
    ).astype(F32)
    scale = jnp.exp(exact(after, logs, NT))
    total = jnp.sum(logs, axis=1, keepdims=True)
    for h in range(4):
        cols = slice(h * 128, h * 128 + 128)
        end = []
        for i, ref in enumerate((keep, got)):
            scaled = ref[0:256, cols].astype(F32) * scale[:, 4 * i + h : 4 * i + h + 1]
            end.append(dot(scaled.astype(BF), ref[256:512, cols], TN))
        own_log, got_log = total[h : h + 1], total[4 + h : 5 + h]
        own_later = jnp.exp(jnp.where(core == 0, got_log, 0.0))
        got_later = jnp.exp(jnp.where(core == 0, 0.0, own_log))
        pay[h, 0:128, :] = (end[0] * own_later + end[1] * got_later).astype(BF)
        pay[h, 128:144, :] = tail(own_log + got_log)
        first[h, :, :] = jnp.where(core == 0, end[0], end[1]).astype(BF)


def blocks_of(got):
    s = [got[i, 0:128, :].astype(F32) for i in range(4)]
    t = [untail(got[i, 128:144, :]) for i in range(4)]
    pair = s[0] * jnp.exp(t[1]) + s[1]
    return s, t, pair


def send_whole(s, t, pair, pay):
    state = (pair * jnp.exp(t[2] + t[3]) + s[2] * jnp.exp(t[3]) + s[3]).astype(BF)
    log = tail(t[0] + t[1] + t[2] + t[3])
    for i in range(4):
        pay[i, 0:128, :] = state
        pay[i, 128:144, :] = log


def lower_states(s, t, pair, at):
    odd, upper = at % 2 == 1, at >= 2
    one = jnp.where(odd, jnp.where(upper, s[2], s[0]), 0.0)
    step = jnp.where(odd, jnp.where(upper, t[2], t[0]), 0.0)
    two = jnp.where(upper, pair * jnp.exp(step), 0.0)
    before = sum(jnp.where(at > i, t[i], 0.0) for i in range(3))
    return one, two, before


def near_body(at, near, pay):
    send_whole(*blocks_of(near), pay)


def far_body(at, near, far, pay, m0, m1, m2, m3, before_out):
    s, t, pair = blocks_of(far)
    send_whole(s, t, pair, pay)
    three, four, before = lower_states(s, t, pair, at[2])
    before_out[...] = jnp.broadcast_to(before, (8, 128))
    s, t, pair = blocks_of(near)
    for k, message in enumerate((m0, m1, m2, m3)):
        one, two, before = lower_states(s, t, pair, at[1] ^ k)
        for i, state in enumerate((one, two, three, four)):
            message[0:128, i * 128 : i * 128 + 128] = state.astype(BF)
        message[128:144, 0:128] = tail(before)
        message[128:144, 128:512] = jnp.zeros((16, 384), BF)


def last_body(at, last, before, message):
    one, two, _ = lower_states(*blocks_of(last), at[3])
    earlier = jnp.exp(before[0:1, :])
    one, two = (one * earlier).astype(BF), (two * earlier).astype(BF)
    for i in range(4):
        message[i, :, 0:128] = one
        message[i, :, 128:256] = two


def place(s, core):
    at = core if s == 0 else 1 - core
    return at, pl.ds(pl.multiple_of(at * 256, 256), 256)


def own_body(at, keep, got, first, mixture, coef):
    core = at[0]
    rows = lax.broadcasted_iota(jnp.int32, (256, 256), 0)
    cols = lax.broadcasted_iota(jnp.int32, (256, 256), 1)
    lower = rows >= cols
    upto = lower.astype(F32)
    both = (logs_of(keep), logs_of(got))
    for s, ref in enumerate((keep, got)):
        second, here = place(s, core)
        logs = both[s]
        at_row = exact(logs[0:8], upto, NT)
        at_col = exact(upto, logs[0:8], NT)
        level = logs.T
        first_log = jnp.sum(both[1 - s][0:4], axis=1, keepdims=True)
        first_log = jnp.where(second == 1, first_log, 0.0)
        for h in range(4):
            hc = slice(h * 128, h * 128 + 128)
            q, kb, v = ref[512:768, hc], ref[0:256, hc], ref[256:512, hc]
            local = at_col[:, h : h + 1]
            gap = jnp.where(lower, local - at_row[h : h + 1, :], -1e30)
            weights = (dot(q, kb, NT) * jnp.exp(gap)).astype(BF)
            m = [level[:, 4 + 4 * l + h : 5 + 4 * l + h] for l in range(8)]
            total = dot(weights, v) * m[0]
            start = jnp.exp(local)
            total += dot(q, first[h]) * jnp.where(second == 1, start * m[1], 0.0)
            mixture[here, hc] = total
            start = start * jnp.exp(first_log[h : h + 1])
            for l in range(2, 8):
                coef[here, 6 * h + l - 2 : 6 * h + l - 1] = start * m[l]


def mix_body(at, keep, got, mixture, coef, m0, m1, m2, m3, mixed, later, states):
    for k, message in enumerate((m0, m1, m2, m3)):
        states[at[1] ^ k] = message[...]
    for h in range(4):
        before = jnp.exp(untail(states[h, 128:144, 0:128])[:, 0:1])
        hc = slice(h * 128, h * 128 + 128)
        for s, ref in enumerate((keep, got)):
            _, here = place(s, at[0])
            total = mixture[here, hc]
            for l in range(4):
                if l % 2 == 0:
                    read = dot(ref[512:768, hc], states[h, 0:128, l * 128 : l * 128 + 256])
                scale = coef[here, 6 * h + l : 6 * h + l + 1]
                scale = scale if l < 2 else scale * before
                total += read[:, (l % 2) * 128 : (l % 2) * 128 + 128] * scale
            mixed[here, hc] = total
            later[here, 2 * h : 2 * h + 2] = coef[here, 6 * h + 4 : 6 * h + 6] * before


def norm_body(at, keep, got, gain, mixture, coef, last, normed):
    core = at[0]
    for h in range(4):
        mine = pl.ds(pl.multiple_of(core * 512 + h * 128, 128), 128)
        hc = slice(h * 128, h * 128 + 128)
        for s, ref in enumerate((keep, got)):
            _, here = place(s, core)
            z = ref[768:1024, hc].astype(F32)
            read = dot(ref[512:768, hc], last[h])
            total = mixture[here, hc]
            total += read[:, 0:128] * coef[here, 2 * h : 2 * h + 1]
            total += read[:, 128:256] * coef[here, 2 * h + 1 : 2 * h + 2]
            gated = total * (z / (1.0 + jnp.exp(-z)))
            size = lax.rsqrt(jnp.mean(gated * gated, axis=1, keepdims=True) + 1e-05)
            normed[here, hc] = (gated * size * gain[:, mine].astype(F32)).astype(BF)


def project_body(
    other, at, a0, a1, a2, a3, b0, b1, b2, b3, gathered, w1, w2, w3, out, left, right, sems
):
    row = (1 - at[0]) if other else at[0]
    rows = pl.ds(pl.multiple_of(row * 256, 256), 256)
    pieces = [gathered.at[:, 0:512], gathered.at[:, 512:1024]]
    pieces += [gathered.at[:, 512 + 512 * k : 1024 + 512 * k] for k in (1, 2, 3)] + [w1, w2, w3]
    copies = [
        pltpu.make_async_copy(piece, right.at[i], sems.at[i]) for i, piece in enumerate(pieces)
    ]
    for copy in copies:
        copy.start()
    for j, (own, got) in enumerate(((a0, b0), (a1, b1), (a2, b2), (a3, b3))):
        spot = (at[4] + 4 - j) % 4
        left[at[0], spot] = own[rows, :]
        left[1 - at[0], spot] = got[rows, :]
    total = 0.0
    for i, (half, k) in enumerate(
        ((0, 0), (1, 0), (0, 1), (0, 2), (0, 3), (1, 1), (1, 2), (1, 3))
    ):
        copies[i].wait()
        total += dot(left[half, (at[3] + 4 - k) % 4], right[i], NT)
    out[...] = total.astype(BF)


def project(at, owns, gots, gathered, lates, other):
    return call(
        functools.partial(project_body, other),
        [((256, 512), BF)],
        (at, *owns, *gots, gathered, *lates),
        scratch=[
            pltpu.VMEM((2, 4, 256, 512), BF),
            pltpu.VMEM((8, 512, 512), BF),
            pltpu.SemaphoreType.DMA((8,)),
        ],
        hbm=range(9, 13),
        vmem=20,
    )[0]


def weave_body(at, own, got, out):
    core = at[0]
    i = lax.broadcasted_iota(jnp.int32, (128, 256), 0)
    j = lax.broadcasted_iota(jnp.int32, (128, 256), 1)
    spot = (i >> 5) * 64 + (i & 31)
    mine = (j == spot + core * 32).astype(BF)
    theirs = (j == spot + (1 - core) * 32).astype(BF)
    for m in range(4):
        cols = slice(m * 128, m * 128 + 128)
        both = dot(own[:, cols], mine) + dot(got[:, cols], theirs)
        out[:, m * 256 : m * 256 + 256] = both.astype(BF)


def shift(value, axis, by):
    return lax.ppermute(value, axis, [(i, (i + by) % 4) for i in range(4)])


def shards(values, keys, queries, gates, log_decay, level_mix, norm_gain, weight):
    y, a, b, c, x = (lax.axis_index(n) for n in ("y", "a", NEAR, "c", "x"))
    at = jnp.stack([c, b, a, y, x]).astype(jnp.int32)
    block = ((LOGS + 48, 512), BF)
    keep, send = call(
        pack_body,
        [block, block],
        (at, keys, values, queries, gates, log_decay, level_mix),
        scratch=[
            pltpu.VMEM((8, 256), F32),
            pltpu.VMEM((8, 8, 256), F32),
            pltpu.SemaphoreType.DMA((10,)),
        ],
        hbm=range(1, 7),
        vmem=60,
    )
    got = swap(send)
    mine = []
    for k in range(4):
        perm = [(s * 4 + f, ((f + k) % 4) * 4 + s) for s in range(4) for f in range(4)]
        mine.append(lax.ppermute(weight[:, : 512 if k else 1024], ("y", "x"), perm))
    mine = jnp.concatenate(mine, axis=1)
    gathered = lax.all_gather(mine, ("a", "p", "q"), axis=0, tiled=True)
    late = gathered[:, 512:1024]
    lates = [shift(late, "y", k) for k in (1, 2, 3)]

    pay = ((4, 144, 128), BF)
    pay_b, first = call(ends_body, [pay, ((4, 128, 128), BF)], (at, keep, got))
    near = lax.all_to_all(pay_b, NEAR, 0, 0, tiled=True)
    (pay_a,) = call(near_body, [pay], (at, near))
    far = lax.all_to_all(pay_a, "a", 0, 0, tiled=True)
    mixture, coef = call(
        own_body, [((512, 512), F32), ((512, 24), F32)], (at, keep, got, first)
    )
    pay_y, *messages, before = call(
        far_body,
        [pay] + [((144, 512), BF)] * 4 + [((8, 128), F32)],
        (at, near, far),
        unread=(mixture,),
    )
    last = lax.all_to_all(pay_y, "y", 0, 0, tiled=True)
    messages = messages[:1] + [
        lax.ppermute(messages[k], NEAR, [(i, i ^ k) for i in range(4)]) for k in (1, 2, 3)
    ]
    (last,) = call(last_body, [((4, 128, 256), BF)], (at, last, before))
    last = lax.all_to_all(last, NEAR, 0, 0, tiled=True)
    mixture, coef = call(
        mix_body,
        [((512, 512), F32), ((512, 8), F32)],
        (at, keep, got, mixture, coef, *messages),
        scratch=[pltpu.VMEM((4, 144, 512), BF)],
    )
    (normed,) = call(
        norm_body, [((512, 512), BF)], (at, keep, got, norm_gain[None], mixture, coef, last)
    )

    owns = [normed] + [shift(normed, "x", j) for j in (1, 2, 3)]
    gots = [swap(block) for block in owns]
    theirs = swap(project(at, owns, gots, gathered, lates, True))
    own = project(at, owns, gots, gathered, lates, False)
    return call(weave_body, [((256, 1024), BF)], (at, own, theirs))[0]


def solution(mesh):
    fine = Mesh(mesh.devices.reshape(4, 4, 2, 2, 2, 4), SEQ + ("x",))
    return jax.shard_map(
        shards,
        mesh=fine,
        in_specs=(
            P(SEQ, "x"),
            P(SEQ, "x"),
            P(SEQ, "x"),
            P(SEQ, "x"),
            P("x", SEQ),
            P(None, "x", SEQ),
            P("x"),
            P(SEQ, "x"),
        ),
        out_specs=P(SEQ, "x"),
        check_vma=False,
    )
```

```python
import functools

import jax
import jax.numpy as jnp
from jax import lax
from jax.experimental import pallas as pl
from jax.experimental.pallas import tpu as pltpu
from jax.sharding import Mesh, PartitionSpec as P

BF = jnp.bfloat16
F32 = jnp.float32
SEQ = ("y", "a", "p", "q", "c")
NEAR = ("p", "q")
NT = (((1,), (1,)), ((), ()))
TN = (((0,), (0,)), ((), ()))
LOGS = 1024
ROWS = 1104


def swap(value):
    return lax.ppermute(value, "c", [(0, 1), (1, 0)])


def dot(left, right, dims=(((1,), (0,)), ((), ()))):
    return lax.dot_general(left, right, dims, preferred_element_type=F32)


def exact(left, right, dims):
    return lax.dot_general(
        left, right, dims, precision=lax.Precision.HIGHEST, preferred_element_type=F32
    )


def tail(log):
    high = log.astype(BF).astype(F32)
    middle = (log - high).astype(BF).astype(F32)
    low = log - high - middle
    row = lax.broadcasted_iota(jnp.int32, (16, 128), 0)
    return jnp.where(
        row == 0, high, jnp.where(row == 1, middle, jnp.where(row == 2, low, 0.0))
    ).astype(BF)


def untail(tile):
    return jnp.sum(tile.astype(F32), axis=0, keepdims=True)


def call(body, outs, args, unread=(), scratch=(), hbm=(), vmem=12):
    specs = [pl.BlockSpec(memory_space=pltpu.SMEM)]
    specs += [
        pl.BlockSpec(memory_space=pltpu.HBM if i in hbm else pltpu.VMEM)
        for i in range(1, len(args))
    ]
    specs += [pl.BlockSpec(memory_space=pl.ANY)] * len(unread)

    def run(*refs):
        body(*refs[: len(args)], *refs[len(args) + len(unread) :])

    return pl.pallas_call(
        run,
        out_shape=[jax.ShapeDtypeStruct(*o) for o in outs],
        in_specs=specs,
        out_specs=[pl.BlockSpec(memory_space=pltpu.VMEM)] * len(outs),
        scratch_shapes=list(scratch),
        compiler_params=pltpu.CompilerParams(vmem_limit_bytes=vmem * 2**20),
        cost_estimate=pl.CostEstimate(flops=10**6, bytes_accessed=10**6, transcendentals=0),
    )(*args, *unread)


def pack_body(
    at, keys, values, queries, gates, weight, decay, mix, keep, send, small, levels, sems
):
    core = at[0]
    mine = pl.ds(pl.multiple_of(core * 512, 512), 512)
    theirs = pl.ds(pl.multiple_of((1 - core) * 512, 512), 512)
    copies = [
        pltpu.make_async_copy(decay, small, sems.at[0]),
        pltpu.make_async_copy(mix, levels, sems.at[1]),
    ]
    for i, ref in enumerate((keys, values, queries, gates, weight)):
        rows = pl.ds(i * 256, 256) if i < 4 else pl.ds(LOGS + 48, 32)
        for out, cols, n in ((send, theirs, 2), (keep, mine, 7)):
            copies.append(pltpu.make_async_copy(ref.at[:, cols], out.at[rows, :], sems.at[n + i]))
    for copy in copies:
        copy.start()
    for copy in copies[:2]:
        copy.wait()
    for out, low in ((keep, core == 0), (send, core == 1)):
        logs = [jnp.where(low, small[0:4], small[4:8])]
        logs += [jnp.where(low, levels[l, 0:4], levels[l, 4:8]) for l in range(8)]
        logs = jnp.concatenate(logs + [jnp.zeros((12, 256), F32)], axis=0)
        high = logs.astype(BF)
        out[LOGS : LOGS + 48, 0:256] = high
        out[LOGS : LOGS + 48, 256:512] = (logs - high.astype(F32)).astype(BF)
    for copy in copies[2:]:
        copy.wait()


def logs_of(block):
    tile = block[LOGS : LOGS + 48, :].astype(F32)
    return tile[:, 0:256] + tile[:, 256:512]


def ends_body(at, keep, got, pay, first):
    core = at[0]
    logs = jnp.concatenate([logs_of(keep)[0:4], logs_of(got)[0:4]], axis=0)
    after = (
        lax.broadcasted_iota(jnp.int32, (256, 256), 1)
        > lax.broadcasted_iota(jnp.int32, (256, 256), 0)
    ).astype(F32)
    scale = jnp.exp(exact(after, logs, NT))
    total = jnp.sum(logs, axis=1, keepdims=True)
    for h in range(4):
        cols = slice(h * 128, h * 128 + 128)
        end = []
        for i, ref in enumerate((keep, got)):
            scaled = ref[0:256, cols].astype(F32) * scale[:, 4 * i + h : 4 * i + h + 1]
            end.append(dot(scaled.astype(BF), ref[256:512, cols], TN))
        own_log, got_log = total[h : h + 1], total[4 + h : 5 + h]
        own_later = jnp.exp(jnp.where(core == 0, got_log, 0.0))
        got_later = jnp.exp(jnp.where(core == 0, 0.0, own_log))
        pay[h, 0:128, :] = (end[0] * own_later + end[1] * got_later).astype(BF)
        pay[h, 128:144, :] = tail(own_log + got_log)
        first[h, :, :] = jnp.where(core == 0, end[0], end[1]).astype(BF)


def blocks_of(got):
    s = [got[i, 0:128, :].astype(F32) for i in range(4)]
    t = [untail(got[i, 128:144, :]) for i in range(4)]
    pair = s[0] * jnp.exp(t[1]) + s[1]
    return s, t, pair


def send_whole(s, t, pair, pay):
    state = (pair * jnp.exp(t[2] + t[3]) + s[2] * jnp.exp(t[3]) + s[3]).astype(BF)
    log = tail(t[0] + t[1] + t[2] + t[3])
    for i in range(4):
        pay[i, 0:128, :] = state
        pay[i, 128:144, :] = log


def lower_states(s, t, pair, at):
    odd, upper = at % 2 == 1, at >= 2
    one = jnp.where(odd, jnp.where(upper, s[2], s[0]), 0.0)
    step = jnp.where(odd, jnp.where(upper, t[2], t[0]), 0.0)
    two = jnp.where(upper, pair * jnp.exp(step), 0.0)
    before = sum(jnp.where(at > i, t[i], 0.0) for i in range(3))
    return one, two, before


def near_body(at, near, pay):
    send_whole(*blocks_of(near), pay)


def far_body(at, far, pay, states, before_out):
    s, t, pair = blocks_of(far)
    send_whole(s, t, pair, pay)
    one, two, before = lower_states(s, t, pair, at[2])
    states[:, 0:128] = one.astype(BF)
    states[:, 128:256] = two.astype(BF)
    before_out[...] = jnp.broadcast_to(before, (8, 128))


def last_body(at, last, before, near, far, message):
    one, two, _ = lower_states(*blocks_of(last), at[3])
    earlier = jnp.exp(before[0:1, :])
    later = [state.astype(BF) for state in (one * earlier, two * earlier)]
    s, t, pair = blocks_of(near)
    for i in range(4):
        one, two, before_near = lower_states(s, t, pair, jnp.int32(i))
        message[i, 0:128, 0:128] = one.astype(BF)
        message[i, 0:128, 128:256] = two.astype(BF)
        message[i, 0:128, 256:512] = far[...]
        message[i, 0:128, 512:640] = later[0]
        message[i, 0:128, 640:768] = later[1]
        message[i, 128:144, 0:128] = tail(before_near)
        message[i, 128:144, 128:768] = jnp.zeros((16, 640), BF)


def place(s, core):
    at = core if s == 0 else 1 - core
    return at, pl.ds(pl.multiple_of(at * 256, 256), 256)


def own_body(at, keep, got, first, mixture, coef):
    core = at[0]
    rows = lax.broadcasted_iota(jnp.int32, (256, 256), 0)
    cols = lax.broadcasted_iota(jnp.int32, (256, 256), 1)
    lower = rows >= cols
    upto = lower.astype(F32)
    both = (logs_of(keep), logs_of(got))
    for s, ref in enumerate((keep, got)):
        second, here = place(s, core)
        logs = both[s]
        at_row = exact(logs[0:8], upto, NT)
        at_col = exact(upto, logs[0:8], NT)
        level = logs.T
        first_log = jnp.sum(both[1 - s][0:4], axis=1, keepdims=True)
        first_log = jnp.where(second == 1, first_log, 0.0)
        for h in range(4):
            hc = slice(h * 128, h * 128 + 128)
            q, kb, v = ref[512:768, hc], ref[0:256, hc], ref[256:512, hc]
            local = at_col[:, h : h + 1]
            gap = jnp.where(lower, local - at_row[h : h + 1, :], -1e30)
            weights = (dot(q, kb, NT) * jnp.exp(gap)).astype(BF)
            m = [level[:, 4 + 4 * l + h : 5 + 4 * l + h] for l in range(8)]
            total = dot(weights, v) * m[0]
            start = jnp.exp(local)
            total += dot(q, first[h]) * jnp.where(second == 1, start * m[1], 0.0)
            mixture[here, hc] = total
            start = start * jnp.exp(first_log[h : h + 1])
            for l in range(2, 8):
                coef[here, 6 * h + l - 2 : 6 * h + l - 1] = start * m[l]


def norm_body(at, keep, got, gain, mixture, coef, states, normed):
    core = at[0]
    for h in range(4):
        mine = pl.ds(pl.multiple_of(core * 512 + h * 128, 128), 128)
        hc = slice(h * 128, h * 128 + 128)
        before = jnp.exp(untail(states[h, 128:144, 0:128])[:, 0:1])
        for s, ref in enumerate((keep, got)):
            _, here = place(s, core)
            z = ref[768:1024, hc].astype(F32)
            total = mixture[here, hc]
            for l in range(6):
                if l % 2 == 0:
                    read = dot(ref[512:768, hc], states[h, 0:128, l * 128 : l * 128 + 256])
                scale = coef[here, 6 * h + l : 6 * h + l + 1]
                scale = scale if l < 2 else scale * before
                total += read[:, (l % 2) * 128 : (l % 2) * 128 + 128] * scale
            gated = total * (z / (1.0 + jnp.exp(-z)))
            size = lax.rsqrt(jnp.mean(gated * gated, axis=1, keepdims=True) + 1e-05)
            normed[here, hc] = (gated * size * gain[:, mine].astype(F32)).astype(BF)


def project_body(other, at, b0, b1, b2, b3, right, out, total):
    step = pl.program_id(0)
    row = (1 - at[0]) if other else at[0]
    rows = pl.ds(pl.multiple_of(row * 256, 256), 256)
    want = (at[4] - at[3] + step + 4) % 4

    @pl.when(step == 0)
    def _():
        total[...] = jnp.zeros_like(total)

    for j, block in enumerate((b0, b1, b2, b3)):

        @pl.when(want == j)
        def _():
            total[...] += dot(block[rows, :], right[...].reshape(1024, 512), NT)

    @pl.when(step == 3)
    def _():
        out[...] = total[...].astype(out.dtype)


def project(at, blocks, right, other):
    whole_block = pl.BlockSpec((512, 512), lambda k, at: (0, 0))
    return pl.pallas_call(
        functools.partial(project_body, other),
        out_shape=jax.ShapeDtypeStruct((256, 1024), BF if other else F32),
        grid_spec=pltpu.PrefetchScalarGridSpec(
            num_scalar_prefetch=1,
            grid=(4,),
            in_specs=[whole_block] * 4
            + [pl.BlockSpec((16, 64, 512), lambda k, at: (0, 0, k))],
            out_specs=pl.BlockSpec((256, 1024), lambda k, at: (0, 0)),
            scratch_shapes=[pltpu.VMEM((256, 1024), F32)],
        ),
        compiler_params=pltpu.CompilerParams(vmem_limit_bytes=20 * 2**20),
        cost_estimate=pl.CostEstimate(
            flops=2**30, bytes_accessed=6 * 2**20, transcendentals=0
        ),
    )(at, *blocks, right)


def shift(value, axis, by):
    return lax.ppermute(value, axis, [(i, (i + by) % 4) for i in range(4)])


def shards(values, keys, queries, gates, log_decay, level_mix, norm_gain, weight):
    y, a, b, c, x = (lax.axis_index(n) for n in ("y", "a", NEAR, "c", "x"))
    at = jnp.stack([c, b, a, y, x]).astype(jnp.int32)
    block = ((ROWS, 512), BF)
    keep, send = call(
        pack_body,
        [block, block],
        (at, keys, values, queries, gates, weight, log_decay, level_mix),
        scratch=[
            pltpu.VMEM((8, 256), F32),
            pltpu.VMEM((8, 8, 256), F32),
            pltpu.SemaphoreType.DMA((12,)),
        ],
        hbm=range(1, 8),
        vmem=60,
    )
    got = swap(send)
    pay = ((4, 144, 128), BF)
    pay_b, first = call(ends_body, [pay, ((4, 128, 128), BF)], (at, keep, got))

    kept, theirs = keep[LOGS + 48 :], got[LOGS + 48 :]
    both = jnp.concatenate(
        [jnp.where(c == 0, kept, theirs), jnp.where(c == 0, theirs, kept)]
    )
    both, pay_b = lax.optimization_barrier((both, pay_b))
    mine = []
    for k in range(4):
        perm = [(s * 4 + f, ((f + k) % 4) * 4 + s) for s in range(4) for f in range(4)]
        mine.append(lax.ppermute(both, ("y", "x"), perm))
    gathered = lax.all_gather(jnp.concatenate(mine, axis=1), ("a", "p", "q"))

    near = lax.all_to_all(pay_b, NEAR, 0, 0, tiled=True)
    (pay_a,) = call(near_body, [pay], (at, near))
    far = lax.all_to_all(pay_a, "a", 0, 0, tiled=True)
    mixture, coef = call(
        own_body, [((512, 512), F32), ((512, 24), F32)], (at, keep, got, first)
    )
    pay_y, far, before = call(
        far_body,
        [pay, ((128, 256), BF), ((8, 128), F32)],
        (at, far),
        unread=(mixture,),
    )
    last = lax.all_to_all(pay_y, "y", 0, 0, tiled=True)
    (last,) = call(last_body, [((4, 144, 768), BF)], (at, last, before, near, far))
    last = lax.all_to_all(last, NEAR, 0, 0, tiled=True)
    (normed,) = call(
        norm_body, [((512, 512), BF)], (at, keep, got, norm_gain[None], mixture, coef, last)
    )

    blocks = [normed] + [shift(normed, "x", j) for j in (1, 2, 3)]
    theirs = swap(project(at, blocks, gathered, True))
    own = project(at, blocks, gathered, False)
    return (own + theirs.astype(F32)).astype(BF)


def solution(mesh):
    fine = Mesh(mesh.devices.reshape(4, 4, 2, 2, 2, 4), SEQ + ("x",))
    return jax.shard_map(
        shards,
        mesh=fine,
        in_specs=(
            P(SEQ, "x"),
            P(SEQ, "x"),
            P(SEQ, "x"),
            P(SEQ, "x"),
            P("x", SEQ),
            P(None, "x", SEQ),
            P("x"),
            P(SEQ, "x"),
        ),
        out_specs=P(SEQ, "x"),
        check_vma=False,
    )
```

```python
import functools

import jax
import jax.numpy as jnp
from jax import lax
from jax.experimental import pallas as pl
from jax.experimental.pallas import tpu as pltpu
from jax.sharding import Mesh, PartitionSpec as P

BF = jnp.bfloat16
F32 = jnp.float32
SEQ = ("y", "a", "p", "q", "c")
NEAR = ("p", "q")
NT = (((1,), (1,)), ((), ()))
TN = (((0,), (0,)), ((), ()))
LOGS = 1024
ROWS = 1104


def swap(value):
    return lax.ppermute(value, "c", [(0, 1), (1, 0)])


def dot(left, right, dims=(((1,), (0,)), ((), ()))):
    return lax.dot_general(left, right, dims, preferred_element_type=F32)


def exact(left, right, dims):
    return lax.dot_general(
        left, right, dims, precision=lax.Precision.HIGHEST, preferred_element_type=F32
    )


def tail(log):
    high = log.astype(BF).astype(F32)
    middle = (log - high).astype(BF).astype(F32)
    low = log - high - middle
    row = lax.broadcasted_iota(jnp.int32, (16, 128), 0)
    return jnp.where(
        row == 0, high, jnp.where(row == 1, middle, jnp.where(row == 2, low, 0.0))
    ).astype(BF)


def untail(tile):
    return jnp.sum(tile.astype(F32), axis=0, keepdims=True)


def call(body, outs, args, unread=(), scratch=(), hbm=(), vmem=12):
    specs = [pl.BlockSpec(memory_space=pltpu.SMEM)]
    specs += [
        pl.BlockSpec(memory_space=pltpu.HBM if i in hbm else pltpu.VMEM)
        for i in range(1, len(args))
    ]
    specs += [pl.BlockSpec(memory_space=pl.ANY)] * len(unread)

    def run(*refs):
        body(*refs[: len(args)], *refs[len(args) + len(unread) :])

    return pl.pallas_call(
        run,
        out_shape=[jax.ShapeDtypeStruct(*o) for o in outs],
        in_specs=specs,
        out_specs=[pl.BlockSpec(memory_space=pltpu.VMEM)] * len(outs),
        scratch_shapes=list(scratch),
        compiler_params=pltpu.CompilerParams(vmem_limit_bytes=vmem * 2**20),
        cost_estimate=pl.CostEstimate(flops=10**6, bytes_accessed=10**6, transcendentals=0),
    )(*args, *unread)


def pack_body(
    at, keys, values, queries, gates, weight, decay, mix, keep, send, small, levels, sems
):
    core = at[0]
    mine = pl.ds(pl.multiple_of(core * 512, 512), 512)
    theirs = pl.ds(pl.multiple_of((1 - core) * 512, 512), 512)
    copies = [
        pltpu.make_async_copy(decay, small, sems.at[0]),
        pltpu.make_async_copy(mix, levels, sems.at[1]),
    ]
    for i, ref in enumerate((keys, values, queries, gates, weight)):
        rows = pl.ds(i * 256, 256) if i < 4 else pl.ds(LOGS + 48, 32)
        for out, cols, n in ((send, theirs, 2), (keep, mine, 7)):
            copies.append(pltpu.make_async_copy(ref.at[:, cols], out.at[rows, :], sems.at[n + i]))
    for copy in copies:
        copy.start()
    for copy in copies[:2]:
        copy.wait()
    for out, low in ((keep, core == 0), (send, core == 1)):
        logs = [jnp.where(low, small[0:4], small[4:8])]
        logs += [jnp.where(low, levels[l, 0:4], levels[l, 4:8]) for l in range(8)]
        logs = jnp.concatenate(logs + [jnp.zeros((12, 256), F32)], axis=0)
        high = logs.astype(BF)
        out[LOGS : LOGS + 48, 0:256] = high
        out[LOGS : LOGS + 48, 256:512] = (logs - high.astype(F32)).astype(BF)
    for copy in copies[2:]:
        copy.wait()


def logs_of(block):
    tile = block[LOGS : LOGS + 48, :].astype(F32)
    return tile[:, 0:256] + tile[:, 256:512]


def ends_body(at, keep, got, pay, first):
    core = at[0]
    logs = jnp.concatenate([logs_of(keep)[0:4], logs_of(got)[0:4]], axis=0)
    after = (
        lax.broadcasted_iota(jnp.int32, (256, 256), 1)
        > lax.broadcasted_iota(jnp.int32, (256, 256), 0)
    ).astype(F32)
    scale = jnp.exp(exact(after, logs, NT))
    total = jnp.sum(logs, axis=1, keepdims=True)
    for h in range(4):
        cols = slice(h * 128, h * 128 + 128)
        end = []
        for i, ref in enumerate((keep, got)):
            scaled = ref[0:256, cols].astype(F32) * scale[:, 4 * i + h : 4 * i + h + 1]
            end.append(dot(scaled.astype(BF), ref[256:512, cols], TN))
        own_log, got_log = total[h : h + 1], total[4 + h : 5 + h]
        own_later = jnp.exp(jnp.where(core == 0, got_log, 0.0))
        got_later = jnp.exp(jnp.where(core == 0, 0.0, own_log))
        pay[h, 0:128, :] = (end[0] * own_later + end[1] * got_later).astype(BF)
        pay[h, 128:144, :] = tail(own_log + got_log)
        first[h, :, :] = jnp.where(core == 0, end[0], end[1]).astype(BF)


def blocks_of(got):
    s = [got[i, 0:128, :].astype(F32) for i in range(4)]
    t = [untail(got[i, 128:144, :]) for i in range(4)]
    pair = s[0] * jnp.exp(t[1]) + s[1]
    return s, t, pair


def send_whole(s, t, pair, pay):
    state = (pair * jnp.exp(t[2] + t[3]) + s[2] * jnp.exp(t[3]) + s[3]).astype(BF)
    log = tail(t[0] + t[1] + t[2] + t[3])
    for i in range(4):
        pay[i, 0:128, :] = state
        pay[i, 128:144, :] = log


def lower_states(s, t, pair, at):
    odd, upper = at % 2 == 1, at >= 2
    one = jnp.where(odd, jnp.where(upper, s[2], s[0]), 0.0)
    step = jnp.where(odd, jnp.where(upper, t[2], t[0]), 0.0)
    two = jnp.where(upper, pair * jnp.exp(step), 0.0)
    before = sum(jnp.where(at > i, t[i], 0.0) for i in range(3))
    return one, two, before


def near_body(at, near, pay):
    send_whole(*blocks_of(near), pay)


def far_body(at, far, pay, states, before_out):
    s, t, pair = blocks_of(far)
    send_whole(s, t, pair, pay)
    one, two, before = lower_states(s, t, pair, at[2])
    states[:, 0:128] = one.astype(BF)
    states[:, 128:256] = two.astype(BF)
    before_out[...] = jnp.broadcast_to(before, (8, 128))


def last_body(at, last, before, near, far, message):
    one, two, _ = lower_states(*blocks_of(last), at[3])
    earlier = jnp.exp(before[0:1, :])
    later = [state.astype(BF) for state in (one * earlier, two * earlier)]
    s, t, pair = blocks_of(near)
    for i in range(4):
        one, two, before_near = lower_states(s, t, pair, jnp.int32(i))
        message[i, 0:128, 0:128] = one.astype(BF)
        message[i, 0:128, 128:256] = two.astype(BF)
        message[i, 0:128, 256:512] = far[...]
        message[i, 0:128, 512:640] = later[0]
        message[i, 0:128, 640:768] = later[1]
        message[i, 128:144, 0:128] = tail(before_near)
        message[i, 128:144, 128:768] = jnp.zeros((16, 640), BF)


def place(s, core):
    at = core if s == 0 else 1 - core
    return at, pl.ds(pl.multiple_of(at * 256, 256), 256)


def own_body(at, keep, got, first, mixture, coef):
    core = at[0]
    rows = lax.broadcasted_iota(jnp.int32, (256, 256), 0)
    cols = lax.broadcasted_iota(jnp.int32, (256, 256), 1)
    lower = rows >= cols
    upto = lower.astype(F32)
    both = (logs_of(keep), logs_of(got))
    for s, ref in enumerate((keep, got)):
        second, here = place(s, core)
        logs = both[s]
        at_row = exact(logs[0:8], upto, NT)
        at_col = exact(upto, logs[0:8], NT)
        level = logs.T
        first_log = jnp.sum(both[1 - s][0:4], axis=1, keepdims=True)
        first_log = jnp.where(second == 1, first_log, 0.0)
        for h in range(4):
            hc = slice(h * 128, h * 128 + 128)
            q, kb, v = ref[512:768, hc], ref[0:256, hc], ref[256:512, hc]
            local = at_col[:, h : h + 1]
            gap = jnp.where(lower, local - at_row[h : h + 1, :], -1e30)
            weights = (dot(q, kb, NT) * jnp.exp(gap)).astype(BF)
            m = [level[:, 4 + 4 * l + h : 5 + 4 * l + h] for l in range(8)]
            total = dot(weights, v) * m[0]
            start = jnp.exp(local)
            total += dot(q, first[h]) * jnp.where(second == 1, start * m[1], 0.0)
            mixture[here, hc] = total
            start = start * jnp.exp(first_log[h : h + 1])
            for l in range(2, 8):
                coef[here, 6 * h + l - 2 : 6 * h + l - 1] = start * m[l]


def norm_body(at, keep, got, gain, mixture, coef, states, normed):
    core = at[0]
    for h in range(4):
        mine = pl.ds(pl.multiple_of(core * 512 + h * 128, 128), 128)
        hc = slice(h * 128, h * 128 + 128)
        before = jnp.exp(untail(states[h, 128:144, 0:128])[:, 0:1])
        for s, ref in enumerate((keep, got)):
            _, here = place(s, core)
            z = ref[768:1024, hc].astype(F32)
            total = mixture[here, hc]
            for l in range(6):
                if l % 2 == 0:
                    read = dot(ref[512:768, hc], states[h, 0:128, l * 128 : l * 128 + 256])
                scale = coef[here, 6 * h + l : 6 * h + l + 1]
                scale = scale if l < 2 else scale * before
                total += read[:, (l % 2) * 128 : (l % 2) * 128 + 128] * scale
            gated = total * (z / (1.0 + jnp.exp(-z)))
            size = lax.rsqrt(jnp.mean(gated * gated, axis=1, keepdims=True) + 1e-05)
            normed[here, hc] = (gated * size * gain[:, mine].astype(F32)).astype(BF)


def project_body(other, at, b0, b1, b2, b3, right, next_right, far_right, out, total):
    step = pl.program_id(0)
    row = (1 - at[0]) if other else at[0]
    rows = pl.ds(pl.multiple_of(row * 256, 256), 256)
    turn = jnp.where(step == 2, 3, jnp.where(step == 3, 2, step))
    want = (at[4] - at[3] + turn + 4) % 4

    @pl.when(step == 0)
    def _():
        total[...] = jnp.zeros_like(total)

    for j, block in enumerate((b0, b1, b2, b3)):
        for ref, now in ((right, step < 2), (next_right, step == 2), (far_right, step == 3)):

            @pl.when(jnp.logical_and(want == j, now))
            def _():
                total[...] += dot(block[rows, :], ref[...].reshape(1024, 512), NT)

    @pl.when(step == 3)
    def _():
        out[...] = total[...].astype(out.dtype)


def project(at, blocks, right, next_right, far_right, other):
    whole_block = pl.BlockSpec((512, 512), lambda k, at: (0, 0))
    whole_right = pl.BlockSpec((16, 64, 512), lambda k, at: (0, 0, 0))
    return pl.pallas_call(
        functools.partial(project_body, other),
        out_shape=jax.ShapeDtypeStruct((256, 1024), BF if other else F32),
        grid_spec=pltpu.PrefetchScalarGridSpec(
            num_scalar_prefetch=1,
            grid=(4,),
            in_specs=[whole_block] * 4
            + [pl.BlockSpec((16, 64, 512), lambda k, at: (0, 0, jnp.minimum(k, 1)))]
            + [whole_right] * 2,
            out_specs=pl.BlockSpec((256, 1024), lambda k, at: (0, 0)),
            scratch_shapes=[pltpu.VMEM((256, 1024), F32)],
        ),
        compiler_params=pltpu.CompilerParams(vmem_limit_bytes=24 * 2**20),
        cost_estimate=pl.CostEstimate(
            flops=2**30, bytes_accessed=6 * 2**20, transcendentals=0
        ),
    )(at, *blocks, right, next_right, far_right)


def shift(value, axis, by):
    return lax.ppermute(value, axis, [(i, (i + by) % 4) for i in range(4)])


def shards(values, keys, queries, gates, log_decay, level_mix, norm_gain, weight):
    y, a, b, c, x = (lax.axis_index(n) for n in ("y", "a", NEAR, "c", "x"))
    at = jnp.stack([c, b, a, y, x]).astype(jnp.int32)
    block = ((ROWS, 512), BF)
    keep, send = call(
        pack_body,
        [block, block],
        (at, keys, values, queries, gates, weight, log_decay, level_mix),
        scratch=[
            pltpu.VMEM((8, 256), F32),
            pltpu.VMEM((8, 8, 256), F32),
            pltpu.SemaphoreType.DMA((12,)),
        ],
        hbm=range(1, 8),
        vmem=60,
    )
    got = swap(send)
    pay = ((4, 144, 128), BF)
    pay_b, first = call(ends_body, [pay, ((4, 128, 128), BF)], (at, keep, got))

    kept, theirs = keep[LOGS + 48 :], got[LOGS + 48 :]
    both = jnp.concatenate(
        [jnp.where(c == 0, kept, theirs), jnp.where(c == 0, theirs, kept)]
    )
    both, pay_b = lax.optimization_barrier((both, pay_b))
    mine = []
    for k in range(2):
        perm = [(s * 4 + f, ((f + k) % 4) * 4 + s) for s in range(4) for f in range(4)]
        mine.append(lax.ppermute(both, ("y", "x"), perm))
    mine = jnp.concatenate(mine, axis=1)
    gathered = lax.all_gather(mine, ("a", "p", "q"))

    near = lax.all_to_all(pay_b, NEAR, 0, 0, tiled=True)
    (pay_a,) = call(near_body, [pay], (at, near), unread=(mine,))
    far = lax.all_to_all(pay_a, "a", 0, 0, tiled=True)
    mixture, coef = call(
        own_body, [((512, 512), F32), ((512, 24), F32)], (at, keep, got, first)
    )
    pay_y, far, before = call(
        far_body,
        [pay, ((128, 256), BF), ((8, 128), F32)],
        (at, far),
        unread=(mixture,),
    )
    last = lax.all_to_all(pay_y, "y", 0, 0, tiled=True)
    (last,) = call(
        last_body, [((4, 144, 768), BF)], (at, last, before, near, far), vmem=60
    )
    last = lax.all_to_all(last, NEAR, 0, 0, tiled=True)
    last, gathered = lax.optimization_barrier((last, gathered))
    next_right = shift(gathered[:, :, :512], "y", 3)
    far_right = shift(gathered[:, :, 512:], "y", 1)
    (normed,) = call(
        norm_body,
        [((512, 512), BF)],
        (at, keep, got, norm_gain[None], mixture, coef, last),
        vmem=60,
    )

    blocks = [normed] + [shift(normed, "x", j) for j in (1, 2, 3)]
    theirs = swap(project(at, blocks, gathered, next_right, far_right, True))
    own = project(at, blocks, gathered, next_right, far_right, False)
    return (own + theirs.astype(F32)).astype(BF)


def solution(mesh):
    fine = Mesh(mesh.devices.reshape(4, 4, 2, 2, 2, 4), SEQ + ("x",))
    return jax.shard_map(
        shards,
        mesh=fine,
        in_specs=(
            P(SEQ, "x"),
            P(SEQ, "x"),
            P(SEQ, "x"),
            P(SEQ, "x"),
            P("x", SEQ),
            P(None, "x", SEQ),
            P("x"),
            P(SEQ, "x"),
        ),
        out_specs=P(SEQ, "x"),
        check_vma=False,
    )
```

```python
import functools

import jax
import jax.numpy as jnp
from jax import lax
from jax.experimental import pallas as pl
from jax.experimental.pallas import tpu as pltpu
from jax.sharding import Mesh, PartitionSpec as P

BF = jnp.bfloat16
F32 = jnp.float32
SEQ = ("y", "a", "p", "q", "c")
NEAR = ("p", "q")
NT = (((1,), (1,)), ((), ()))
TN = (((0,), (0,)), ((), ()))
LOGS = 1024
ROWS = 1072


def swap(value):
    return lax.ppermute(value, "c", [(0, 1), (1, 0)])


def dot(left, right, dims=(((1,), (0,)), ((), ()))):
    return lax.dot_general(left, right, dims, preferred_element_type=F32)


def exact(left, right, dims):
    return lax.dot_general(
        left, right, dims, precision=lax.Precision.HIGHEST, preferred_element_type=F32
    )


def tail(log):
    high = log.astype(BF).astype(F32)
    middle = (log - high).astype(BF).astype(F32)
    low = log - high - middle
    row = lax.broadcasted_iota(jnp.int32, (16, 128), 0)
    return jnp.where(
        row == 0, high, jnp.where(row == 1, middle, jnp.where(row == 2, low, 0.0))
    ).astype(BF)


def untail(tile):
    return jnp.sum(tile.astype(F32), axis=0, keepdims=True)


def call(body, outs, args, unread=(), scratch=(), hbm=(), vmem=12):
    specs = [pl.BlockSpec(memory_space=pltpu.SMEM)]
    specs += [
        pl.BlockSpec(memory_space=pltpu.HBM if i in hbm else pltpu.VMEM)
        for i in range(1, len(args))
    ]
    specs += [pl.BlockSpec(memory_space=pl.ANY)] * len(unread)

    def run(*refs):
        body(*refs[: len(args)], *refs[len(args) + len(unread) :])

    return pl.pallas_call(
        run,
        out_shape=[jax.ShapeDtypeStruct(*o) for o in outs],
        in_specs=specs,
        out_specs=[pl.BlockSpec(memory_space=pltpu.VMEM)] * len(outs),
        scratch_shapes=list(scratch),
        compiler_params=pltpu.CompilerParams(vmem_limit_bytes=vmem * 2**20),
        cost_estimate=pl.CostEstimate(flops=10**6, bytes_accessed=10**6, transcendentals=0),
    )(*args, *unread)


def pack_body(
    at, keys, values, queries, gates, decay, mix, keep, send, small, levels, sems
):
    core = at[0]
    mine = pl.ds(pl.multiple_of(core * 512, 512), 512)
    theirs = pl.ds(pl.multiple_of((1 - core) * 512, 512), 512)
    copies = [
        pltpu.make_async_copy(decay, small, sems.at[0]),
        pltpu.make_async_copy(mix, levels, sems.at[1]),
    ]
    for i, ref in enumerate((keys, values, queries, gates)):
        rows = pl.ds(i * 256, 256)
        for out, cols, n in ((send, theirs, 2), (keep, mine, 6)):
            copies.append(pltpu.make_async_copy(ref.at[:, cols], out.at[rows, :], sems.at[n + i]))
    for copy in copies:
        copy.start()
    for copy in copies[:2]:
        copy.wait()
    for out, low in ((keep, core == 0), (send, core == 1)):
        logs = [jnp.where(low, small[0:4], small[4:8])]
        logs += [jnp.where(low, levels[l, 0:4], levels[l, 4:8]) for l in range(8)]
        logs = jnp.concatenate(logs + [jnp.zeros((12, 256), F32)], axis=0)
        high = logs.astype(BF)
        out[LOGS : LOGS + 48, 0:256] = high
        out[LOGS : LOGS + 48, 256:512] = (logs - high.astype(F32)).astype(BF)
    for copy in copies[2:]:
        copy.wait()


def logs_of(block):
    tile = block[LOGS : LOGS + 48, :].astype(F32)
    return tile[:, 0:256] + tile[:, 256:512]


def ends_body(at, keep, got, pay, first):
    core = at[0]
    logs = jnp.concatenate([logs_of(keep)[0:4], logs_of(got)[0:4]], axis=0)
    after = (
        lax.broadcasted_iota(jnp.int32, (256, 256), 1)
        > lax.broadcasted_iota(jnp.int32, (256, 256), 0)
    ).astype(F32)
    scale = jnp.exp(exact(after, logs, NT))
    total = jnp.sum(logs, axis=1, keepdims=True)
    for h in range(4):
        cols = slice(h * 128, h * 128 + 128)
        end = []
        for i, ref in enumerate((keep, got)):
            scaled = ref[0:256, cols].astype(F32) * scale[:, 4 * i + h : 4 * i + h + 1]
            end.append(dot(scaled.astype(BF), ref[256:512, cols], TN))
        own_log, got_log = total[h : h + 1], total[4 + h : 5 + h]
        own_later = jnp.exp(jnp.where(core == 0, got_log, 0.0))
        got_later = jnp.exp(jnp.where(core == 0, 0.0, own_log))
        pay[h, 0:128, :] = (end[0] * own_later + end[1] * got_later).astype(BF)
        pay[h, 128:144, :] = tail(own_log + got_log)
        first[h, :, :] = jnp.where(core == 0, end[0], end[1]).astype(BF)


def blocks_of(got):
    s = [got[i, 0:128, :].astype(F32) for i in range(4)]
    t = [untail(got[i, 128:144, :]) for i in range(4)]
    pair = s[0] * jnp.exp(t[1]) + s[1]
    return s, t, pair


def send_whole(s, t, pair, pay):
    state = (pair * jnp.exp(t[2] + t[3]) + s[2] * jnp.exp(t[3]) + s[3]).astype(BF)
    log = tail(t[0] + t[1] + t[2] + t[3])
    for i in range(4):
        pay[i, 0:128, :] = state
        pay[i, 128:144, :] = log


def lower_states(s, t, pair, at):
    odd, upper = at % 2 == 1, at >= 2
    one = jnp.where(odd, jnp.where(upper, s[2], s[0]), 0.0)
    step = jnp.where(odd, jnp.where(upper, t[2], t[0]), 0.0)
    two = jnp.where(upper, pair * jnp.exp(step), 0.0)
    before = sum(jnp.where(at > i, t[i], 0.0) for i in range(3))
    return one, two, before


def near_body(at, near, pay):
    send_whole(*blocks_of(near), pay)


def far_body(at, near, far, message):
    s, t, pair = blocks_of(far)
    row = (pair * jnp.exp(t[2] + t[3]) + s[2] * jnp.exp(t[3]) + s[3]).astype(BF)
    row_log = tail(t[0] + t[1] + t[2] + t[3])
    three, four, before_far = lower_states(s, t, pair, at[2])
    three, four, before_far = three.astype(BF), four.astype(BF), tail(before_far)
    s, t, pair = blocks_of(near)
    for i in range(4):
        one, two, before = lower_states(s, t, pair, jnp.int32(i))
        for l, state in enumerate((one.astype(BF), two.astype(BF), three, four, row)):
            message[i, 0:128, l * 128 : l * 128 + 128] = state
        message[i, 128:144, 0:128] = tail(before)
        message[i, 128:144, 128:256] = before_far
        message[i, 128:144, 256:512] = jnp.zeros((16, 256), BF)
        message[i, 128:144, 512:640] = row_log


def spread_body(at, message, pay):
    for i in range(4):
        pay[i] = message[:, :, 512:640]


def place(s, core):
    at = core if s == 0 else 1 - core
    return at, pl.ds(pl.multiple_of(at * 256, 256), 256)


def own_body(at, keep, got, first, mixture, coef):
    core = at[0]
    rows = lax.broadcasted_iota(jnp.int32, (256, 256), 0)
    cols = lax.broadcasted_iota(jnp.int32, (256, 256), 1)
    lower = rows >= cols
    upto = lower.astype(F32)
    both = (logs_of(keep), logs_of(got))
    for s, ref in enumerate((keep, got)):
        second, here = place(s, core)
        logs = both[s]
        at_row = exact(logs[0:8], upto, NT)
        at_col = exact(upto, logs[0:8], NT)
        level = logs.T
        first_log = jnp.sum(both[1 - s][0:4], axis=1, keepdims=True)
        first_log = jnp.where(second == 1, first_log, 0.0)
        for h in range(4):
            hc = slice(h * 128, h * 128 + 128)
            q, kb, v = ref[512:768, hc], ref[0:256, hc], ref[256:512, hc]
            local = at_col[:, h : h + 1]
            gap = jnp.where(lower, local - at_row[h : h + 1, :], -1e30)
            weights = (dot(q, kb, NT) * jnp.exp(gap)).astype(BF)
            m = [level[:, 4 + 4 * l + h : 5 + 4 * l + h] for l in range(8)]
            total = dot(weights, v) * m[0]
            start = jnp.exp(local)
            total += dot(q, first[h]) * jnp.where(second == 1, start * m[1], 0.0)
            mixture[here, hc] = total
            start = start * jnp.exp(first_log[h : h + 1])
            for l in range(2, 8):
                coef[here, 6 * h + l - 2 : 6 * h + l - 1] = start * m[l]


def mix_body(at, keep, got, mixture, coef, states, mixed, later):
    for h in range(4):
        near = untail(states[h, 128:144, 0:128])[:, 0:1]
        far = untail(states[h, 128:144, 128:256])[:, 0:1]
        hc = slice(h * 128, h * 128 + 128)
        for s, ref in enumerate((keep, got)):
            _, here = place(s, at[0])
            total = mixture[here, hc]
            for l in range(4):
                if l % 2 == 0:
                    read = dot(ref[512:768, hc], states[h, 0:128, l * 128 : l * 128 + 256])
                scale = coef[here, 6 * h + l : 6 * h + l + 1]
                scale = scale if l < 2 else scale * jnp.exp(near)
                total += read[:, (l % 2) * 128 : (l % 2) * 128 + 128] * scale
            mixed[here, hc] = total
            later[here, 2 * h : 2 * h + 2] = coef[here, 6 * h + 4 : 6 * h + 6] * jnp.exp(near + far)


def norm_body(at, keep, got, gain, mixture, coef, rows, normed):
    core = at[0]
    for h in range(4):
        one, two, _ = lower_states(*blocks_of(rows.at[:, h]), at[3])
        states = jnp.concatenate([one.astype(BF), two.astype(BF)], axis=1)
        mine = pl.ds(pl.multiple_of(core * 512 + h * 128, 128), 128)
        hc = slice(h * 128, h * 128 + 128)
        for s, ref in enumerate((keep, got)):
            _, here = place(s, core)
            z = ref[768:1024, hc].astype(F32)
            read = dot(ref[512:768, hc], states)
            total = mixture[here, hc]
            total += read[:, 0:128] * coef[here, 2 * h : 2 * h + 1]
            total += read[:, 128:256] * coef[here, 2 * h + 1 : 2 * h + 2]
            gated = total * (z / (1.0 + jnp.exp(-z)))
            size = lax.rsqrt(jnp.mean(gated * gated, axis=1, keepdims=True) + 1e-05)
            normed[here, hc] = (gated * size * gain[:, mine].astype(F32)).astype(BF)


def project_body(other, at, b0, b1, b2, b3, gathered, next_right, far_right, out, left, right, sems):
    row = (1 - at[0]) if other else at[0]
    rows = pl.ds(pl.multiple_of(row * 256, 256), 256)
    pieces = (gathered.at[:, :, 0:512], gathered.at[:, :, 512:1024], next_right, far_right)
    copies = [
        pltpu.make_async_copy(piece, right.at[k], sems.at[k]) for k, piece in enumerate(pieces)
    ]
    for copy in copies:
        copy.start()
    for j, block in enumerate((b0, b1, b2, b3)):
        left[(at[4] + 4 - j) % 4] = block[rows, :]
    total = 0.0
    for k, turn in enumerate((0, 3, 1, 2)):
        copies[k].wait()
        total += dot(left[(at[3] + turn) % 4], right[k].reshape(1024, 512), NT)
    out[...] = total.astype(out.dtype)


def project(at, blocks, gathered, next_right, far_right, other):
    return call(
        functools.partial(project_body, other),
        [((256, 1024), BF if other else F32)],
        (at, *blocks, gathered, next_right, far_right),
        scratch=[
            pltpu.VMEM((4, 256, 512), BF),
            pltpu.VMEM((4, 16, 64, 512), BF),
            pltpu.SemaphoreType.DMA((4,)),
        ],
        hbm=(5, 6, 7),
        vmem=20,
    )[0]


def shift(value, axis, by):
    return lax.ppermute(value, axis, [(i, (i + by) % 4) for i in range(4)])


def shards(values, keys, queries, gates, log_decay, level_mix, norm_gain, weight):
    y, a, b, c, x = (lax.axis_index(n) for n in ("y", "a", NEAR, "c", "x"))
    at = jnp.stack([c, b, a, y, x]).astype(jnp.int32)
    kept = lax.dynamic_slice_in_dim(weight, c * 512, 512, 1)
    theirs = swap(lax.dynamic_slice_in_dim(weight, (1 - c) * 512, 512, 1))
    both = jnp.concatenate(
        [jnp.where(c == 0, kept, theirs), jnp.where(c == 0, theirs, kept)]
    )
    mine = []
    for k in range(2):
        perm = [(s * 4 + f, ((f + k) % 4) * 4 + s) for s in range(4) for f in range(4)]
        mine.append(lax.ppermute(both, ("y", "x"), perm))
    block = ((ROWS, 512), BF)
    keep, send = call(
        pack_body,
        [block, block],
        (at, keys, values, queries, gates, log_decay, level_mix),
        scratch=[
            pltpu.VMEM((8, 256), F32),
            pltpu.VMEM((8, 8, 256), F32),
            pltpu.SemaphoreType.DMA((10,)),
        ],
        hbm=range(1, 7),
        vmem=60,
    )
    mine, send = lax.optimization_barrier((mine, send))
    mine = jnp.concatenate(mine, axis=1)
    gathered = lax.all_gather(mine, ("a", "p", "q"))

    got = swap(send)
    pay = ((4, 144, 128), BF)
    pay_b, first = call(ends_body, [pay, ((4, 128, 128), BF)], (at, keep, got))
    near = lax.all_to_all(pay_b, NEAR, 0, 0, tiled=True)
    (pay_a,) = call(near_body, [pay], (at, near))
    far = lax.all_to_all(pay_a, "a", 0, 0, tiled=True)
    mixture, coef = call(
        own_body, [((512, 512), F32), ((512, 24), F32)], (at, keep, got, first)
    )
    (message,) = call(far_body, [((4, 144, 640), BF)], (at, near, far), unread=(mixture,))
    states = lax.all_to_all(message, NEAR, 0, 0, tiled=True)
    (pay_y,) = call(spread_body, [((4, 4, 144, 128), BF)], (at, states))
    rows = lax.all_to_all(pay_y, "y", 0, 0, tiled=True)
    mixture, coef = call(
        mix_body,
        [((512, 512), F32), ((512, 8), F32)],
        (at, keep, got, mixture, coef, states),
    )
    (normed,) = call(
        norm_body, [((512, 512), BF)], (at, keep, got, norm_gain[None], mixture, coef, rows)
    )

    normed, gathered = lax.optimization_barrier((normed, gathered))
    next_right = shift(gathered[:, :, :512], "y", 3)
    far_right = shift(gathered[:, :, 512:], "y", 1)
    blocks = [normed] + [shift(normed, "x", j) for j in (1, 2, 3)]
    theirs = swap(project(at, blocks, gathered, next_right, far_right, True))
    own = project(at, blocks, gathered, next_right, far_right, False)
    return (own + theirs.astype(F32)).astype(BF)


def solution(mesh):
    fine = Mesh(mesh.devices.reshape(4, 4, 2, 2, 2, 4), SEQ + ("x",))
    return jax.shard_map(
        shards,
        mesh=fine,
        in_specs=(
            P(SEQ, "x"),
            P(SEQ, "x"),
            P(SEQ, "x"),
            P(SEQ, "x"),
            P("x", SEQ),
            P(None, "x", SEQ),
            P("x"),
            P(SEQ, "x"),
        ),
        out_specs=P(SEQ, "x"),
        check_vma=False,
    )
```

```python
import functools

import jax
import jax.numpy as jnp
from jax import lax
from jax.experimental import pallas as pl
from jax.experimental.pallas import tpu as pltpu
from jax.sharding import Mesh, PartitionSpec as P

BF = jnp.bfloat16
F32 = jnp.float32
SEQ = ("y", "a", "p", "q", "c")
NEAR = ("p", "q")
NT = (((1,), (1,)), ((), ()))
TN = (((0,), (0,)), ((), ()))
LOGS = 1024
ROWS = 1072


def swap(value):
    return lax.ppermute(value, "c", [(0, 1), (1, 0)])


def dot(left, right, dims=(((1,), (0,)), ((), ()))):
    return lax.dot_general(left, right, dims, preferred_element_type=F32)


def exact(left, right, dims):
    return lax.dot_general(
        left, right, dims, precision=lax.Precision.HIGHEST, preferred_element_type=F32
    )


def tail(log):
    high = log.astype(BF).astype(F32)
    middle = (log - high).astype(BF).astype(F32)
    low = log - high - middle
    row = lax.broadcasted_iota(jnp.int32, (16, 128), 0)
    return jnp.where(
        row == 0, high, jnp.where(row == 1, middle, jnp.where(row == 2, low, 0.0))
    ).astype(BF)


def untail(tile):
    return jnp.sum(tile.astype(F32), axis=0, keepdims=True)


def call(body, outs, args, unread=(), scratch=(), hbm=(), vmem=12):
    specs = [pl.BlockSpec(memory_space=pltpu.SMEM)]
    specs += [
        pl.BlockSpec(memory_space=pltpu.HBM if i in hbm else pltpu.VMEM)
        for i in range(1, len(args))
    ]
    specs += [pl.BlockSpec(memory_space=pl.ANY)] * len(unread)

    def run(*refs):
        body(*refs[: len(args)], *refs[len(args) + len(unread) :])

    return pl.pallas_call(
        run,
        out_shape=[jax.ShapeDtypeStruct(*o) for o in outs],
        in_specs=specs,
        out_specs=[pl.BlockSpec(memory_space=pltpu.VMEM)] * len(outs),
        scratch_shapes=list(scratch),
        compiler_params=pltpu.CompilerParams(vmem_limit_bytes=vmem * 2**20),
        cost_estimate=pl.CostEstimate(flops=10**6, bytes_accessed=10**6, transcendentals=0),
    )(*args, *unread)


def pack_body(
    at, keys, values, queries, gates, decay, mix, keep, send, small, levels, sems
):
    core = at[0]
    mine = pl.ds(pl.multiple_of(core * 512, 512), 512)
    theirs = pl.ds(pl.multiple_of((1 - core) * 512, 512), 512)
    copies = [
        pltpu.make_async_copy(decay, small, sems.at[0]),
        pltpu.make_async_copy(mix, levels, sems.at[1]),
    ]
    for i, ref in enumerate((keys, values, queries, gates)):
        rows = pl.ds(i * 256, 256)
        for out, cols, n in ((send, theirs, 2), (keep, mine, 6)):
            copies.append(pltpu.make_async_copy(ref.at[:, cols], out.at[rows, :], sems.at[n + i]))
    for copy in copies:
        copy.start()
    for copy in copies[:2]:
        copy.wait()
    for out, low in ((keep, core == 0), (send, core == 1)):
        logs = [jnp.where(low, small[0:4], small[4:8])]
        logs += [jnp.where(low, levels[l, 0:4], levels[l, 4:8]) for l in range(8)]
        logs = jnp.concatenate(logs + [jnp.zeros((12, 256), F32)], axis=0)
        high = logs.astype(BF)
        out[LOGS : LOGS + 48, 0:256] = high
        out[LOGS : LOGS + 48, 256:512] = (logs - high.astype(F32)).astype(BF)
    for copy in copies[2:]:
        copy.wait()


def logs_of(block):
    tile = block[LOGS : LOGS + 48, :].astype(F32)
    return tile[:, 0:256] + tile[:, 256:512]


def ends_body(at, keep, got, pay, first):
    core = at[0]
    logs = jnp.concatenate([logs_of(keep)[0:4], logs_of(got)[0:4]], axis=0)
    after = (
        lax.broadcasted_iota(jnp.int32, (256, 256), 1)
        > lax.broadcasted_iota(jnp.int32, (256, 256), 0)
    ).astype(F32)
    scale = jnp.exp(exact(after, logs, NT))
    total = jnp.sum(logs, axis=1, keepdims=True)
    for h in range(4):
        cols = slice(h * 128, h * 128 + 128)
        end = []
        for i, ref in enumerate((keep, got)):
            scaled = ref[0:256, cols].astype(F32) * scale[:, 4 * i + h : 4 * i + h + 1]
            end.append(dot(scaled.astype(BF), ref[256:512, cols], TN))
        own_log, got_log = total[h : h + 1], total[4 + h : 5 + h]
        own_later = jnp.exp(jnp.where(core == 0, got_log, 0.0))
        got_later = jnp.exp(jnp.where(core == 0, 0.0, own_log))
        pay[h, 0:128, :] = (end[0] * own_later + end[1] * got_later).astype(BF)
        pay[h, 128:144, :] = tail(own_log + got_log)
        first[h, :, :] = jnp.where(core == 0, end[0], end[1]).astype(BF)


def blocks_of(got):
    s = [got[i, 0:128, :].astype(F32) for i in range(4)]
    t = [untail(got[i, 128:144, :]) for i in range(4)]
    pair = s[0] * jnp.exp(t[1]) + s[1]
    return s, t, pair


def send_whole(s, t, pair, pay):
    state = (pair * jnp.exp(t[2] + t[3]) + s[2] * jnp.exp(t[3]) + s[3]).astype(BF)
    log = tail(t[0] + t[1] + t[2] + t[3])
    for i in range(4):
        pay[i, 0:128, :] = state
        pay[i, 128:144, :] = log


def lower_states(s, t, pair, at):
    odd, upper = at % 2 == 1, at >= 2
    one = jnp.where(odd, jnp.where(upper, s[2], s[0]), 0.0)
    step = jnp.where(odd, jnp.where(upper, t[2], t[0]), 0.0)
    two = jnp.where(upper, pair * jnp.exp(step), 0.0)
    before = sum(jnp.where(at > i, t[i], 0.0) for i in range(3))
    return one, two, before


def near_body(at, near, pay, *messages):
    s, t, pair = blocks_of(near)
    send_whole(s, t, pair, pay)
    for k, message in enumerate(messages):
        one, two, before = lower_states(s, t, pair, at[1] ^ k)
        message[0:128, 0:128] = one.astype(BF)
        message[0:128, 128:256] = two.astype(BF)
        message[128:144, 0:128] = tail(before)
        message[128:144, 128:256] = jnp.zeros((16, 128), BF)


def far_body(at, far, pay, states, before_out):
    s, t, pair = blocks_of(far)
    send_whole(s, t, pair, pay)
    one, two, before = lower_states(s, t, pair, at[2])
    states[:, 0:128] = one.astype(BF)
    states[:, 128:256] = two.astype(BF)
    before_out[...] = jnp.broadcast_to(before, (8, 128))


def last_body(at, rows, before, far, message):
    one, two, _ = lower_states(*blocks_of(rows), at[3])
    earlier = jnp.exp(before[0:1, :])
    one, two = (one * earlier).astype(BF), (two * earlier).astype(BF)
    for i in range(4):
        message[i, :, 0:256] = far[...]
        message[i, :, 256:384] = one
        message[i, :, 384:512] = two


def place(s, core):
    at = core if s == 0 else 1 - core
    return at, pl.ds(pl.multiple_of(at * 256, 256), 256)


def own_body(at, keep, got, first, mixture, coef):
    core = at[0]
    rows = lax.broadcasted_iota(jnp.int32, (256, 256), 0)
    cols = lax.broadcasted_iota(jnp.int32, (256, 256), 1)
    lower = rows >= cols
    upto = lower.astype(F32)
    both = (logs_of(keep), logs_of(got))
    for s, ref in enumerate((keep, got)):
        second, here = place(s, core)
        logs = both[s]
        at_row = exact(logs[0:8], upto, NT)
        at_col = exact(upto, logs[0:8], NT)
        level = logs.T
        first_log = jnp.sum(both[1 - s][0:4], axis=1, keepdims=True)
        first_log = jnp.where(second == 1, first_log, 0.0)
        for h in range(4):
            hc = slice(h * 128, h * 128 + 128)
            q, kb, v = ref[512:768, hc], ref[0:256, hc], ref[256:512, hc]
            local = at_col[:, h : h + 1]
            gap = jnp.where(lower, local - at_row[h : h + 1, :], -1e30)
            weights = (dot(q, kb, NT) * jnp.exp(gap)).astype(BF)
            m = [level[:, 4 + 4 * l + h : 5 + 4 * l + h] for l in range(8)]
            total = dot(weights, v) * m[0]
            start = jnp.exp(local)
            total += dot(q, first[h]) * jnp.where(second == 1, start * m[1], 0.0)
            mixture[here, hc] = total
            start = start * jnp.exp(first_log[h : h + 1])
            for l in range(2, 8):
                coef[here, 6 * h + l - 2 : 6 * h + l - 1] = start * m[l]


def mix_body(at, keep, got, mixture, coef, n0, n1, n2, n3, mixed, later, near):
    for k, n in enumerate((n0, n1, n2, n3)):
        near[at[1] ^ k] = n[...]
    for h in range(4):
        before = jnp.exp(untail(near[h, 128:144, 0:128])[:, 0:1])
        hc = slice(h * 128, h * 128 + 128)
        for s, ref in enumerate((keep, got)):
            _, here = place(s, at[0])
            read = dot(ref[512:768, hc], near[h, 0:128, :])
            total = mixture[here, hc] + read[:, 0:128] * coef[here, 6 * h : 6 * h + 1]
            mixed[here, hc] = total + read[:, 128:256] * coef[here, 6 * h + 1 : 6 * h + 2]
            later[here, 4 * h : 4 * h + 4] = coef[here, 6 * h + 2 : 6 * h + 6] * before


def norm_body(at, keep, got, gain, mixture, coef, states, normed):
    core = at[0]
    for h in range(4):
        mine = pl.ds(pl.multiple_of(core * 512 + h * 128, 128), 128)
        hc = slice(h * 128, h * 128 + 128)
        for s, ref in enumerate((keep, got)):
            _, here = place(s, core)
            z = ref[768:1024, hc].astype(F32)
            total = mixture[here, hc]
            for l in range(0, 4, 2):
                read = dot(ref[512:768, hc], states[h, :, l * 128 : l * 128 + 256])
                total += read[:, 0:128] * coef[here, 4 * h + l : 4 * h + l + 1]
                total += read[:, 128:256] * coef[here, 4 * h + l + 1 : 4 * h + l + 2]
            gated = total * (z / (1.0 + jnp.exp(-z)))
            size = lax.rsqrt(jnp.mean(gated * gated, axis=1, keepdims=True) + 1e-05)
            normed[here, hc] = (gated * size * gain[:, mine].astype(F32)).astype(BF)


def project_body(other, at, b0, b1, b2, b3, gathered, next_right, far_right, out, left, right, sems):
    row = (1 - at[0]) if other else at[0]
    rows = pl.ds(pl.multiple_of(row * 256, 256), 256)
    pieces = (gathered.at[:, :, 0:512], gathered.at[:, :, 512:1024], next_right, far_right)
    copies = [
        pltpu.make_async_copy(piece, right.at[k], sems.at[k]) for k, piece in enumerate(pieces)
    ]
    for copy in copies:
        copy.start()
    for j, block in enumerate((b0, b1, b2, b3)):
        left[(at[4] + 4 - j) % 4] = block[rows, :]
    total = 0.0
    for k, turn in enumerate((0, 3, 1, 2)):
        copies[k].wait()
        total += dot(left[(at[3] + turn) % 4], right[k].reshape(1024, 512), NT)
    out[...] = total.astype(out.dtype)


def project(at, blocks, gathered, next_right, far_right, other):
    return call(
        functools.partial(project_body, other),
        [((256, 1024), BF if other else F32)],
        (at, *blocks, gathered, next_right, far_right),
        scratch=[
            pltpu.VMEM((4, 256, 512), BF),
            pltpu.VMEM((4, 16, 64, 512), BF),
            pltpu.SemaphoreType.DMA((4,)),
        ],
        hbm=(5, 6, 7),
        vmem=20,
    )[0]


def shift(value, axis, by):
    return lax.ppermute(value, axis, [(i, (i + by) % 4) for i in range(4)])


def shards(values, keys, queries, gates, log_decay, level_mix, norm_gain, weight):
    y, a, b, c, x = (lax.axis_index(n) for n in ("y", "a", NEAR, "c", "x"))
    at = jnp.stack([c, b, a, y, x]).astype(jnp.int32)
    kept = lax.dynamic_slice_in_dim(weight, c * 512, 512, 1)
    theirs = swap(lax.dynamic_slice_in_dim(weight, (1 - c) * 512, 512, 1))
    both = jnp.concatenate(
        [jnp.where(c == 0, kept, theirs), jnp.where(c == 0, theirs, kept)]
    )
    mine = []
    for k in range(2):
        perm = [(s * 4 + f, ((f + k) % 4) * 4 + s) for s in range(4) for f in range(4)]
        mine.append(lax.ppermute(both, ("y", "x"), perm))
    block = ((ROWS, 512), BF)
    keep, send = call(
        pack_body,
        [block, block],
        (at, keys, values, queries, gates, log_decay, level_mix),
        scratch=[
            pltpu.VMEM((8, 256), F32),
            pltpu.VMEM((8, 8, 256), F32),
            pltpu.SemaphoreType.DMA((10,)),
        ],
        hbm=range(1, 7),
        vmem=60,
    )
    mine, send = lax.optimization_barrier((mine, send))
    mine = jnp.concatenate(mine, axis=1)
    gathered = lax.all_gather(mine, ("a", "p", "q"))

    got = swap(send)
    pay = ((4, 144, 128), BF)
    pay_b, first = call(ends_body, [pay, ((4, 128, 128), BF)], (at, keep, got))
    near = lax.all_to_all(pay_b, NEAR, 0, 0, tiled=True)
    pay_a, *near = call(near_body, [pay] + [((144, 256), BF)] * 4, (at, near))
    far = lax.all_to_all(pay_a, "a", 0, 0, tiled=True)
    near = near[:1] + [
        lax.ppermute(near[k], NEAR, [(i, i ^ k) for i in range(4)]) for k in (1, 2, 3)
    ]
    mixture, coef = call(
        own_body, [((512, 512), F32), ((512, 24), F32)], (at, keep, got, first)
    )
    pay_y, far, before = call(
        far_body,
        [pay, ((128, 256), BF), ((8, 128), F32)],
        (at, far),
        unread=(mixture, *near[1:]),
    )
    rows = lax.all_to_all(pay_y, "y", 0, 0, tiled=True)
    (states,) = call(last_body, [((4, 128, 512), BF)], (at, rows, before, far))
    states = lax.all_to_all(states, NEAR, 0, 0, tiled=True)
    mixture, coef = call(
        mix_body,
        [((512, 512), F32), ((512, 16), F32)],
        (at, keep, got, mixture, coef, *near),
        scratch=[pltpu.VMEM((4, 144, 256), BF)],
    )
    (normed,) = call(
        norm_body, [((512, 512), BF)], (at, keep, got, norm_gain[None], mixture, coef, states)
    )

    _, gathered = lax.optimization_barrier((normed, gathered))
    next_right = shift(gathered[:, :, :512], "y", 3)
    far_right = shift(gathered[:, :, 512:], "y", 1)
    blocks = [normed] + [shift(normed, "x", j) for j in (1, 2, 3)]
    theirs = swap(project(at, blocks, gathered, next_right, far_right, True))
    own = project(at, blocks, gathered, next_right, far_right, False)
    return (own + theirs.astype(F32)).astype(BF)


def solution(mesh):
    fine = Mesh(mesh.devices.reshape(4, 4, 2, 2, 2, 4), SEQ + ("x",))
    return jax.shard_map(
        shards,
        mesh=fine,
        in_specs=(
            P(SEQ, "x"),
            P(SEQ, "x"),
            P(SEQ, "x"),
            P(SEQ, "x"),
            P("x", SEQ),
            P(None, "x", SEQ),
            P("x"),
            P(SEQ, "x"),
        ),
        out_specs=P(SEQ, "x"),
        check_vma=False,
    )
```

```python
import functools

import jax
import jax.numpy as jnp
from jax import lax
from jax.experimental import pallas as pl
from jax.experimental.pallas import tpu as pltpu
from jax.sharding import Mesh, PartitionSpec as P

BF = jnp.bfloat16
F32 = jnp.float32
SEQ = ("y", "a", "p", "q", "c")
NEAR = ("p", "q")
NT = (((1,), (1,)), ((), ()))
TN = (((0,), (0,)), ((), ()))
LOGS = 1024
ROWS = 1072


def swap(value):
    return lax.ppermute(value, "c", [(0, 1), (1, 0)])


def dot(left, right, dims=(((1,), (0,)), ((), ()))):
    return lax.dot_general(left, right, dims, preferred_element_type=F32)


def exact(left, right, dims):
    return lax.dot_general(
        left, right, dims, precision=lax.Precision.HIGHEST, preferred_element_type=F32
    )


def tail(log):
    high = log.astype(BF).astype(F32)
    middle = (log - high).astype(BF).astype(F32)
    low = log - high - middle
    row = lax.broadcasted_iota(jnp.int32, (16, 128), 0)
    return jnp.where(
        row == 0, high, jnp.where(row == 1, middle, jnp.where(row == 2, low, 0.0))
    ).astype(BF)


def untail(tile):
    return jnp.sum(tile.astype(F32), axis=0, keepdims=True)


def call(body, outs, args, unread=(), scratch=(), hbm=(), vmem=12):
    specs = [pl.BlockSpec(memory_space=pltpu.SMEM)]
    specs += [
        pl.BlockSpec(memory_space=pltpu.HBM if i in hbm else pltpu.VMEM)
        for i in range(1, len(args))
    ]
    specs += [pl.BlockSpec(memory_space=pl.ANY)] * len(unread)

    def run(*refs):
        body(*refs[: len(args)], *refs[len(args) + len(unread) :])

    return pl.pallas_call(
        run,
        out_shape=[jax.ShapeDtypeStruct(*o) for o in outs],
        in_specs=specs,
        out_specs=[pl.BlockSpec(memory_space=pltpu.VMEM)] * len(outs),
        scratch_shapes=list(scratch),
        compiler_params=pltpu.CompilerParams(vmem_limit_bytes=vmem * 2**20),
        cost_estimate=pl.CostEstimate(flops=10**6, bytes_accessed=10**6, transcendentals=0),
    )(*args, *unread)


def pack_body(
    at, keys, values, queries, gates, decay, mix, keep, send, small, levels, sems
):
    core = at[0]
    mine = pl.ds(pl.multiple_of(core * 512, 512), 512)
    theirs = pl.ds(pl.multiple_of((1 - core) * 512, 512), 512)
    copies = [
        pltpu.make_async_copy(decay, small, sems.at[0]),
        pltpu.make_async_copy(mix, levels, sems.at[1]),
    ]
    for i, ref in enumerate((keys, values, queries, gates)):
        rows = pl.ds(i * 256, 256)
        for out, cols, n in ((send, theirs, 2), (keep, mine, 6)):
            copies.append(pltpu.make_async_copy(ref.at[:, cols], out.at[rows, :], sems.at[n + i]))
    for copy in copies:
        copy.start()
    for copy in copies[:2]:
        copy.wait()
    for out, low in ((keep, core == 0), (send, core == 1)):
        logs = [jnp.where(low, small[0:4], small[4:8])]
        logs += [jnp.where(low, levels[l, 0:4], levels[l, 4:8]) for l in range(8)]
        logs = jnp.concatenate(logs + [jnp.zeros((12, 256), F32)], axis=0)
        high = logs.astype(BF)
        out[LOGS : LOGS + 48, 0:256] = high
        out[LOGS : LOGS + 48, 256:512] = (logs - high.astype(F32)).astype(BF)
    for copy in copies[2:]:
        copy.wait()


def logs_of(block, start=LOGS):
    tile = block[start : start + 48, :].astype(F32)
    return tile[:, 0:256] + tile[:, 256:512]


def ends_body(at, keep, got, pay, first, blocks, logs_in, sems):
    core = at[0]
    copies = []
    for i, ref in enumerate((keep, got)):
        copy = pltpu.make_async_copy(ref.at[LOGS : LOGS + 48], logs_in.at[i], sems.at[i, 4])
        copy.start()
        copies.append([copy])
    for h in range(4):
        cols = pl.ds(h * 128, 128)
        for i, ref in enumerate((keep, got)):
            copy = pltpu.make_async_copy(
                ref.at[0:512, cols], blocks.at[i, :, cols], sems.at[i, h]
            )
            copy.start()
            copies[i].append(copy)
    for i in range(2):
        copies[i][0].wait()
    logs = jnp.concatenate([logs_of(logs_in.at[i], 0)[0:4] for i in range(2)], axis=0)
    after = (
        lax.broadcasted_iota(jnp.int32, (256, 256), 1)
        > lax.broadcasted_iota(jnp.int32, (256, 256), 0)
    ).astype(F32)
    scale = jnp.exp(exact(after, logs, NT))
    total = jnp.sum(logs, axis=1, keepdims=True)
    for h in range(4):
        cols = slice(h * 128, h * 128 + 128)
        end = []
        for i in range(2):
            copies[i][1 + h].wait()
            scaled = blocks[i, 0:256, cols].astype(F32) * scale[:, 4 * i + h : 4 * i + h + 1]
            end.append(dot(scaled.astype(BF), blocks[i, 256:512, cols], TN))
        own_log, got_log = total[h : h + 1], total[4 + h : 5 + h]
        own_later = jnp.exp(jnp.where(core == 0, got_log, 0.0))
        got_later = jnp.exp(jnp.where(core == 0, 0.0, own_log))
        pay[h, 0:128, :] = (end[0] * own_later + end[1] * got_later).astype(BF)
        pay[h, 128:144, :] = tail(own_log + got_log)
        first[h, :, :] = jnp.where(core == 0, end[0], end[1]).astype(BF)


def blocks_of(got):
    s = [got[i, 0:128, :].astype(F32) for i in range(4)]
    t = [untail(got[i, 128:144, :]) for i in range(4)]
    pair = s[0] * jnp.exp(t[1]) + s[1]
    return s, t, pair


def send_whole(s, t, pair, pay):
    state = (pair * jnp.exp(t[2] + t[3]) + s[2] * jnp.exp(t[3]) + s[3]).astype(BF)
    log = tail(t[0] + t[1] + t[2] + t[3])
    for i in range(4):
        pay[i, 0:128, :] = state
        pay[i, 128:144, :] = log


def lower_states(s, t, pair, at):
    odd, upper = at % 2 == 1, at >= 2
    one = jnp.where(odd, jnp.where(upper, s[2], s[0]), 0.0)
    step = jnp.where(odd, jnp.where(upper, t[2], t[0]), 0.0)
    two = jnp.where(upper, pair * jnp.exp(step), 0.0)
    before = sum(jnp.where(at > i, t[i], 0.0) for i in range(3))
    return one, two, before


def near_body(at, near, pay, *messages):
    s, t, pair = blocks_of(near)
    send_whole(s, t, pair, pay)
    for k, message in enumerate(messages):
        one, two, before = lower_states(s, t, pair, at[1] ^ k)
        message[0:128, 0:128] = one.astype(BF)
        message[0:128, 128:256] = two.astype(BF)
        message[128:144, 0:128] = tail(before)
        message[128:144, 128:256] = jnp.zeros((16, 128), BF)


def far_body(at, far, pay, states, before_out):
    s, t, pair = blocks_of(far)
    send_whole(s, t, pair, pay)
    one, two, before = lower_states(s, t, pair, at[2])
    states[:, 0:128] = one.astype(BF)
    states[:, 128:256] = two.astype(BF)
    before_out[...] = jnp.broadcast_to(before, (8, 128))


def last_body(at, rows, before, far, message):
    one, two, _ = lower_states(*blocks_of(rows), at[3])
    earlier = jnp.exp(before[0:1, :])
    one, two = (one * earlier).astype(BF), (two * earlier).astype(BF)
    for i in range(4):
        message[i, :, 0:256] = far[...]
        message[i, :, 256:384] = one
        message[i, :, 384:512] = two


def place(s, core):
    at = core if s == 0 else 1 - core
    return at, pl.ds(pl.multiple_of(at * 256, 256), 256)


def own_body(at, keep, got, first, mixture, coef):
    core = at[0]
    rows = lax.broadcasted_iota(jnp.int32, (256, 256), 0)
    cols = lax.broadcasted_iota(jnp.int32, (256, 256), 1)
    lower = rows >= cols
    upto = lower.astype(F32)
    both = (logs_of(keep), logs_of(got))
    for s, ref in enumerate((keep, got)):
        second, here = place(s, core)
        logs = both[s]
        at_row = exact(logs[0:8], upto, NT)
        at_col = exact(upto, logs[0:8], NT)
        level = logs.T
        first_log = jnp.sum(both[1 - s][0:4], axis=1, keepdims=True)
        first_log = jnp.where(second == 1, first_log, 0.0)
        for h in range(4):
            hc = slice(h * 128, h * 128 + 128)
            q, kb, v = ref[512:768, hc], ref[0:256, hc], ref[256:512, hc]
            local = at_col[:, h : h + 1]
            gap = jnp.where(lower, local - at_row[h : h + 1, :], -1e30)
            weights = (dot(q, kb, NT) * jnp.exp(gap)).astype(BF)
            m = [level[:, 4 + 4 * l + h : 5 + 4 * l + h] for l in range(8)]
            total = dot(weights, v) * m[0]
            start = jnp.exp(local)
            total += dot(q, first[h]) * jnp.where(second == 1, start * m[1], 0.0)
            mixture[here, hc] = total
            start = start * jnp.exp(first_log[h : h + 1])
            for l in range(2, 8):
                coef[here, 6 * h + l - 2 : 6 * h + l - 1] = start * m[l]


def mix_body(at, keep, got, mixture, coef, n0, n1, n2, n3, mixed, later, near):
    for k, n in enumerate((n0, n1, n2, n3)):
        near[at[1] ^ k] = n[...]
    for h in range(4):
        before = jnp.exp(untail(near[h, 128:144, 0:128])[:, 0:1])
        hc = slice(h * 128, h * 128 + 128)
        for s, ref in enumerate((keep, got)):
            _, here = place(s, at[0])
            read = dot(ref[512:768, hc], near[h, 0:128, :])
            total = mixture[here, hc] + read[:, 0:128] * coef[here, 6 * h : 6 * h + 1]
            mixed[here, hc] = total + read[:, 128:256] * coef[here, 6 * h + 1 : 6 * h + 2]
            later[here, 4 * h : 4 * h + 4] = coef[here, 6 * h + 2 : 6 * h + 6] * before


def norm_body(
    at, keep, got, gain, mixture_in, coef_in, states_in, normed, blocks, mixture, coef, states, sems
):
    core = at[0]
    copies = [[pltpu.make_async_copy(coef_in, coef, sems.at[0, 4])]]
    copies[0][0].start()
    for h in range(4):
        cols = pl.ds(h * 128, 128)
        copies.append(
            [
                pltpu.make_async_copy(ref.at[512:1024, cols], blocks.at[i, :, cols], sems.at[i, h])
                for i, ref in enumerate((keep, got))
            ]
            + [
                pltpu.make_async_copy(mixture_in.at[:, cols], mixture.at[:, cols], sems.at[2, h]),
                pltpu.make_async_copy(states_in.at[h], states.at[h], sems.at[3, h]),
            ]
        )
        for copy in copies[-1]:
            copy.start()
    copies[0][0].wait()
    for h in range(4):
        mine = pl.ds(pl.multiple_of(core * 512 + h * 128, 128), 128)
        hc = slice(h * 128, h * 128 + 128)
        for copy in copies[1 + h]:
            copy.wait()
        for s in range(2):
            _, here = place(s, core)
            q, z = blocks[s, 0:256, hc], blocks[s, 256:512, hc].astype(F32)
            total = mixture[here, hc]
            for l in range(0, 4, 2):
                read = dot(q, states[h, :, l * 128 : l * 128 + 256])
                total += read[:, 0:128] * coef[here, 4 * h + l : 4 * h + l + 1]
                total += read[:, 128:256] * coef[here, 4 * h + l + 1 : 4 * h + l + 2]
            gated = total * (z / (1.0 + jnp.exp(-z)))
            size = lax.rsqrt(jnp.mean(gated * gated, axis=1, keepdims=True) + 1e-05)
            normed[here, hc] = (gated * size * gain[:, mine].astype(F32)).astype(BF)


def project_body(other, at, b0, b1, b2, b3, w0, w1, w2, w3, out, left, right, sems):
    row = (1 - at[0]) if other else at[0]
    rows = pl.ds(pl.multiple_of(row * 256, 256), 256)
    copies = [
        pltpu.make_async_copy(w, right.at[k], sems.at[k]) for k, w in enumerate((w0, w1, w2, w3))
    ]
    for copy in copies:
        copy.start()
    for j, block in enumerate((b0, b1, b2, b3)):
        left[(at[4] + 4 - j) % 4] = block[rows, :]
    total = 0.0
    for k, turn in enumerate((0, 1, 3, 2)):
        copies[k].wait()
        total += dot(left[(at[3] + turn) % 4], right[k].reshape(1024, 512), NT)
    out[...] = total.astype(out.dtype)


def project(at, blocks, rights, other):
    return call(
        functools.partial(project_body, other),
        [((256, 1024), BF if other else F32)],
        (at, *blocks, *rights),
        scratch=[
            pltpu.VMEM((4, 256, 512), BF),
            pltpu.VMEM((4, 16, 64, 512), BF),
            pltpu.SemaphoreType.DMA((4,)),
        ],
        hbm=range(5, 9),
        vmem=20,
    )[0]


def shift(value, axis, by):
    return lax.ppermute(value, axis, [(i, (i + by) % 4) for i in range(4)])


def shards(values, keys, queries, gates, log_decay, level_mix, norm_gain, weight):
    y, a, b, c, x = (lax.axis_index(n) for n in ("y", "a", NEAR, "c", "x"))
    at = jnp.stack([c, b, a, y, x]).astype(jnp.int32)
    kept = lax.dynamic_slice_in_dim(weight, c * 512, 512, 1)
    theirs = swap(lax.dynamic_slice_in_dim(weight, (1 - c) * 512, 512, 1))
    both = jnp.concatenate(
        [jnp.where(c == 0, kept, theirs), jnp.where(c == 0, theirs, kept)]
    )
    perm = [(s * 4 + f, f * 4 + s) for s in range(4) for f in range(4)]
    mine = lax.ppermute(both, ("y", "x"), perm)
    block = ((ROWS, 512), BF)
    keep, send = call(
        pack_body,
        [block, block],
        (at, keys, values, queries, gates, log_decay, level_mix),
        scratch=[
            pltpu.VMEM((8, 256), F32),
            pltpu.VMEM((8, 8, 256), F32),
            pltpu.SemaphoreType.DMA((10,)),
        ],
        hbm=range(1, 7),
        vmem=60,
    )
    mine, send = lax.optimization_barrier((mine, send))
    gathered = lax.all_gather(mine, ("a", "p", "q"))

    got = swap(send)
    pay = ((4, 144, 128), BF)
    pay_b, first = call(
        ends_body,
        [pay, ((4, 128, 128), BF)],
        (at, keep, got),
        scratch=[
            pltpu.VMEM((2, 512, 512), BF),
            pltpu.VMEM((2, 48, 512), BF),
            pltpu.SemaphoreType.DMA((2, 5)),
        ],
        hbm=(1, 2),
        vmem=60,
    )
    near = lax.all_to_all(pay_b, NEAR, 0, 0, tiled=True)
    pay_a, *near = call(near_body, [pay] + [((144, 256), BF)] * 4, (at, near))
    far = lax.all_to_all(pay_a, "a", 0, 0, tiled=True)
    near = near[:1] + [
        lax.ppermute(near[k], NEAR, [(i, i ^ k) for i in range(4)]) for k in (1, 2, 3)
    ]
    mixture, coef = call(
        own_body, [((512, 512), F32), ((512, 24), F32)], (at, keep, got, first), vmem=60
    )
    pay_y, far, before = call(
        far_body,
        [pay, ((128, 256), BF), ((8, 128), F32)],
        (at, far),
        unread=near[1:],
    )
    rows = lax.all_to_all(pay_y, "y", 0, 0, tiled=True)
    (states,) = call(
        last_body, [((4, 128, 512), BF)], (at, rows, before, far), unread=(mixture,)
    )
    states, gathered = lax.optimization_barrier((states, gathered))
    rights = [gathered] + [shift(gathered, "y", 4 - k) for k in (1, 3, 2)]
    states = lax.all_to_all(states, NEAR, 0, 0, tiled=True)
    mixture, coef = call(
        mix_body,
        [((512, 512), F32), ((512, 16), F32)],
        (at, keep, got, mixture, coef, *near),
        scratch=[pltpu.VMEM((4, 144, 256), BF)],
        vmem=60,
    )
    (normed,) = call(
        norm_body,
        [((512, 512), BF)],
        (at, keep, got, norm_gain[None], mixture, coef, states),
        scratch=[
            pltpu.VMEM((2, 512, 512), BF),
            pltpu.VMEM((512, 512), F32),
            pltpu.VMEM((512, 16), F32),
            pltpu.VMEM((4, 128, 512), BF),
            pltpu.SemaphoreType.DMA((4, 5)),
        ],
        hbm=(1, 2, 4, 5, 6),
        vmem=60,
    )

    blocks = [normed] + [shift(normed, "x", j) for j in (1, 2, 3)]
    theirs = swap(project(at, blocks, rights, True))
    own = project(at, blocks, rights, False)
    return (own + theirs.astype(F32)).astype(BF)


def solution(mesh):
    fine = Mesh(mesh.devices.reshape(4, 4, 2, 2, 2, 4), SEQ + ("x",))
    return jax.shard_map(
        shards,
        mesh=fine,
        in_specs=(
            P(SEQ, "x"),
            P(SEQ, "x"),
            P(SEQ, "x"),
            P(SEQ, "x"),
            P("x", SEQ),
            P(None, "x", SEQ),
            P("x"),
            P(SEQ, "x"),
        ),
        out_specs=P(SEQ, "x"),
        check_vma=False,
    )
```

```python
import functools

import jax
import jax.numpy as jnp
from jax import lax
from jax.experimental import pallas as pl
from jax.experimental.pallas import tpu as pltpu
from jax.sharding import Mesh, PartitionSpec as P

BF = jnp.bfloat16
F32 = jnp.float32
SEQ = ("y", "a", "p", "q", "c")
NEAR = ("p", "q")
NT = (((1,), (1,)), ((), ()))
TN = (((0,), (0,)), ((), ()))
LOGS = 1024
ROWS = 1072


def swap(value):
    return lax.ppermute(value, "c", [(0, 1), (1, 0)])


def dot(left, right, dims=(((1,), (0,)), ((), ()))):
    return lax.dot_general(left, right, dims, preferred_element_type=F32)


def exact(left, right, dims):
    return lax.dot_general(
        left, right, dims, precision=lax.Precision.HIGHEST, preferred_element_type=F32
    )


def tail(log):
    high = log.astype(BF).astype(F32)
    middle = (log - high).astype(BF).astype(F32)
    low = log - high - middle
    row = lax.broadcasted_iota(jnp.int32, (16, 128), 0)
    return jnp.where(
        row == 0, high, jnp.where(row == 1, middle, jnp.where(row == 2, low, 0.0))
    ).astype(BF)


def untail(tile):
    return jnp.sum(tile.astype(F32), axis=0, keepdims=True)


def call(body, outs, args, unread=(), scratch=(), hbm=(), vmem=12):
    specs = [pl.BlockSpec(memory_space=pltpu.SMEM)]
    specs += [
        pl.BlockSpec(memory_space=pltpu.HBM if i in hbm else pltpu.VMEM)
        for i in range(1, len(args))
    ]
    specs += [pl.BlockSpec(memory_space=pl.ANY)] * len(unread)

    def run(*refs):
        body(*refs[: len(args)], *refs[len(args) + len(unread) :])

    return pl.pallas_call(
        run,
        out_shape=[jax.ShapeDtypeStruct(*o) for o in outs],
        in_specs=specs,
        out_specs=[pl.BlockSpec(memory_space=pltpu.VMEM)] * len(outs),
        scratch_shapes=list(scratch),
        compiler_params=pltpu.CompilerParams(vmem_limit_bytes=vmem * 2**20),
        cost_estimate=pl.CostEstimate(flops=10**6, bytes_accessed=10**6, transcendentals=0),
    )(*args, *unread)


def pack_body(
    at, keys, values, queries, gates, decay, mix, keep, send, small, levels, sems
):
    core = at[0]
    mine = pl.ds(pl.multiple_of(core * 512, 512), 512)
    theirs = pl.ds(pl.multiple_of((1 - core) * 512, 512), 512)
    copies = [
        pltpu.make_async_copy(decay, small, sems.at[0]),
        pltpu.make_async_copy(mix, levels, sems.at[1]),
    ]
    for i, ref in enumerate((keys, values, queries, gates)):
        rows = pl.ds(i * 256, 256)
        for out, cols, n in ((send, theirs, 2), (keep, mine, 6)):
            copies.append(pltpu.make_async_copy(ref.at[:, cols], out.at[rows, :], sems.at[n + i]))
    for copy in copies:
        copy.start()
    for copy in copies[:2]:
        copy.wait()
    for out, low in ((keep, core == 0), (send, core == 1)):
        logs = [jnp.where(low, small[0:4], small[4:8])]
        logs += [jnp.where(low, levels[l, 0:4], levels[l, 4:8]) for l in range(8)]
        logs = jnp.concatenate(logs + [jnp.zeros((12, 256), F32)], axis=0)
        high = logs.astype(BF)
        out[LOGS : LOGS + 48, 0:256] = high
        out[LOGS : LOGS + 48, 256:512] = (logs - high.astype(F32)).astype(BF)
    for copy in copies[2:]:
        copy.wait()


def logs_of(block):
    tile = block[LOGS : LOGS + 48, :].astype(F32)
    return tile[:, 0:256] + tile[:, 256:512]


def ends_body(at, keep, got, pay, first):
    core = at[0]
    logs = jnp.concatenate([logs_of(keep)[0:4], logs_of(got)[0:4]], axis=0)
    after = (
        lax.broadcasted_iota(jnp.int32, (256, 256), 1)
        > lax.broadcasted_iota(jnp.int32, (256, 256), 0)
    ).astype(F32)
    scale = jnp.exp(exact(after, logs, NT))
    total = jnp.sum(logs, axis=1, keepdims=True)
    for h in range(4):
        cols = slice(h * 128, h * 128 + 128)
        end = []
        for i, ref in enumerate((keep, got)):
            scaled = ref[0:256, cols].astype(F32) * scale[:, 4 * i + h : 4 * i + h + 1]
            end.append(dot(scaled.astype(BF), ref[256:512, cols], TN))
        own_log, got_log = total[h : h + 1], total[4 + h : 5 + h]
        own_later = jnp.exp(jnp.where(core == 0, got_log, 0.0))
        got_later = jnp.exp(jnp.where(core == 0, 0.0, own_log))
        pay[h, 0:128, :] = (end[0] * own_later + end[1] * got_later).astype(BF)
        pay[h, 128:144, :] = tail(own_log + got_log)
        first[h, :, :] = jnp.where(core == 0, end[0], end[1]).astype(BF)


def blocks_of(got):
    s = [got[i, 0:128, :].astype(F32) for i in range(4)]
    t = [untail(got[i, 128:144, :]) for i in range(4)]
    pair = s[0] * jnp.exp(t[1]) + s[1]
    return s, t, pair


def send_whole(s, t, pair, pay):
    state = (pair * jnp.exp(t[2] + t[3]) + s[2] * jnp.exp(t[3]) + s[3]).astype(BF)
    log = tail(t[0] + t[1] + t[2] + t[3])
    for i in range(4):
        pay[i, 0:128, :] = state
        pay[i, 128:144, :] = log


def lower_states(s, t, pair, at):
    odd, upper = at % 2 == 1, at >= 2
    one = jnp.where(odd, jnp.where(upper, s[2], s[0]), 0.0)
    step = jnp.where(odd, jnp.where(upper, t[2], t[0]), 0.0)
    two = jnp.where(upper, pair * jnp.exp(step), 0.0)
    before = sum(jnp.where(at > i, t[i], 0.0) for i in range(3))
    return one, two, before


def near_body(at, near, pay, *messages):
    s, t, pair = blocks_of(near)
    send_whole(s, t, pair, pay)
    for k, message in enumerate(messages):
        one, two, before = lower_states(s, t, pair, at[1] ^ k)
        message[0:128, 0:128] = one.astype(BF)
        message[0:128, 128:256] = two.astype(BF)
        message[128:144, 0:128] = tail(before)
        message[128:144, 128:256] = jnp.zeros((16, 128), BF)


def far_body(at, far, pay, states, before_out):
    s, t, pair = blocks_of(far)
    send_whole(s, t, pair, pay)
    one, two, before = lower_states(s, t, pair, at[2])
    states[:, 0:128] = one.astype(BF)
    states[:, 128:256] = two.astype(BF)
    before_out[...] = jnp.broadcast_to(before, (8, 128))


def last_body(at, rows, before, far, message):
    one, two, _ = lower_states(*blocks_of(rows), at[3])
    earlier = jnp.exp(before[0:1, :])
    one, two = (one * earlier).astype(BF), (two * earlier).astype(BF)
    for i in range(4):
        message[i, :, 0:256] = far[...]
        message[i, :, 256:384] = one
        message[i, :, 384:512] = two


def place(s, core):
    at = core if s == 0 else 1 - core
    return at, pl.ds(pl.multiple_of(at * 256, 256), 256)


def own_body(at, keep, got, first, mixture, coef):
    core = at[0]
    rows = lax.broadcasted_iota(jnp.int32, (256, 256), 0)
    cols = lax.broadcasted_iota(jnp.int32, (256, 256), 1)
    lower = rows >= cols
    upto = lower.astype(F32)
    both = (logs_of(keep), logs_of(got))
    for s, ref in enumerate((keep, got)):
        second, here = place(s, core)
        logs = both[s]
        at_row = exact(logs[0:8], upto, NT)
        at_col = exact(upto, logs[0:8], NT)
        level = logs.T
        first_log = jnp.sum(both[1 - s][0:4], axis=1, keepdims=True)
        first_log = jnp.where(second == 1, first_log, 0.0)
        for h in range(4):
            hc = slice(h * 128, h * 128 + 128)
            q, kb, v = ref[512:768, hc], ref[0:256, hc], ref[256:512, hc]
            local = at_col[:, h : h + 1]
            gap = jnp.where(lower, local - at_row[h : h + 1, :], -1e30)
            weights = (dot(q, kb, NT) * jnp.exp(gap)).astype(BF)
            m = [level[:, 4 + 4 * l + h : 5 + 4 * l + h] for l in range(8)]
            total = dot(weights, v) * m[0]
            start = jnp.exp(local)
            total += dot(q, first[h]) * jnp.where(second == 1, start * m[1], 0.0)
            mixture[here, hc] = total
            start = start * jnp.exp(first_log[h : h + 1])
            for l in range(2, 8):
                coef[here, 6 * h + l - 2 : 6 * h + l - 1] = start * m[l]


def mix_body(at, keep, got, mixture, coef, n0, n1, n2, n3, mixed, later, near):
    for k, n in enumerate((n0, n1, n2, n3)):
        near[at[1] ^ k] = n[...]
    for h in range(4):
        before = jnp.exp(untail(near[h, 128:144, 0:128])[:, 0:1])
        hc = slice(h * 128, h * 128 + 128)
        for s, ref in enumerate((keep, got)):
            _, here = place(s, at[0])
            read = dot(ref[512:768, hc], near[h, 0:128, :])
            total = mixture[here, hc] + read[:, 0:128] * coef[here, 6 * h : 6 * h + 1]
            mixed[here, hc] = total + read[:, 128:256] * coef[here, 6 * h + 1 : 6 * h + 2]
            later[here, 4 * h : 4 * h + 4] = coef[here, 6 * h + 2 : 6 * h + 6] * before


def norm_body(at, keep, got, gain, mixture, coef, states, normed):
    core = at[0]
    for h in range(4):
        mine = pl.ds(pl.multiple_of(core * 512 + h * 128, 128), 128)
        hc = slice(h * 128, h * 128 + 128)
        for s, ref in enumerate((keep, got)):
            _, here = place(s, core)
            z = ref[768:1024, hc].astype(F32)
            total = mixture[here, hc]
            for l in range(0, 4, 2):
                read = dot(ref[512:768, hc], states[h, :, l * 128 : l * 128 + 256])
                total += read[:, 0:128] * coef[here, 4 * h + l : 4 * h + l + 1]
                total += read[:, 128:256] * coef[here, 4 * h + l + 1 : 4 * h + l + 2]
            gated = total * (z / (1.0 + jnp.exp(-z)))
            size = lax.rsqrt(jnp.mean(gated * gated, axis=1, keepdims=True) + 1e-05)
            normed[here, hc] = (gated * size * gain[:, mine].astype(F32)).astype(BF)


def project_body(other, at, b0, b1, b2, b3, w0, w1, w2, w3, out, left, right, sems):
    row = (1 - at[0]) if other else at[0]
    rows = pl.ds(pl.multiple_of(row * 256, 256), 256)
    copies = [
        pltpu.make_async_copy(w, right.at[k], sems.at[k]) for k, w in enumerate((w0, w1, w2, w3))
    ]
    for copy in copies:
        copy.start()
    for j, block in enumerate((b0, b1, b2, b3)):
        left[(at[4] + 4 - j) % 4] = block[rows, :]
    total = 0.0
    for k, turn in enumerate((0, 1, 3, 2)):
        copies[k].wait()
        total += dot(left[(at[3] + turn) % 4], right[k].reshape(1024, 512), NT)
    out[...] = total.astype(out.dtype)


def project(at, blocks, rights, other):
    return call(
        functools.partial(project_body, other),
        [((256, 1024), BF if other else F32)],
        (at, *blocks, *rights),
        scratch=[
            pltpu.VMEM((4, 256, 512), BF),
            pltpu.VMEM((4, 16, 64, 512), BF),
            pltpu.SemaphoreType.DMA((4,)),
        ],
        hbm=range(5, 9),
        vmem=20,
    )[0]


def shift(value, axis, by):
    return lax.ppermute(value, axis, [(i, (i + by) % 4) for i in range(4)])


def shards(values, keys, queries, gates, log_decay, level_mix, norm_gain, weight):
    y, a, b, q, c, x = (lax.axis_index(n) for n in ("y", "a", NEAR, "q", "c", "x"))
    at = jnp.stack([c, b, a, y, x]).astype(jnp.int32)
    kept = lax.dynamic_slice_in_dim(weight, c * 512, 512, 1)
    theirs = swap(lax.dynamic_slice_in_dim(weight, (1 - c) * 512, 512, 1))
    both = jnp.concatenate(
        [jnp.where(c == 0, kept, theirs), jnp.where(c == 0, theirs, kept)]
    )
    perm = [(s * 4 + f, f * 4 + s) for s in range(4) for f in range(4)]
    mine = lax.ppermute(both, ("y", "x"), perm)
    block = ((ROWS, 512), BF)
    keep, send = call(
        pack_body,
        [block, block],
        (at, keys, values, queries, gates, log_decay, level_mix),
        scratch=[
            pltpu.VMEM((8, 256), F32),
            pltpu.VMEM((8, 8, 256), F32),
            pltpu.SemaphoreType.DMA((10,)),
        ],
        hbm=range(1, 7),
        vmem=60,
    )
    mine, send = lax.optimization_barrier((mine, send))
    theirs = lax.ppermute(mine, "q", [(0, 1), (1, 0)])
    mine = jnp.stack([jnp.where(q == 0, mine, theirs), jnp.where(q == 0, theirs, mine)])
    gathered = lax.all_gather(mine, ("a", "p"), axis=0, tiled=True)

    got = swap(send)
    pay = ((4, 144, 128), BF)
    pay_b, first = call(ends_body, [pay, ((4, 128, 128), BF)], (at, keep, got))
    near = lax.all_to_all(pay_b, NEAR, 0, 0, tiled=True)
    pay_a, *near = call(near_body, [pay] + [((144, 256), BF)] * 4, (at, near))
    far = lax.all_to_all(pay_a, "a", 0, 0, tiled=True)
    near = near[:1] + [
        lax.ppermute(near[k], NEAR, [(i, i ^ k) for i in range(4)]) for k in (1, 2, 3)
    ]
    mixture, coef = call(
        own_body, [((512, 512), F32), ((512, 24), F32)], (at, keep, got, first)
    )
    pay_y, far, before = call(
        far_body,
        [pay, ((128, 256), BF), ((8, 128), F32)],
        (at, far),
        unread=near[1:],
    )
    rows = lax.all_to_all(pay_y, "y", 0, 0, tiled=True)
    (states,) = call(
        last_body, [((4, 128, 512), BF)], (at, rows, before, far), unread=(mixture,)
    )
    states = lax.all_to_all(states, NEAR, 0, 0, tiled=True)
    mixture, coef = call(
        mix_body,
        [((512, 512), F32), ((512, 16), F32)],
        (at, keep, got, mixture, coef, *near),
        scratch=[pltpu.VMEM((4, 144, 256), BF)],
    )
    _, gathered = lax.optimization_barrier((coef, gathered))
    rights = [gathered] + [shift(gathered, "y", 4 - k) for k in (1, 3, 2)]
    (normed,) = call(
        norm_body, [((512, 512), BF)], (at, keep, got, norm_gain[None], mixture, coef, states)
    )

    blocks = [normed] + [shift(normed, "x", j) for j in (1, 2, 3)]
    theirs = swap(project(at, blocks, rights, True))
    own = project(at, blocks, rights, False)
    return (own + theirs.astype(F32)).astype(BF)


def solution(mesh):
    fine = Mesh(mesh.devices.reshape(4, 4, 2, 2, 2, 4), SEQ + ("x",))
    return jax.shard_map(
        shards,
        mesh=fine,
        in_specs=(
            P(SEQ, "x"),
            P(SEQ, "x"),
            P(SEQ, "x"),
            P(SEQ, "x"),
            P("x", SEQ),
            P(None, "x", SEQ),
            P("x"),
            P(SEQ, "x"),
        ),
        out_specs=P(SEQ, "x"),
        check_vma=False,
    )
```

```python
import functools

import jax
import jax.numpy as jnp
from jax import lax
from jax.experimental import pallas as pl
from jax.experimental.pallas import tpu as pltpu
from jax.sharding import Mesh, PartitionSpec as P

BF = jnp.bfloat16
F32 = jnp.float32
SEQ = ("y", "a", "p", "q", "c")
NEAR = ("p", "q")
NT = (((1,), (1,)), ((), ()))
TN = (((0,), (0,)), ((), ()))
LOGS = 1024
ROWS = 1072


def swap(value):
    return lax.ppermute(value, "c", [(0, 1), (1, 0)])


def dot(left, right, dims=(((1,), (0,)), ((), ()))):
    return lax.dot_general(left, right, dims, preferred_element_type=F32)


def exact(left, right, dims):
    return lax.dot_general(
        left, right, dims, precision=lax.Precision.HIGHEST, preferred_element_type=F32
    )


def tail(log):
    high = log.astype(BF).astype(F32)
    middle = (log - high).astype(BF).astype(F32)
    low = log - high - middle
    row = lax.broadcasted_iota(jnp.int32, (16, 128), 0)
    return jnp.where(
        row == 0, high, jnp.where(row == 1, middle, jnp.where(row == 2, low, 0.0))
    ).astype(BF)


def untail(tile):
    return jnp.sum(tile.astype(F32), axis=0, keepdims=True)


def call(body, outs, args, unread=(), scratch=(), hbm=(), vmem=12):
    specs = [pl.BlockSpec(memory_space=pltpu.SMEM)]
    specs += [
        pl.BlockSpec(memory_space=pltpu.HBM if i in hbm else pltpu.VMEM)
        for i in range(1, len(args))
    ]
    specs += [pl.BlockSpec(memory_space=pl.ANY)] * len(unread)

    def run(*refs):
        body(*refs[: len(args)], *refs[len(args) + len(unread) :])

    return pl.pallas_call(
        run,
        out_shape=[jax.ShapeDtypeStruct(*o) for o in outs],
        in_specs=specs,
        out_specs=[pl.BlockSpec(memory_space=pltpu.VMEM)] * len(outs),
        scratch_shapes=list(scratch),
        compiler_params=pltpu.CompilerParams(vmem_limit_bytes=vmem * 2**20),
        cost_estimate=pl.CostEstimate(flops=10**6, bytes_accessed=10**6, transcendentals=0),
    )(*args, *unread)


def pack_body(
    at, keys, values, queries, gates, decay, mix, keep, send, small, levels, sems
):
    core = at[0]
    mine = pl.ds(pl.multiple_of(core * 512, 512), 512)
    theirs = pl.ds(pl.multiple_of((1 - core) * 512, 512), 512)
    copies = [
        pltpu.make_async_copy(decay, small, sems.at[0]),
        pltpu.make_async_copy(mix, levels, sems.at[1]),
    ]
    for i, ref in enumerate((keys, values, queries, gates)):
        rows = pl.ds(i * 256, 256)
        for out, cols, n in ((send, theirs, 2), (keep, mine, 6)):
            copies.append(pltpu.make_async_copy(ref.at[:, cols], out.at[rows, :], sems.at[n + i]))
    for copy in copies:
        copy.start()
    for copy in copies[:2]:
        copy.wait()
    for out, low in ((keep, core == 0), (send, core == 1)):
        logs = [jnp.where(low, small[0:4], small[4:8])]
        logs += [jnp.where(low, levels[l, 0:4], levels[l, 4:8]) for l in range(8)]
        logs = jnp.concatenate(logs + [jnp.zeros((12, 256), F32)], axis=0)
        high = logs.astype(BF)
        out[LOGS : LOGS + 48, 0:256] = high
        out[LOGS : LOGS + 48, 256:512] = (logs - high.astype(F32)).astype(BF)
    for copy in copies[2:]:
        copy.wait()


def logs_of(block):
    tile = block[LOGS : LOGS + 48, :].astype(F32)
    return tile[:, 0:256] + tile[:, 256:512]


def ends_body(at, keep, got, pay, first):
    core = at[0]
    logs = jnp.concatenate([logs_of(keep)[0:4], logs_of(got)[0:4]], axis=0)
    after = (
        lax.broadcasted_iota(jnp.int32, (256, 256), 1)
        > lax.broadcasted_iota(jnp.int32, (256, 256), 0)
    ).astype(F32)
    scale = jnp.exp(exact(after, logs, NT))
    total = jnp.sum(logs, axis=1, keepdims=True)
    for h in range(4):
        cols = slice(h * 128, h * 128 + 128)
        end = []
        for i, ref in enumerate((keep, got)):
            scaled = ref[0:256, cols].astype(F32) * scale[:, 4 * i + h : 4 * i + h + 1]
            end.append(dot(scaled.astype(BF), ref[256:512, cols], TN))
        own_log, got_log = total[h : h + 1], total[4 + h : 5 + h]
        own_later = jnp.exp(jnp.where(core == 0, got_log, 0.0))
        got_later = jnp.exp(jnp.where(core == 0, 0.0, own_log))
        pay[h, 0:128, :] = (end[0] * own_later + end[1] * got_later).astype(BF)
        pay[h, 128:144, :] = tail(own_log + got_log)
        first[h, :, :] = jnp.where(core == 0, end[0], end[1]).astype(BF)


def blocks_of(got):
    s = [got[i, 0:128, :].astype(F32) for i in range(4)]
    t = [untail(got[i, 128:144, :]) for i in range(4)]
    pair = s[0] * jnp.exp(t[1]) + s[1]
    return s, t, pair


def send_whole(s, t, pair, pay):
    state = (pair * jnp.exp(t[2] + t[3]) + s[2] * jnp.exp(t[3]) + s[3]).astype(BF)
    log = tail(t[0] + t[1] + t[2] + t[3])
    for i in range(4):
        pay[i, 0:128, :] = state
        pay[i, 128:144, :] = log


def lower_states(s, t, pair, at):
    odd, upper = at % 2 == 1, at >= 2
    one = jnp.where(odd, jnp.where(upper, s[2], s[0]), 0.0)
    step = jnp.where(odd, jnp.where(upper, t[2], t[0]), 0.0)
    two = jnp.where(upper, pair * jnp.exp(step), 0.0)
    before = sum(jnp.where(at > i, t[i], 0.0) for i in range(3))
    return one, two, before


def near_body(at, near, pay):
    send_whole(*blocks_of(near), pay)


def pair_body(at, own, other, pay):
    odd = at[1] % 2 == 1
    for h in range(4):
        s = [ref[h, 0:128, :].astype(F32) for ref in (own, other)]
        t = [untail(ref[h, 128:144, :]) for ref in (own, other)]
        scales = (jnp.where(odd, 0.0, t[1]), jnp.where(odd, t[0], 0.0))
        pay[h, 0:128, :] = (s[0] * jnp.exp(scales[0]) + s[1] * jnp.exp(scales[1])).astype(BF)
        pay[h, 128:144, :] = tail(t[0] + t[1])


def far_body(at, far, pay, states, before_out):
    s, t, pair = blocks_of(far)
    send_whole(s, t, pair, pay)
    one, two, before = lower_states(s, t, pair, at[2])
    states[:, 0:128] = one.astype(BF)
    states[:, 128:256] = two.astype(BF)
    before_out[...] = jnp.broadcast_to(before, (8, 128))


def last_body(at, rows, before, far, message):
    one, two, _ = lower_states(*blocks_of(rows), at[3])
    earlier = jnp.exp(before[0:1, :])
    one, two = (one * earlier).astype(BF), (two * earlier).astype(BF)
    for i in range(4):
        message[i, :, 0:256] = far[...]
        message[i, :, 256:384] = one
        message[i, :, 384:512] = two


def place(s, core):
    at = core if s == 0 else 1 - core
    return at, pl.ds(pl.multiple_of(at * 256, 256), 256)


def own_body(at, keep, got, first, mixture, coef):
    core = at[0]
    rows = lax.broadcasted_iota(jnp.int32, (256, 256), 0)
    cols = lax.broadcasted_iota(jnp.int32, (256, 256), 1)
    lower = rows >= cols
    upto = lower.astype(F32)
    both = (logs_of(keep), logs_of(got))
    for s, ref in enumerate((keep, got)):
        second, here = place(s, core)
        logs = both[s]
        at_row = exact(logs[0:8], upto, NT)
        at_col = exact(upto, logs[0:8], NT)
        level = logs.T
        first_log = jnp.sum(both[1 - s][0:4], axis=1, keepdims=True)
        first_log = jnp.where(second == 1, first_log, 0.0)
        for h in range(4):
            hc = slice(h * 128, h * 128 + 128)
            q, kb, v = ref[512:768, hc], ref[0:256, hc], ref[256:512, hc]
            local = at_col[:, h : h + 1]
            gap = jnp.where(lower, local - at_row[h : h + 1, :], -1e30)
            weights = (dot(q, kb, NT) * jnp.exp(gap)).astype(BF)
            m = [level[:, 4 + 4 * l + h : 5 + 4 * l + h] for l in range(8)]
            total = dot(weights, v) * m[0]
            start = jnp.exp(local)
            total += dot(q, first[h]) * jnp.where(second == 1, start * m[1], 0.0)
            mixture[here, hc] = total
            start = start * jnp.exp(first_log[h : h + 1])
            for l in range(2, 8):
                coef[here, 6 * h + l - 2 : 6 * h + l - 1] = start * m[l]


def mix_body(at, keep, got, mixture, coef, other, pair, mixed, later):
    odd, upper = at[1] % 2 == 1, at[1] >= 2
    for h in range(4):
        step = jnp.where(odd, untail(other[h, 128:144, :]), 0.0)
        one = jnp.where(odd, other[h, 0:128, :].astype(F32), 0.0).astype(BF)
        two = jnp.where(upper, pair[h, 0:128, :].astype(F32) * jnp.exp(step), 0.0).astype(BF)
        before = jnp.exp(step + jnp.where(upper, untail(pair[h, 128:144, :]), 0.0))[:, 0:1]
        states = jnp.concatenate([one, two], axis=1)
        hc = slice(h * 128, h * 128 + 128)
        for s, ref in enumerate((keep, got)):
            _, here = place(s, at[0])
            read = dot(ref[512:768, hc], states)
            total = mixture[here, hc] + read[:, 0:128] * coef[here, 6 * h : 6 * h + 1]
            mixed[here, hc] = total + read[:, 128:256] * coef[here, 6 * h + 1 : 6 * h + 2]
            later[here, 4 * h : 4 * h + 4] = coef[here, 6 * h + 2 : 6 * h + 6] * before


def norm_body(at, keep, got, gain, mixture, coef, states, normed):
    core = at[0]
    for h in range(4):
        mine = pl.ds(pl.multiple_of(core * 512 + h * 128, 128), 128)
        hc = slice(h * 128, h * 128 + 128)
        for s, ref in enumerate((keep, got)):
            _, here = place(s, core)
            z = ref[768:1024, hc].astype(F32)
            total = mixture[here, hc]
            for l in range(0, 4, 2):
                read = dot(ref[512:768, hc], states[h, :, l * 128 : l * 128 + 256])
                total += read[:, 0:128] * coef[here, 4 * h + l : 4 * h + l + 1]
                total += read[:, 128:256] * coef[here, 4 * h + l + 1 : 4 * h + l + 2]
            gated = total * (z / (1.0 + jnp.exp(-z)))
            size = lax.rsqrt(jnp.mean(gated * gated, axis=1, keepdims=True) + 1e-05)
            normed[here, hc] = (gated * size * gain[:, mine].astype(F32)).astype(BF)


def project_body(other, at, b0, b1, b2, b3, right, out, total):
    step = pl.program_id(0)
    row = (1 - at[0]) if other else at[0]
    rows = pl.ds(pl.multiple_of(row * 256, 256), 256)
    want = (at[4] - at[3] + step + 4) % 4

    @pl.when(step == 0)
    def _():
        total[...] = jnp.zeros_like(total)

    for j, block in enumerate((b0, b1, b2, b3)):

        @pl.when(want == j)
        def _():
            total[...] += dot(block[rows, :], right[...].reshape(1024, 512), NT)

    @pl.when(step == 3)
    def _():
        out[...] = total[...].astype(out.dtype)


def project(at, blocks, right, other):
    whole_block = pl.BlockSpec((512, 512), lambda k, at: (0, 0))
    return pl.pallas_call(
        functools.partial(project_body, other),
        out_shape=jax.ShapeDtypeStruct((256, 1024), BF if other else F32),
        grid_spec=pltpu.PrefetchScalarGridSpec(
            num_scalar_prefetch=1,
            grid=(4,),
            in_specs=[whole_block] * 4
            + [pl.BlockSpec((16, 64, 512), lambda k, at: (0, 0, k))],
            out_specs=pl.BlockSpec((256, 1024), lambda k, at: (0, 0)),
            scratch_shapes=[pltpu.VMEM((256, 1024), F32)],
        ),
        compiler_params=pltpu.CompilerParams(vmem_limit_bytes=20 * 2**20),
        cost_estimate=pl.CostEstimate(
            flops=2**30, bytes_accessed=6 * 2**20, transcendentals=0
        ),
    )(at, *blocks, right)


def shift(value, axis, by):
    return lax.ppermute(value, axis, [(i, (i + by) % 4) for i in range(4)])


def shards(values, keys, queries, gates, log_decay, level_mix, norm_gain, weight):
    y, a, b, c, x = (lax.axis_index(n) for n in ("y", "a", NEAR, "c", "x"))
    at = jnp.stack([c, b, a, y, x]).astype(jnp.int32)
    kept = lax.dynamic_slice_in_dim(weight, c * 512, 512, 1)
    theirs = swap(lax.dynamic_slice_in_dim(weight, (1 - c) * 512, 512, 1))
    both = jnp.concatenate(
        [jnp.where(c == 0, kept, theirs), jnp.where(c == 0, theirs, kept)]
    )
    mine = []
    for k in range(4):
        perm = [(s * 4 + f, ((f + k) % 4) * 4 + s) for s in range(4) for f in range(4)]
        mine.append(lax.ppermute(both, ("y", "x"), perm))
    block = ((ROWS, 512), BF)
    keep, send = call(
        pack_body,
        [block, block],
        (at, keys, values, queries, gates, log_decay, level_mix),
        scratch=[
            pltpu.VMEM((8, 256), F32),
            pltpu.VMEM((8, 8, 256), F32),
            pltpu.SemaphoreType.DMA((10,)),
        ],
        hbm=range(1, 7),
        vmem=60,
    )
    mine, send = lax.optimization_barrier((mine, send))
    gathered = lax.all_gather(jnp.concatenate(mine, axis=1), ("a", "p", "q"))

    got = swap(send)
    pay = ((4, 144, 128), BF)
    pay_b, first = call(ends_body, [pay, ((4, 128, 128), BF)], (at, keep, got))
    near = lax.all_to_all(pay_b, NEAR, 0, 0, tiled=True)
    other = lax.ppermute(pay_b, NEAR, [(i, i ^ 1) for i in range(4)])
    (pay_a,) = call(near_body, [pay], (at, near), unread=(other,))
    far = lax.all_to_all(pay_a, "a", 0, 0, tiled=True)
    (pair,) = call(pair_body, [pay], (at, pay_b, other))
    pair = lax.ppermute(pair, NEAR, [(i, i ^ 2) for i in range(4)])
    pay_y, far, before = call(
        far_body,
        [pay, ((128, 256), BF), ((8, 128), F32)],
        (at, far),
        unread=(pair,),
    )
    rows = lax.all_to_all(pay_y, "y", 0, 0, tiled=True)
    (states,) = call(last_body, [((4, 128, 512), BF)], (at, rows, before, far))
    states = lax.all_to_all(states, NEAR, 0, 0, tiled=True)
    mixture, coef = call(
        own_body, [((512, 512), F32), ((512, 24), F32)], (at, keep, got, first)
    )
    mixture, coef = call(
        mix_body,
        [((512, 512), F32), ((512, 16), F32)],
        (at, keep, got, mixture, coef, other, pair),
    )
    (normed,) = call(
        norm_body, [((512, 512), BF)], (at, keep, got, norm_gain[None], mixture, coef, states)
    )

    blocks = [normed] + [shift(normed, "x", j) for j in (1, 2, 3)]
    theirs = swap(project(at, blocks, gathered, True))
    own = project(at, blocks, gathered, False)
    return (own + theirs.astype(F32)).astype(BF)


def solution(mesh):
    fine = Mesh(mesh.devices.reshape(4, 4, 2, 2, 2, 4), SEQ + ("x",))
    return jax.shard_map(
        shards,
        mesh=fine,
        in_specs=(
            P(SEQ, "x"),
            P(SEQ, "x"),
            P(SEQ, "x"),
            P(SEQ, "x"),
            P("x", SEQ),
            P(None, "x", SEQ),
            P("x"),
            P(SEQ, "x"),
        ),
        out_specs=P(SEQ, "x"),
        check_vma=False,
    )
```

```python
import functools

import jax
import jax.numpy as jnp
from jax import lax
from jax.experimental import pallas as pl
from jax.experimental.pallas import tpu as pltpu
from jax.sharding import Mesh, PartitionSpec as P

BF = jnp.bfloat16
F32 = jnp.float32
SEQ = ("y", "a", "p", "q", "c")
NEAR = ("p", "q")
NT = (((1,), (1,)), ((), ()))
TN = (((0,), (0,)), ((), ()))
LOGS = 1024
ROWS = 1072


def swap(value):
    return lax.ppermute(value, "c", [(0, 1), (1, 0)])


def dot(left, right, dims=(((1,), (0,)), ((), ()))):
    return lax.dot_general(left, right, dims, preferred_element_type=F32)


def exact(left, right, dims):
    return lax.dot_general(
        left, right, dims, precision=lax.Precision.HIGHEST, preferred_element_type=F32
    )


def tail(log):
    high = log.astype(BF).astype(F32)
    middle = (log - high).astype(BF).astype(F32)
    low = log - high - middle
    row = lax.broadcasted_iota(jnp.int32, (16, 128), 0)
    return jnp.where(
        row == 0, high, jnp.where(row == 1, middle, jnp.where(row == 2, low, 0.0))
    ).astype(BF)


def untail(tile):
    return jnp.sum(tile.astype(F32), axis=0, keepdims=True)


def call(body, outs, args, unread=(), scratch=(), hbm=(), vmem=12):
    specs = [pl.BlockSpec(memory_space=pltpu.SMEM)]
    specs += [
        pl.BlockSpec(memory_space=pltpu.HBM if i in hbm else pltpu.VMEM)
        for i in range(1, len(args))
    ]
    specs += [pl.BlockSpec(memory_space=pl.ANY)] * len(unread)

    def run(*refs):
        body(*refs[: len(args)], *refs[len(args) + len(unread) :])

    return pl.pallas_call(
        run,
        out_shape=[jax.ShapeDtypeStruct(*o) for o in outs],
        in_specs=specs,
        out_specs=[pl.BlockSpec(memory_space=pltpu.VMEM)] * len(outs),
        scratch_shapes=list(scratch),
        compiler_params=pltpu.CompilerParams(vmem_limit_bytes=vmem * 2**20),
        cost_estimate=pl.CostEstimate(flops=10**6, bytes_accessed=10**6, transcendentals=0),
    )(*args, *unread)


def pack_body(
    at, keys, values, queries, gates, decay, mix, keep, send, small, levels, sems
):
    core = at[0]
    mine = pl.ds(pl.multiple_of(core * 512, 512), 512)
    theirs = pl.ds(pl.multiple_of((1 - core) * 512, 512), 512)
    copies = [
        pltpu.make_async_copy(decay, small, sems.at[0]),
        pltpu.make_async_copy(mix, levels, sems.at[1]),
    ]
    for i, ref in enumerate((keys, values, queries, gates)):
        rows = pl.ds(i * 256, 256)
        for out, cols, n in ((send, theirs, 2), (keep, mine, 6)):
            copies.append(pltpu.make_async_copy(ref.at[:, cols], out.at[rows, :], sems.at[n + i]))
    for copy in copies:
        copy.start()
    for copy in copies[:2]:
        copy.wait()
    for out, low in ((keep, core == 0), (send, core == 1)):
        logs = [jnp.where(low, small[0:4], small[4:8])]
        logs += [jnp.where(low, levels[l, 0:4], levels[l, 4:8]) for l in range(8)]
        logs = jnp.concatenate(logs + [jnp.zeros((12, 256), F32)], axis=0)
        high = logs.astype(BF)
        out[LOGS : LOGS + 48, 0:256] = high
        out[LOGS : LOGS + 48, 256:512] = (logs - high.astype(F32)).astype(BF)
    for copy in copies[2:]:
        copy.wait()


def logs_of(block):
    tile = block[LOGS : LOGS + 48, :].astype(F32)
    return tile[:, 0:256] + tile[:, 256:512]


def ends_body(at, keep, got, pay, first):
    core = at[0]
    logs = jnp.concatenate([logs_of(keep)[0:4], logs_of(got)[0:4]], axis=0)
    after = (
        lax.broadcasted_iota(jnp.int32, (256, 256), 1)
        > lax.broadcasted_iota(jnp.int32, (256, 256), 0)
    ).astype(F32)
    scale = jnp.exp(exact(after, logs, NT))
    total = jnp.sum(logs, axis=1, keepdims=True)
    for h in range(4):
        cols = slice(h * 128, h * 128 + 128)
        end = []
        for i, ref in enumerate((keep, got)):
            scaled = ref[0:256, cols].astype(F32) * scale[:, 4 * i + h : 4 * i + h + 1]
            end.append(dot(scaled.astype(BF), ref[256:512, cols], TN))
        own_log, got_log = total[h : h + 1], total[4 + h : 5 + h]
        own_later = jnp.exp(jnp.where(core == 0, got_log, 0.0))
        got_later = jnp.exp(jnp.where(core == 0, 0.0, own_log))
        pay[h, 0:128, :] = (end[0] * own_later + end[1] * got_later).astype(BF)
        pay[h, 128:144, :] = tail(own_log + got_log)
        first[h, :, :] = jnp.where(core == 0, end[0], end[1]).astype(BF)


def blocks_of(got):
    s = [got[i, 0:128, :].astype(F32) for i in range(4)]
    t = [untail(got[i, 128:144, :]) for i in range(4)]
    pair = s[0] * jnp.exp(t[1]) + s[1]
    return s, t, pair


def send_whole(s, t, pair, pay):
    state = (pair * jnp.exp(t[2] + t[3]) + s[2] * jnp.exp(t[3]) + s[3]).astype(BF)
    log = tail(t[0] + t[1] + t[2] + t[3])
    for i in range(4):
        pay[i, 0:128, :] = state
        pay[i, 128:144, :] = log


def lower_states(s, t, pair, at):
    odd, upper = at % 2 == 1, at >= 2
    one = jnp.where(odd, jnp.where(upper, s[2], s[0]), 0.0)
    step = jnp.where(odd, jnp.where(upper, t[2], t[0]), 0.0)
    two = jnp.where(upper, pair * jnp.exp(step), 0.0)
    before = sum(jnp.where(at > i, t[i], 0.0) for i in range(3))
    return one, two, before


def near_body(at, near, pay):
    send_whole(*blocks_of(near), pay)


def pair_body(at, own, other, pay):
    odd = at[1] % 2 == 1
    for h in range(4):
        s = [ref[h, 0:128, :].astype(F32) for ref in (own, other)]
        t = [untail(ref[h, 128:144, :]) for ref in (own, other)]
        scales = (jnp.where(odd, 0.0, t[1]), jnp.where(odd, t[0], 0.0))
        pay[h, 0:128, :] = (s[0] * jnp.exp(scales[0]) + s[1] * jnp.exp(scales[1])).astype(BF)
        pay[h, 128:144, :] = tail(t[0] + t[1])


def far_body(at, far, pay, states, before_out):
    s, t, pair = blocks_of(far)
    send_whole(s, t, pair, pay)
    one, two, before = lower_states(s, t, pair, at[2])
    states[:, 0:128] = one.astype(BF)
    states[:, 128:256] = two.astype(BF)
    before_out[...] = jnp.broadcast_to(before, (8, 128))


def last_body(at, rows, before, far, message):
    one, two, _ = lower_states(*blocks_of(rows), at[3])
    earlier = jnp.exp(before[0:1, :])
    one, two = (one * earlier).astype(BF), (two * earlier).astype(BF)
    for i in range(4):
        message[i, :, 0:256] = far[...]
        message[i, :, 256:384] = one
        message[i, :, 384:512] = two


def place(s, core):
    at = core if s == 0 else 1 - core
    return at, pl.ds(pl.multiple_of(at * 256, 256), 256)


def own_body(at, keep, got, first, mixture, coef):
    core = at[0]
    rows = lax.broadcasted_iota(jnp.int32, (256, 256), 0)
    cols = lax.broadcasted_iota(jnp.int32, (256, 256), 1)
    lower = rows >= cols
    upto = lower.astype(F32)
    both = (logs_of(keep), logs_of(got))
    for s, ref in enumerate((keep, got)):
        second, here = place(s, core)
        logs = both[s]
        at_row = exact(logs[0:8], upto, NT)
        at_col = exact(upto, logs[0:8], NT)
        level = logs.T
        first_log = jnp.sum(both[1 - s][0:4], axis=1, keepdims=True)
        first_log = jnp.where(second == 1, first_log, 0.0)
        for h in range(4):
            hc = slice(h * 128, h * 128 + 128)
            q, kb, v = ref[512:768, hc], ref[0:256, hc], ref[256:512, hc]
            local = at_col[:, h : h + 1]
            gap = jnp.where(lower, local - at_row[h : h + 1, :], -1e30)
            weights = (dot(q, kb, NT) * jnp.exp(gap)).astype(BF)
            m = [level[:, 4 + 4 * l + h : 5 + 4 * l + h] for l in range(8)]
            total = dot(weights, v) * m[0]
            start = jnp.exp(local)
            total += dot(q, first[h]) * jnp.where(second == 1, start * m[1], 0.0)
            mixture[here, hc] = total
            start = start * jnp.exp(first_log[h : h + 1])
            for l in range(2, 8):
                coef[here, 6 * h + l - 2 : 6 * h + l - 1] = start * m[l]


def mix_body(at, keep, got, mixture, coef, other, pair, mixed, later):
    odd, upper = at[1] % 2 == 1, at[1] >= 2
    for h in range(4):
        step = jnp.where(odd, untail(other[h, 128:144, :]), 0.0)
        one = jnp.where(odd, other[h, 0:128, :].astype(F32), 0.0).astype(BF)
        two = jnp.where(upper, pair[h, 0:128, :].astype(F32) * jnp.exp(step), 0.0).astype(BF)
        before = jnp.exp(step + jnp.where(upper, untail(pair[h, 128:144, :]), 0.0))[:, 0:1]
        states = jnp.concatenate([one, two], axis=1)
        hc = slice(h * 128, h * 128 + 128)
        for s, ref in enumerate((keep, got)):
            _, here = place(s, at[0])
            read = dot(ref[512:768, hc], states)
            total = mixture[here, hc] + read[:, 0:128] * coef[here, 6 * h : 6 * h + 1]
            mixed[here, hc] = total + read[:, 128:256] * coef[here, 6 * h + 1 : 6 * h + 2]
            later[here, 4 * h : 4 * h + 4] = coef[here, 6 * h + 2 : 6 * h + 6] * before


def norm_body(at, keep, got, gain, mixture, coef, states, normed):
    core = at[0]
    for h in range(4):
        mine = pl.ds(pl.multiple_of(core * 512 + h * 128, 128), 128)
        hc = slice(h * 128, h * 128 + 128)
        for s, ref in enumerate((keep, got)):
            _, here = place(s, core)
            z = ref[768:1024, hc].astype(F32)
            total = mixture[here, hc]
            for l in range(0, 4, 2):
                read = dot(ref[512:768, hc], states[h, :, l * 128 : l * 128 + 256])
                total += read[:, 0:128] * coef[here, 4 * h + l : 4 * h + l + 1]
                total += read[:, 128:256] * coef[here, 4 * h + l + 1 : 4 * h + l + 2]
            gated = total * (z / (1.0 + jnp.exp(-z)))
            size = lax.rsqrt(jnp.mean(gated * gated, axis=1, keepdims=True) + 1e-05)
            normed[here, hc] = (gated * size * gain[:, mine].astype(F32)).astype(BF)


def project_body(other, at, b0, b1, b2, b3, w0, w1, w2, w3, out, left, right, sems):
    row = (1 - at[0]) if other else at[0]
    rows = pl.ds(pl.multiple_of(row * 256, 256), 256)
    copies = [
        pltpu.make_async_copy(w, right.at[k], sems.at[k]) for k, w in enumerate((w0, w1, w2, w3))
    ]
    for copy in copies:
        copy.start()
    for j, block in enumerate((b0, b1, b2, b3)):
        left[(at[4] + 4 - j) % 4] = block[rows, :]
    total = 0.0
    for k, turn in enumerate((0, 1, 3, 2)):
        copies[k].wait()
        total += dot(left[(at[3] + turn) % 4], right[k].reshape(1024, 512), NT)
    out[...] = total.astype(out.dtype)


def project(at, blocks, rights, other):
    return call(
        functools.partial(project_body, other),
        [((256, 1024), BF if other else F32)],
        (at, *blocks, *rights),
        scratch=[
            pltpu.VMEM((4, 256, 512), BF),
            pltpu.VMEM((4, 16, 64, 512), BF),
            pltpu.SemaphoreType.DMA((4,)),
        ],
        hbm=range(5, 9),
        vmem=20,
    )[0]


def shift(value, axis, by):
    return lax.ppermute(value, axis, [(i, (i + by) % 4) for i in range(4)])


def shards(values, keys, queries, gates, log_decay, level_mix, norm_gain, weight):
    y, a, b, q, c, x = (lax.axis_index(n) for n in ("y", "a", NEAR, "q", "c", "x"))
    at = jnp.stack([c, b, a, y, x]).astype(jnp.int32)
    kept = lax.dynamic_slice_in_dim(weight, c * 512, 512, 1)
    theirs = swap(lax.dynamic_slice_in_dim(weight, (1 - c) * 512, 512, 1))
    both = jnp.concatenate(
        [jnp.where(c == 0, kept, theirs), jnp.where(c == 0, theirs, kept)]
    )
    perm = [(s * 4 + f, f * 4 + s) for s in range(4) for f in range(4)]
    mine = lax.ppermute(both, ("y", "x"), perm)
    theirs = lax.ppermute(mine, "q", [(0, 1), (1, 0)])
    block = ((ROWS, 512), BF)
    keep, send = call(
        pack_body,
        [block, block],
        (at, keys, values, queries, gates, log_decay, level_mix),
        scratch=[
            pltpu.VMEM((8, 256), F32),
            pltpu.VMEM((8, 8, 256), F32),
            pltpu.SemaphoreType.DMA((10,)),
        ],
        hbm=range(1, 7),
        vmem=60,
    )
    theirs, send = lax.optimization_barrier((theirs, send))
    mine = jnp.stack([jnp.where(q == 0, mine, theirs), jnp.where(q == 0, theirs, mine)])
    gathered = lax.all_gather(mine, ("a", "p"), axis=0, tiled=True)

    got = swap(send)
    pay = ((4, 144, 128), BF)
    pay_b, first = call(ends_body, [pay, ((4, 128, 128), BF)], (at, keep, got))
    near = lax.all_to_all(pay_b, NEAR, 0, 0, tiled=True)
    other = lax.ppermute(pay_b, NEAR, [(i, i ^ 1) for i in range(4)])
    (pay_a,) = call(near_body, [pay], (at, near), unread=(other,))
    far = lax.all_to_all(pay_a, "a", 0, 0, tiled=True)
    (pair,) = call(pair_body, [pay], (at, pay_b, other))
    pair = lax.ppermute(pair, NEAR, [(i, i ^ 2) for i in range(4)])
    pay_y, far, before = call(
        far_body,
        [pay, ((128, 256), BF), ((8, 128), F32)],
        (at, far),
        unread=(pair,),
    )
    rows = lax.all_to_all(pay_y, "y", 0, 0, tiled=True)
    (states,) = call(last_body, [((4, 128, 512), BF)], (at, rows, before, far))
    states = lax.all_to_all(states, NEAR, 0, 0, tiled=True)
    mixture, coef = call(
        own_body, [((512, 512), F32), ((512, 24), F32)], (at, keep, got, first)
    )
    mixture, coef = call(
        mix_body,
        [((512, 512), F32), ((512, 16), F32)],
        (at, keep, got, mixture, coef, other, pair),
    )
    _, gathered = lax.optimization_barrier((coef, gathered))
    rights = [gathered] + [shift(gathered, "y", 4 - k) for k in (1, 3, 2)]
    (normed,) = call(
        norm_body, [((512, 512), BF)], (at, keep, got, norm_gain[None], mixture, coef, states)
    )

    blocks = [normed] + [shift(normed, "x", j) for j in (1, 2, 3)]
    theirs = swap(project(at, blocks, rights, True))
    own = project(at, blocks, rights, False)
    return (own + theirs.astype(F32)).astype(BF)


def solution(mesh):
    fine = Mesh(mesh.devices.reshape(4, 4, 2, 2, 2, 4), SEQ + ("x",))
    return jax.shard_map(
        shards,
        mesh=fine,
        in_specs=(
            P(SEQ, "x"),
            P(SEQ, "x"),
            P(SEQ, "x"),
            P(SEQ, "x"),
            P("x", SEQ),
            P(None, "x", SEQ),
            P("x"),
            P(SEQ, "x"),
        ),
        out_specs=P(SEQ, "x"),
        check_vma=False,
    )
```

```python
import functools

import jax
import jax.numpy as jnp
from jax import lax
from jax.experimental import pallas as pl
from jax.experimental.pallas import tpu as pltpu
from jax.sharding import Mesh, PartitionSpec as P

BF = jnp.bfloat16
F32 = jnp.float32
SEQ = ("y", "a", "p", "q", "c")
NEAR = ("p", "q")
NT = (((1,), (1,)), ((), ()))
TN = (((0,), (0,)), ((), ()))
LOGS = 1024
ROWS = 1072


def swap(value):
    return lax.ppermute(value, "c", [(0, 1), (1, 0)])


def dot(left, right, dims=(((1,), (0,)), ((), ()))):
    return lax.dot_general(left, right, dims, preferred_element_type=F32)


def exact(left, right, dims):
    return lax.dot_general(
        left, right, dims, precision=lax.Precision.HIGHEST, preferred_element_type=F32
    )


def tail(log):
    high = log.astype(BF).astype(F32)
    middle = (log - high).astype(BF).astype(F32)
    low = log - high - middle
    row = lax.broadcasted_iota(jnp.int32, (16, 128), 0)
    return jnp.where(
        row == 0, high, jnp.where(row == 1, middle, jnp.where(row == 2, low, 0.0))
    ).astype(BF)


def untail(tile):
    return jnp.sum(tile.astype(F32), axis=0, keepdims=True)


def call(body, outs, args, unread=(), scratch=(), hbm=(), vmem=12):
    specs = [pl.BlockSpec(memory_space=pltpu.SMEM)]
    specs += [
        pl.BlockSpec(memory_space=pltpu.HBM if i in hbm else pltpu.VMEM)
        for i in range(1, len(args))
    ]
    specs += [pl.BlockSpec(memory_space=pl.ANY)] * len(unread)

    def run(*refs):
        body(*refs[: len(args)], *refs[len(args) + len(unread) :])

    return pl.pallas_call(
        run,
        out_shape=[jax.ShapeDtypeStruct(*o) for o in outs],
        in_specs=specs,
        out_specs=[pl.BlockSpec(memory_space=pltpu.VMEM)] * len(outs),
        scratch_shapes=list(scratch),
        compiler_params=pltpu.CompilerParams(vmem_limit_bytes=vmem * 2**20),
        cost_estimate=pl.CostEstimate(flops=10**6, bytes_accessed=10**6, transcendentals=0),
    )(*args, *unread)


def pack_body(
    at, keys, values, queries, gates, decay, mix, keep, send, small, levels, sems
):
    core = at[0]
    mine = pl.ds(pl.multiple_of(core * 512, 512), 512)
    theirs = pl.ds(pl.multiple_of((1 - core) * 512, 512), 512)
    copies = [
        pltpu.make_async_copy(decay, small, sems.at[0]),
        pltpu.make_async_copy(mix, levels, sems.at[1]),
    ]
    for i, ref in enumerate((keys, values, queries, gates)):
        rows = pl.ds(i * 256, 256)
        for out, cols, n in ((send, theirs, 2), (keep, mine, 6)):
            copies.append(pltpu.make_async_copy(ref.at[:, cols], out.at[rows, :], sems.at[n + i]))
    for copy in copies:
        copy.start()
    for copy in copies[:2]:
        copy.wait()
    for out, low in ((keep, core == 0), (send, core == 1)):
        logs = [jnp.where(low, small[0:4], small[4:8])]
        logs += [jnp.where(low, levels[l, 0:4], levels[l, 4:8]) for l in range(8)]
        logs = jnp.concatenate(logs + [jnp.zeros((12, 256), F32)], axis=0)
        high = logs.astype(BF)
        out[LOGS : LOGS + 48, 0:256] = high
        out[LOGS : LOGS + 48, 256:512] = (logs - high.astype(F32)).astype(BF)
    for copy in copies[2:]:
        copy.wait()


def logs_of(block):
    tile = block[LOGS : LOGS + 48, :].astype(F32)
    return tile[:, 0:256] + tile[:, 256:512]


def ends_body(at, keep, got, pay, first):
    core = at[0]
    logs = jnp.concatenate([logs_of(keep)[0:4], logs_of(got)[0:4]], axis=0)
    after = (
        lax.broadcasted_iota(jnp.int32, (256, 256), 1)
        > lax.broadcasted_iota(jnp.int32, (256, 256), 0)
    ).astype(F32)
    scale = jnp.exp(exact(after, logs, NT))
    total = jnp.sum(logs, axis=1, keepdims=True)
    for h in range(4):
        cols = slice(h * 128, h * 128 + 128)
        end = []
        for i, ref in enumerate((keep, got)):
            scaled = ref[0:256, cols].astype(F32) * scale[:, 4 * i + h : 4 * i + h + 1]
            end.append(dot(scaled.astype(BF), ref[256:512, cols], TN))
        own_log, got_log = total[h : h + 1], total[4 + h : 5 + h]
        own_later = jnp.exp(jnp.where(core == 0, got_log, 0.0))
        got_later = jnp.exp(jnp.where(core == 0, 0.0, own_log))
        pay[h, 0:128, :] = (end[0] * own_later + end[1] * got_later).astype(BF)
        pay[h, 128:144, :] = tail(own_log + got_log)
        first[h, :, :] = jnp.where(core == 0, end[0], end[1]).astype(BF)


def blocks_of(got):
    s = [got[i, 0:128, :].astype(F32) for i in range(4)]
    t = [untail(got[i, 128:144, :]) for i in range(4)]
    pair = s[0] * jnp.exp(t[1]) + s[1]
    return s, t, pair


def send_whole(s, t, pair, pay):
    state = (pair * jnp.exp(t[2] + t[3]) + s[2] * jnp.exp(t[3]) + s[3]).astype(BF)
    log = tail(t[0] + t[1] + t[2] + t[3])
    for i in range(4):
        pay[i, 0:128, :] = state
        pay[i, 128:144, :] = log


def lower_states(s, t, pair, at):
    odd, upper = at % 2 == 1, at >= 2
    one = jnp.where(odd, jnp.where(upper, s[2], s[0]), 0.0)
    step = jnp.where(odd, jnp.where(upper, t[2], t[0]), 0.0)
    two = jnp.where(upper, pair * jnp.exp(step), 0.0)
    before = sum(jnp.where(at > i, t[i], 0.0) for i in range(3))
    return one, two, before


def near_body(at, near, pay, *messages):
    s, t, pair = blocks_of(near)
    send_whole(s, t, pair, pay)
    for k, message in enumerate(messages):
        one, two, before = lower_states(s, t, pair, at[1] ^ k)
        message[0:128, 0:128] = one.astype(BF)
        message[0:128, 128:256] = two.astype(BF)
        message[128:144, 0:128] = tail(before)
        message[128:144, 128:256] = jnp.zeros((16, 128), BF)


def far_body(at, far, pay, states, before_out):
    s, t, pair = blocks_of(far)
    send_whole(s, t, pair, pay)
    one, two, before = lower_states(s, t, pair, at[2])
    states[:, 0:128] = one.astype(BF)
    states[:, 128:256] = two.astype(BF)
    before_out[...] = jnp.broadcast_to(before, (8, 128))


def last_body(at, rows, before, far, message):
    one, two, _ = lower_states(*blocks_of(rows), at[3])
    earlier = jnp.exp(before[0:1, :])
    one, two = (one * earlier).astype(BF), (two * earlier).astype(BF)
    for i in range(4):
        message[i, :, 0:256] = far[...]
        message[i, :, 256:384] = one
        message[i, :, 384:512] = two


def place(s, core):
    at = core if s == 0 else 1 - core
    return at, pl.ds(pl.multiple_of(at * 256, 256), 256)


def own_body(at, keep, got, first, mixture, coef):
    core = at[0]
    rows = lax.broadcasted_iota(jnp.int32, (256, 256), 0)
    cols = lax.broadcasted_iota(jnp.int32, (256, 256), 1)
    lower = rows >= cols
    upto = lower.astype(F32)
    both = (logs_of(keep), logs_of(got))
    for s, ref in enumerate((keep, got)):
        second, here = place(s, core)
        logs = both[s]
        at_row = exact(logs[0:8], upto, NT)
        at_col = exact(upto, logs[0:8], NT)
        level = logs.T
        first_log = jnp.sum(both[1 - s][0:4], axis=1, keepdims=True)
        first_log = jnp.where(second == 1, first_log, 0.0)
        for h in range(4):
            hc = slice(h * 128, h * 128 + 128)
            q, kb, v = ref[512:768, hc], ref[0:256, hc], ref[256:512, hc]
            local = at_col[:, h : h + 1]
            gap = jnp.where(lower, local - at_row[h : h + 1, :], -1e30)
            weights = (dot(q, kb, NT) * jnp.exp(gap)).astype(BF)
            m = [level[:, 4 + 4 * l + h : 5 + 4 * l + h] for l in range(8)]
            total = dot(weights, v) * m[0]
            start = jnp.exp(local)
            total += dot(q, first[h]) * jnp.where(second == 1, start * m[1], 0.0)
            mixture[here, hc] = total
            start = start * jnp.exp(first_log[h : h + 1])
            for l in range(2, 8):
                coef[here, 6 * h + l - 2 : 6 * h + l - 1] = start * m[l]


def mix_body(at, keep, got, mixture, coef, n0, n1, n2, n3, mixed, later, near):
    for k, n in enumerate((n0, n1, n2, n3)):
        near[at[1] ^ k] = n[...]
    for h in range(4):
        before = jnp.exp(untail(near[h, 128:144, 0:128])[:, 0:1])
        hc = slice(h * 128, h * 128 + 128)
        for s, ref in enumerate((keep, got)):
            _, here = place(s, at[0])
            read = dot(ref[512:768, hc], near[h, 0:128, :])
            total = mixture[here, hc] + read[:, 0:128] * coef[here, 6 * h : 6 * h + 1]
            mixed[here, hc] = total + read[:, 128:256] * coef[here, 6 * h + 1 : 6 * h + 2]
            later[here, 4 * h : 4 * h + 4] = coef[here, 6 * h + 2 : 6 * h + 6] * before


def norm_body(at, keep, got, gain, mixture, coef, states, normed):
    core = at[0]
    for h in range(4):
        mine = pl.ds(pl.multiple_of(core * 512 + h * 128, 128), 128)
        hc = slice(h * 128, h * 128 + 128)
        for s, ref in enumerate((keep, got)):
            _, here = place(s, core)
            z = ref[768:1024, hc].astype(F32)
            total = mixture[here, hc]
            for l in range(0, 4, 2):
                read = dot(ref[512:768, hc], states[h, :, l * 128 : l * 128 + 256])
                total += read[:, 0:128] * coef[here, 4 * h + l : 4 * h + l + 1]
                total += read[:, 128:256] * coef[here, 4 * h + l + 1 : 4 * h + l + 2]
            gated = total * (z / (1.0 + jnp.exp(-z)))
            size = lax.rsqrt(jnp.mean(gated * gated, axis=1, keepdims=True) + 1e-05)
            normed[here, hc] = (gated * size * gain[:, mine].astype(F32)).astype(BF)


def project_body(other, at, b0, b1, b2, b3, w0, w1, w2, w3, out, left, right, sems):
    row = (1 - at[0]) if other else at[0]
    rows = pl.ds(pl.multiple_of(row * 256, 256), 256)
    copies = [
        pltpu.make_async_copy(w, right.at[k], sems.at[k]) for k, w in enumerate((w0, w1, w2, w3))
    ]
    for copy in copies:
        copy.start()
    for j, block in enumerate((b0, b1, b2, b3)):
        left[(at[4] + 4 - j) % 4] = block[rows, :]
    total = 0.0
    for k, turn in enumerate((0, 1, 3, 2)):
        copies[k].wait()
        total += dot(left[(at[3] + turn) % 4], right[k].reshape(1024, 512), NT)
    out[...] = total.astype(out.dtype)


def project(at, blocks, rights, other):
    return call(
        functools.partial(project_body, other),
        [((256, 1024), BF if other else F32)],
        (at, *blocks, *rights),
        scratch=[
            pltpu.VMEM((4, 256, 512), BF),
            pltpu.VMEM((4, 16, 64, 512), BF),
            pltpu.SemaphoreType.DMA((4,)),
        ],
        hbm=range(5, 9),
        vmem=20,
    )[0]


def shift(value, axis, by):
    return lax.ppermute(value, axis, [(i, (i + by) % 4) for i in range(4)])


def shards(values, keys, queries, gates, log_decay, level_mix, norm_gain, weight):
    y, a, b, c, x = (lax.axis_index(n) for n in ("y", "a", NEAR, "c", "x"))
    at = jnp.stack([c, b, a, y, x]).astype(jnp.int32)
    kept = lax.dynamic_slice_in_dim(weight, c * 512, 512, 1)
    theirs = swap(lax.dynamic_slice_in_dim(weight, (1 - c) * 512, 512, 1))
    both = jnp.concatenate(
        [jnp.where(c == 0, kept, theirs), jnp.where(c == 0, theirs, kept)]
    )
    perm = [(s * 4 + f, f * 4 + s) for s in range(4) for f in range(4)]
    mine = lax.ppermute(both, ("y", "x"), perm)
    block = ((ROWS, 512), BF)
    keep, send = call(
        pack_body,
        [block, block],
        (at, keys, values, queries, gates, log_decay, level_mix),
        scratch=[
            pltpu.VMEM((8, 256), F32),
            pltpu.VMEM((8, 8, 256), F32),
            pltpu.SemaphoreType.DMA((10,)),
        ],
        hbm=range(1, 7),
        vmem=60,
    )
    mine, send = lax.optimization_barrier((mine, send))
    gathered = lax.all_gather(mine, ("a", "p", "q"))

    got = swap(send)
    pay = ((4, 144, 128), BF)
    pay_b, first = call(ends_body, [pay, ((4, 128, 128), BF)], (at, keep, got))
    near = lax.all_to_all(pay_b, NEAR, 0, 0, tiled=True)
    pay_a, *near = call(near_body, [pay] + [((144, 256), BF)] * 4, (at, near))
    far = lax.all_to_all(pay_a, "a", 0, 0, tiled=True)
    near = near[:1] + [
        lax.ppermute(near[k], NEAR, [(i, i ^ k) for i in range(4)]) for k in (1, 2, 3)
    ]
    mixture, coef = call(
        own_body, [((512, 512), F32), ((512, 24), F32)], (at, keep, got, first)
    )
    pay_y, far, before = call(
        far_body,
        [pay, ((128, 256), BF), ((8, 128), F32)],
        (at, far),
        unread=near[1:],
    )
    rows = lax.all_to_all(pay_y, "y", 0, 0, tiled=True)
    (states,) = call(
        last_body, [((4, 128, 512), BF)], (at, rows, before, far), unread=(mixture,)
    )
    states = lax.all_to_all(states, NEAR, 0, 0, tiled=True)
    mixture, coef = call(
        mix_body,
        [((512, 512), F32), ((512, 16), F32)],
        (at, keep, got, mixture, coef, *near),
        scratch=[pltpu.VMEM((4, 144, 256), BF)],
    )
    _, gathered = lax.optimization_barrier((coef, gathered))
    rights = [gathered] + [shift(gathered, "y", 4 - k) for k in (1, 3, 2)]
    (normed,) = call(
        norm_body, [((512, 512), BF)], (at, keep, got, norm_gain[None], mixture, coef, states)
    )

    blocks = [normed] + [shift(normed, "x", j) for j in (1, 2, 3)]
    theirs = swap(project(at, blocks, rights, True))
    own = project(at, blocks, rights, False)
    return (own + theirs.astype(F32)).astype(BF)


def solution(mesh):
    fine = Mesh(mesh.devices.reshape(4, 4, 2, 2, 2, 4), SEQ + ("x",))
    return jax.shard_map(
        shards,
        mesh=fine,
        in_specs=(
            P(SEQ, "x"),
            P(SEQ, "x"),
            P(SEQ, "x"),
            P(SEQ, "x"),
            P("x", SEQ),
            P(None, "x", SEQ),
            P("x"),
            P(SEQ, "x"),
        ),
        out_specs=P(SEQ, "x"),
        check_vma=False,
    )
```

```python
import functools

import jax
import jax.numpy as jnp
from jax import lax
from jax.experimental import pallas as pl
from jax.experimental.pallas import tpu as pltpu
from jax.sharding import Mesh, PartitionSpec as P

BF = jnp.bfloat16
F32 = jnp.float32
SEQ = ("y", "a", "p", "q", "c")
NEAR = ("p", "q")
NT = (((1,), (1,)), ((), ()))
TN = (((0,), (0,)), ((), ()))
LOGS = 1024
ROWS = 1072


def swap(value):
    return lax.ppermute(value, "c", [(0, 1), (1, 0)])


def dot(left, right, dims=(((1,), (0,)), ((), ()))):
    return lax.dot_general(left, right, dims, preferred_element_type=F32)


def exact(left, right, dims):
    return lax.dot_general(
        left, right, dims, precision=lax.Precision.HIGHEST, preferred_element_type=F32
    )


def tail(log):
    high = log.astype(BF).astype(F32)
    middle = (log - high).astype(BF).astype(F32)
    low = log - high - middle
    row = lax.broadcasted_iota(jnp.int32, (16, 128), 0)
    return jnp.where(
        row == 0, high, jnp.where(row == 1, middle, jnp.where(row == 2, low, 0.0))
    ).astype(BF)


def untail(tile):
    return jnp.sum(tile.astype(F32), axis=0, keepdims=True)


def call(body, outs, args, unread=(), scratch=(), hbm=(), vmem=12):
    specs = [pl.BlockSpec(memory_space=pltpu.SMEM)]
    specs += [
        pl.BlockSpec(memory_space=pltpu.HBM if i in hbm else pltpu.VMEM)
        for i in range(1, len(args))
    ]
    specs += [pl.BlockSpec(memory_space=pl.ANY)] * len(unread)

    def run(*refs):
        body(*refs[: len(args)], *refs[len(args) + len(unread) :])

    return pl.pallas_call(
        run,
        out_shape=[jax.ShapeDtypeStruct(*o) for o in outs],
        in_specs=specs,
        out_specs=[pl.BlockSpec(memory_space=pltpu.VMEM)] * len(outs),
        scratch_shapes=list(scratch),
        compiler_params=pltpu.CompilerParams(vmem_limit_bytes=vmem * 2**20),
        cost_estimate=pl.CostEstimate(flops=10**6, bytes_accessed=10**6, transcendentals=0),
    )(*args, *unread)


def pack_body(
    at, keys, values, queries, gates, decay, mix, keep, send, small, levels, sems
):
    core = at[0]
    mine = pl.ds(pl.multiple_of(core * 512, 512), 512)
    theirs = pl.ds(pl.multiple_of((1 - core) * 512, 512), 512)
    copies = [
        pltpu.make_async_copy(decay, small, sems.at[0]),
        pltpu.make_async_copy(mix, levels, sems.at[1]),
    ]
    for i, ref in enumerate((keys, values, queries, gates)):
        rows = pl.ds(i * 256, 256)
        for out, cols, n in ((send, theirs, 2), (keep, mine, 6)):
            copies.append(pltpu.make_async_copy(ref.at[:, cols], out.at[rows, :], sems.at[n + i]))
    for copy in copies:
        copy.start()
    for copy in copies[:2]:
        copy.wait()
    for out, low in ((keep, core == 0), (send, core == 1)):
        logs = [jnp.where(low, small[0:4], small[4:8])]
        logs += [jnp.where(low, levels[l, 0:4], levels[l, 4:8]) for l in range(8)]
        logs = jnp.concatenate(logs + [jnp.zeros((12, 256), F32)], axis=0)
        high = logs.astype(BF)
        out[LOGS : LOGS + 48, 0:256] = high
        out[LOGS : LOGS + 48, 256:512] = (logs - high.astype(F32)).astype(BF)
    for copy in copies[2:]:
        copy.wait()


def logs_of(block):
    tile = block[LOGS : LOGS + 48, :].astype(F32)
    return tile[:, 0:256] + tile[:, 256:512]


def ends_body(at, keep, got, pay, first):
    core = at[0]
    logs = jnp.concatenate([logs_of(keep)[0:4], logs_of(got)[0:4]], axis=0)
    after = (
        lax.broadcasted_iota(jnp.int32, (256, 256), 1)
        > lax.broadcasted_iota(jnp.int32, (256, 256), 0)
    ).astype(F32)
    scale = jnp.exp(exact(after, logs, NT))
    total = jnp.sum(logs, axis=1, keepdims=True)
    for h in range(4):
        cols = slice(h * 128, h * 128 + 128)
        end = []
        for i, ref in enumerate((keep, got)):
            scaled = ref[0:256, cols].astype(F32) * scale[:, 4 * i + h : 4 * i + h + 1]
            end.append(dot(scaled.astype(BF), ref[256:512, cols], TN))
        own_log, got_log = total[h : h + 1], total[4 + h : 5 + h]
        own_later = jnp.exp(jnp.where(core == 0, got_log, 0.0))
        got_later = jnp.exp(jnp.where(core == 0, 0.0, own_log))
        pay[h, 0:128, :] = (end[0] * own_later + end[1] * got_later).astype(BF)
        pay[h, 128:144, :] = tail(own_log + got_log)
        first[h, :, :] = jnp.where(core == 0, end[0], end[1]).astype(BF)


def blocks_of(got):
    s = [got[i, 0:128, :].astype(F32) for i in range(4)]
    t = [untail(got[i, 128:144, :]) for i in range(4)]
    pair = s[0] * jnp.exp(t[1]) + s[1]
    return s, t, pair


def send_whole(s, t, pair, pay):
    state = (pair * jnp.exp(t[2] + t[3]) + s[2] * jnp.exp(t[3]) + s[3]).astype(BF)
    log = tail(t[0] + t[1] + t[2] + t[3])
    for i in range(4):
        pay[i, 0:128, :] = state
        pay[i, 128:144, :] = log


def lower_states(s, t, pair, at):
    odd, upper = at % 2 == 1, at >= 2
    one = jnp.where(odd, jnp.where(upper, s[2], s[0]), 0.0)
    step = jnp.where(odd, jnp.where(upper, t[2], t[0]), 0.0)
    two = jnp.where(upper, pair * jnp.exp(step), 0.0)
    before = sum(jnp.where(at > i, t[i], 0.0) for i in range(3))
    return one, two, before


def near_body(at, near, pay, *messages):
    s, t, pair = blocks_of(near)
    send_whole(s, t, pair, pay)
    for k, message in enumerate(messages):
        one, two, before = lower_states(s, t, pair, at[1] ^ k)
        message[0:128, 0:128] = one.astype(BF)
        message[0:128, 128:256] = two.astype(BF)
        message[128:144, 0:128] = tail(before)
        message[128:144, 128:256] = jnp.zeros((16, 128), BF)


def far_body(at, far, pay, states, before_out):
    s, t, pair = blocks_of(far)
    send_whole(s, t, pair, pay)
    one, two, before = lower_states(s, t, pair, at[2])
    states[:, 0:128] = one.astype(BF)
    states[:, 128:256] = two.astype(BF)
    before_out[...] = jnp.broadcast_to(before, (8, 128))


def last_body(at, rows, before, far, message):
    one, two, _ = lower_states(*blocks_of(rows), at[3])
    earlier = jnp.exp(before[0:1, :])
    one, two = (one * earlier).astype(BF), (two * earlier).astype(BF)
    for i in range(4):
        message[i, :, 0:256] = far[...]
        message[i, :, 256:384] = one
        message[i, :, 384:512] = two


def place(s, core):
    at = core if s == 0 else 1 - core
    return at, pl.ds(pl.multiple_of(at * 256, 256), 256)


def own_body(at, keep, got, first, mixture, coef):
    core = at[0]
    rows = lax.broadcasted_iota(jnp.int32, (256, 256), 0)
    cols = lax.broadcasted_iota(jnp.int32, (256, 256), 1)
    lower = rows >= cols
    upto = lower.astype(F32)
    both = (logs_of(keep), logs_of(got))
    for s, ref in enumerate((keep, got)):
        second, here = place(s, core)
        logs = both[s]
        at_row = exact(logs[0:8], upto, NT)
        at_col = exact(upto, logs[0:8], NT)
        level = logs.T
        first_log = jnp.sum(both[1 - s][0:4], axis=1, keepdims=True)
        first_log = jnp.where(second == 1, first_log, 0.0)
        for h in range(4):
            hc = slice(h * 128, h * 128 + 128)
            q, kb, v = ref[512:768, hc], ref[0:256, hc], ref[256:512, hc]
            local = at_col[:, h : h + 1]
            gap = jnp.where(lower, local - at_row[h : h + 1, :], -1e30)
            weights = (dot(q, kb, NT) * jnp.exp(gap)).astype(BF)
            m = [level[:, 4 + 4 * l + h : 5 + 4 * l + h] for l in range(8)]
            total = dot(weights, v) * m[0]
            start = jnp.exp(local)
            total += dot(q, first[h]) * jnp.where(second == 1, start * m[1], 0.0)
            mixture[here, hc] = total
            start = start * jnp.exp(first_log[h : h + 1])
            for l in range(2, 8):
                coef[here, 6 * h + l - 2 : 6 * h + l - 1] = start * m[l]


def mix_body(at, keep, got, mixture, coef, n0, n1, n2, n3, mixed, later, near):
    for k, n in enumerate((n0, n1, n2, n3)):
        near[at[1] ^ k] = n[...]
    for h in range(4):
        before = jnp.exp(untail(near[h, 128:144, 0:128])[:, 0:1])
        hc = slice(h * 128, h * 128 + 128)
        for s, ref in enumerate((keep, got)):
            _, here = place(s, at[0])
            read = dot(ref[512:768, hc], near[h, 0:128, :])
            total = mixture[here, hc] + read[:, 0:128] * coef[here, 6 * h : 6 * h + 1]
            mixed[here, hc] = total + read[:, 128:256] * coef[here, 6 * h + 1 : 6 * h + 2]
            later[here, 4 * h : 4 * h + 4] = coef[here, 6 * h + 2 : 6 * h + 6] * before


def norm_body(at, keep, got, gain, mixture, coef, states, normed):
    core = at[0]
    for h in range(4):
        mine = pl.ds(pl.multiple_of(core * 512 + h * 128, 128), 128)
        hc = slice(h * 128, h * 128 + 128)
        for s, ref in enumerate((keep, got)):
            _, here = place(s, core)
            z = ref[768:1024, hc].astype(F32)
            total = mixture[here, hc]
            for l in range(0, 4, 2):
                read = dot(ref[512:768, hc], states[h, :, l * 128 : l * 128 + 256])
                total += read[:, 0:128] * coef[here, 4 * h + l : 4 * h + l + 1]
                total += read[:, 128:256] * coef[here, 4 * h + l + 1 : 4 * h + l + 2]
            gated = total * (z / (1.0 + jnp.exp(-z)))
            size = lax.rsqrt(jnp.mean(gated * gated, axis=1, keepdims=True) + 1e-05)
            normed[here, hc] = (gated * size * gain[:, mine].astype(F32)).astype(BF)


def project_body(other, at, b0, b1, b2, b3, weights, out, left, right, sems):
    row = (1 - at[0]) if other else at[0]
    rows = pl.ds(pl.multiple_of(row * 256, 256), 256)
    copies = [pltpu.make_async_copy(weights.at[f], right.at[f], sems.at[f]) for f in range(4)]
    for copy in copies:
        copy.start()
    for j, block in enumerate((b0, b1, b2, b3)):
        left[(at[4] + 4 - j) % 4] = block[rows, :]
    total = 0.0
    for f in range(4):
        copies[f].wait()
        total += dot(left[f], right[f].reshape(1024, 512), NT)
    out[...] = total.astype(out.dtype)


def project(at, blocks, weights, other):
    return call(
        functools.partial(project_body, other),
        [((256, 1024), BF if other else F32)],
        (at, *blocks, weights),
        scratch=[
            pltpu.VMEM((4, 256, 512), BF),
            pltpu.VMEM((4, 16, 64, 512), BF),
            pltpu.SemaphoreType.DMA((4,)),
        ],
        hbm=(5,),
        vmem=20,
    )[0]


def shift(value, axis, by):
    return lax.ppermute(value, axis, [(i, (i + by) % 4) for i in range(4)])


def shards(values, keys, queries, gates, log_decay, level_mix, norm_gain, weight):
    y, a, b, c, x = (lax.axis_index(n) for n in ("y", "a", NEAR, "c", "x"))
    at = jnp.stack([c, b, a, y, x]).astype(jnp.int32)
    kept = lax.dynamic_slice_in_dim(weight, c * 512, 512, 1)
    theirs = swap(lax.dynamic_slice_in_dim(weight, (1 - c) * 512, 512, 1))
    both = jnp.concatenate(
        [jnp.where(c == 0, kept, theirs), jnp.where(c == 0, theirs, kept)]
    )
    perm = [(s * 4 + f, f * 4 + s) for s in range(4) for f in range(4)]
    mine = lax.ppermute(both, ("y", "x"), perm)
    block = ((ROWS, 512), BF)
    keep, send = call(
        pack_body,
        [block, block],
        (at, keys, values, queries, gates, log_decay, level_mix),
        scratch=[
            pltpu.VMEM((8, 256), F32),
            pltpu.VMEM((8, 8, 256), F32),
            pltpu.SemaphoreType.DMA((10,)),
        ],
        hbm=range(1, 7),
        vmem=60,
    )
    gathered = lax.all_gather(mine, ("a", "p", "q"))

    got = swap(send)
    pay = ((4, 144, 128), BF)
    pay_b, first = call(ends_body, [pay, ((4, 128, 128), BF)], (at, keep, got))
    near = lax.all_to_all(pay_b, NEAR, 0, 0, tiled=True)
    pay_a, *near = call(near_body, [pay] + [((144, 256), BF)] * 4, (at, near))
    far = lax.all_to_all(pay_a, "a", 0, 0, tiled=True)
    near = near[:1] + [
        lax.ppermute(near[k], NEAR, [(i, i ^ k) for i in range(4)]) for k in (1, 2, 3)
    ]
    mixture, coef = call(
        own_body, [((512, 512), F32), ((512, 24), F32)], (at, keep, got, first)
    )
    pay_y, far, before = call(
        far_body,
        [pay, ((128, 256), BF), ((8, 128), F32)],
        (at, far),
        unread=near[1:],
    )
    rows = lax.all_to_all(pay_y, "y", 0, 0, tiled=True)
    (states,) = call(last_body, [((4, 128, 512), BF)], (at, rows, before, far))
    states = lax.all_to_all(states, NEAR, 0, 0, tiled=True)
    mixture, coef = call(
        mix_body,
        [((512, 512), F32), ((512, 16), F32)],
        (at, keep, got, mixture, coef, *near),
        scratch=[pltpu.VMEM((4, 144, 256), BF)],
    )
    _, gathered = lax.optimization_barrier((coef, gathered))
    gathered = jnp.broadcast_to(gathered[None], (4, 16, 64, 512))
    weights = lax.all_to_all(gathered, "y", 0, 0, tiled=True)
    (normed,) = call(
        norm_body, [((512, 512), BF)], (at, keep, got, norm_gain[None], mixture, coef, states)
    )

    blocks = [normed] + [shift(normed, "x", j) for j in (1, 2, 3)]
    theirs = swap(project(at, blocks, weights, True))
    own = project(at, blocks, weights, False)
    return (own + theirs.astype(F32)).astype(BF)


def solution(mesh):
    fine = Mesh(mesh.devices.reshape(4, 4, 2, 2, 2, 4), SEQ + ("x",))
    return jax.shard_map(
        shards,
        mesh=fine,
        in_specs=(
            P(SEQ, "x"),
            P(SEQ, "x"),
            P(SEQ, "x"),
            P(SEQ, "x"),
            P("x", SEQ),
            P(None, "x", SEQ),
            P("x"),
            P(SEQ, "x"),
        ),
        out_specs=P(SEQ, "x"),
        check_vma=False,
    )
```

```python
import functools

import jax
import jax.numpy as jnp
from jax import lax
from jax.experimental import pallas as pl
from jax.experimental.pallas import tpu as pltpu
from jax.sharding import Mesh, PartitionSpec as P

BF = jnp.bfloat16
F32 = jnp.float32
SEQ = ("y", "a", "p", "q", "c")
NEAR = ("p", "q")
NT = (((1,), (1,)), ((), ()))
TN = (((0,), (0,)), ((), ()))
LOGS = 1024
ROWS = 1072


def swap(value):
    return lax.ppermute(value, "c", [(0, 1), (1, 0)])


def dot(left, right, dims=(((1,), (0,)), ((), ()))):
    return lax.dot_general(left, right, dims, preferred_element_type=F32)


def exact(left, right, dims):
    return lax.dot_general(
        left, right, dims, precision=lax.Precision.HIGHEST, preferred_element_type=F32
    )


def tail(log):
    high = log.astype(BF).astype(F32)
    middle = (log - high).astype(BF).astype(F32)
    low = log - high - middle
    row = lax.broadcasted_iota(jnp.int32, (16, 128), 0)
    return jnp.where(
        row == 0, high, jnp.where(row == 1, middle, jnp.where(row == 2, low, 0.0))
    ).astype(BF)


def untail(tile):
    return jnp.sum(tile.astype(F32), axis=0, keepdims=True)


def call(body, outs, args, unread=(), scratch=(), hbm=(), vmem=12):
    specs = [pl.BlockSpec(memory_space=pltpu.SMEM)]
    specs += [
        pl.BlockSpec(memory_space=pltpu.HBM if i in hbm else pltpu.VMEM)
        for i in range(1, len(args))
    ]
    specs += [pl.BlockSpec(memory_space=pl.ANY)] * len(unread)

    def run(*refs):
        body(*refs[: len(args)], *refs[len(args) + len(unread) :])

    return pl.pallas_call(
        run,
        out_shape=[jax.ShapeDtypeStruct(*o) for o in outs],
        in_specs=specs,
        out_specs=[pl.BlockSpec(memory_space=pltpu.VMEM)] * len(outs),
        scratch_shapes=list(scratch),
        compiler_params=pltpu.CompilerParams(vmem_limit_bytes=vmem * 2**20),
        cost_estimate=pl.CostEstimate(flops=10**6, bytes_accessed=10**6, transcendentals=0),
    )(*args, *unread)


def pack_body(
    at, keys, values, queries, gates, decay, mix, keep, send, small, levels, sems
):
    core = at[0]
    mine = pl.ds(pl.multiple_of(core * 512, 512), 512)
    theirs = pl.ds(pl.multiple_of((1 - core) * 512, 512), 512)
    copies = [
        pltpu.make_async_copy(decay, small, sems.at[0]),
        pltpu.make_async_copy(mix, levels, sems.at[1]),
    ]
    for i, ref in enumerate((keys, values, queries, gates)):
        rows = pl.ds(i * 256, 256)
        for out, cols, n in ((send, theirs, 2), (keep, mine, 6)):
            copies.append(pltpu.make_async_copy(ref.at[:, cols], out.at[rows, :], sems.at[n + i]))
    for copy in copies:
        copy.start()
    for copy in copies[:2]:
        copy.wait()
    for out, low in ((keep, core == 0), (send, core == 1)):
        logs = [jnp.where(low, small[0:4], small[4:8])]
        logs += [jnp.where(low, levels[l, 0:4], levels[l, 4:8]) for l in range(8)]
        logs = jnp.concatenate(logs + [jnp.zeros((12, 256), F32)], axis=0)
        high = logs.astype(BF)
        out[LOGS : LOGS + 48, 0:256] = high
        out[LOGS : LOGS + 48, 256:512] = (logs - high.astype(F32)).astype(BF)
    for copy in copies[2:]:
        copy.wait()


def logs_of(block):
    tile = block[LOGS : LOGS + 48, :].astype(F32)
    return tile[:, 0:256] + tile[:, 256:512]


def ends_body(at, keep, got, pay, first):
    core = at[0]
    logs = jnp.concatenate([logs_of(keep)[0:4], logs_of(got)[0:4]], axis=0)
    after = (
        lax.broadcasted_iota(jnp.int32, (256, 256), 1)
        > lax.broadcasted_iota(jnp.int32, (256, 256), 0)
    ).astype(F32)
    scale = jnp.exp(exact(after, logs, NT))
    total = jnp.sum(logs, axis=1, keepdims=True)
    for h in range(4):
        cols = slice(h * 128, h * 128 + 128)
        end = []
        for i, ref in enumerate((keep, got)):
            scaled = ref[0:256, cols].astype(F32) * scale[:, 4 * i + h : 4 * i + h + 1]
            end.append(dot(scaled.astype(BF), ref[256:512, cols], TN))
        own_log, got_log = total[h : h + 1], total[4 + h : 5 + h]
        own_later = jnp.exp(jnp.where(core == 0, got_log, 0.0))
        got_later = jnp.exp(jnp.where(core == 0, 0.0, own_log))
        pay[h, 0:128, :] = (end[0] * own_later + end[1] * got_later).astype(BF)
        pay[h, 128:144, :] = tail(own_log + got_log)
        first[h, :, :] = jnp.where(core == 0, end[0], end[1]).astype(BF)


def blocks_of(got):
    s = [got[i, 0:128, :].astype(F32) for i in range(4)]
    t = [untail(got[i, 128:144, :]) for i in range(4)]
    pair = s[0] * jnp.exp(t[1]) + s[1]
    return s, t, pair


def send_whole(s, t, pair, pay):
    state = (pair * jnp.exp(t[2] + t[3]) + s[2] * jnp.exp(t[3]) + s[3]).astype(BF)
    log = tail(t[0] + t[1] + t[2] + t[3])
    for i in range(4):
        pay[i, 0:128, :] = state
        pay[i, 128:144, :] = log


def lower_states(s, t, pair, at):
    odd, upper = at % 2 == 1, at >= 2
    one = jnp.where(odd, jnp.where(upper, s[2], s[0]), 0.0)
    step = jnp.where(odd, jnp.where(upper, t[2], t[0]), 0.0)
    two = jnp.where(upper, pair * jnp.exp(step), 0.0)
    before = sum(jnp.where(at > i, t[i], 0.0) for i in range(3))
    return one, two, before


def near_body(at, near, pay, *messages):
    s, t, pair = blocks_of(near)
    send_whole(s, t, pair, pay)
    for k, message in enumerate(messages):
        one, two, before = lower_states(s, t, pair, at[1] ^ k)
        message[0:128, 0:128] = one.astype(BF)
        message[0:128, 128:256] = two.astype(BF)
        message[128:144, 0:128] = tail(before)
        message[128:144, 128:256] = jnp.zeros((16, 128), BF)


def far_body(at, far, pay, states, before_out):
    s, t, pair = blocks_of(far)
    send_whole(s, t, pair, pay)
    one, two, before = lower_states(s, t, pair, at[2])
    states[:, 0:128] = one.astype(BF)
    states[:, 128:256] = two.astype(BF)
    before_out[...] = jnp.broadcast_to(before, (8, 128))


def last_body(at, rows, before, far, message):
    one, two, _ = lower_states(*blocks_of(rows), at[3])
    earlier = jnp.exp(before[0:1, :])
    one, two = (one * earlier).astype(BF), (two * earlier).astype(BF)
    for i in range(4):
        message[i, :, 0:256] = far[...]
        message[i, :, 256:384] = one
        message[i, :, 384:512] = two


def place(s, core):
    at = core if s == 0 else 1 - core
    return at, pl.ds(pl.multiple_of(at * 256, 256), 256)


def own_body(at, keep, got, first, mixture, coef):
    core = at[0]
    rows = lax.broadcasted_iota(jnp.int32, (256, 256), 0)
    cols = lax.broadcasted_iota(jnp.int32, (256, 256), 1)
    lower = rows >= cols
    upto = lower.astype(F32)
    both = (logs_of(keep), logs_of(got))
    for s, ref in enumerate((keep, got)):
        second, here = place(s, core)
        logs = both[s]
        at_row = exact(logs[0:8], upto, NT)
        at_col = exact(upto, logs[0:8], NT)
        level = logs.T
        first_log = jnp.sum(both[1 - s][0:4], axis=1, keepdims=True)
        first_log = jnp.where(second == 1, first_log, 0.0)
        for h in range(4):
            hc = slice(h * 128, h * 128 + 128)
            q, kb, v = ref[512:768, hc], ref[0:256, hc], ref[256:512, hc]
            local = at_col[:, h : h + 1]
            gap = jnp.where(lower, local - at_row[h : h + 1, :], -1e30)
            weights = (dot(q, kb, NT) * jnp.exp(gap)).astype(BF)
            m = [level[:, 4 + 4 * l + h : 5 + 4 * l + h] for l in range(8)]
            total = dot(weights, v) * m[0]
            start = jnp.exp(local)
            total += dot(q, first[h]) * jnp.where(second == 1, start * m[1], 0.0)
            mixture[here, hc] = total
            start = start * jnp.exp(first_log[h : h + 1])
            for l in range(2, 8):
                coef[here, 6 * h + l - 2 : 6 * h + l - 1] = start * m[l]


def mix_body(at, keep, got, mixture, coef, n0, n1, n2, n3, mixed, later, near):
    for k, n in enumerate((n0, n1, n2, n3)):
        near[at[1] ^ k] = n[...]
    for h in range(4):
        before = jnp.exp(untail(near[h, 128:144, 0:128])[:, 0:1])
        hc = slice(h * 128, h * 128 + 128)
        for s, ref in enumerate((keep, got)):
            _, here = place(s, at[0])
            read = dot(ref[512:768, hc], near[h, 0:128, :])
            total = mixture[here, hc] + read[:, 0:128] * coef[here, 6 * h : 6 * h + 1]
            mixed[here, hc] = total + read[:, 128:256] * coef[here, 6 * h + 1 : 6 * h + 2]
            later[here, 4 * h : 4 * h + 4] = coef[here, 6 * h + 2 : 6 * h + 6] * before


def norm_body(at, keep, got, gain, mixture, coef, states, normed):
    core = at[0]
    for h in range(4):
        mine = pl.ds(pl.multiple_of(core * 512 + h * 128, 128), 128)
        hc = slice(h * 128, h * 128 + 128)
        for s, ref in enumerate((keep, got)):
            _, here = place(s, core)
            z = ref[768:1024, hc].astype(F32)
            total = mixture[here, hc]
            for l in range(0, 4, 2):
                read = dot(ref[512:768, hc], states[h, :, l * 128 : l * 128 + 256])
                total += read[:, 0:128] * coef[here, 4 * h + l : 4 * h + l + 1]
                total += read[:, 128:256] * coef[here, 4 * h + l + 1 : 4 * h + l + 2]
            gated = total * (z / (1.0 + jnp.exp(-z)))
            size = lax.rsqrt(jnp.mean(gated * gated, axis=1, keepdims=True) + 1e-05)
            normed[here, hc] = (gated * size * gain[:, mine].astype(F32)).astype(BF)


def project_body(other, at, b0, b1, b2, b3, w0, w1, w2, w3, out, left, right, sems):
    row = (1 - at[0]) if other else at[0]
    rows = pl.ds(pl.multiple_of(row * 256, 256), 256)
    copies = [
        pltpu.make_async_copy(w, right.at[k], sems.at[k]) for k, w in enumerate((w0, w1, w2, w3))
    ]
    for copy in copies:
        copy.start()
    for j, block in enumerate((b0, b1, b2, b3)):
        left[(at[4] + 4 - j) % 4] = block[rows, :]
    total = 0.0
    for k, turn in enumerate((0, 1, 3, 2)):
        copies[k].wait()
        total += dot(left[(at[3] + turn) % 4], right[k].reshape(1024, 512), NT)
    out[...] = total.astype(out.dtype)


def project(at, blocks, rights, other):
    return call(
        functools.partial(project_body, other),
        [((256, 1024), BF if other else F32)],
        (at, *blocks, *rights),
        scratch=[
            pltpu.VMEM((4, 256, 512), BF),
            pltpu.VMEM((4, 16, 64, 512), BF),
            pltpu.SemaphoreType.DMA((4,)),
        ],
        hbm=range(5, 9),
        vmem=20,
    )[0]


def shift(value, axis, by):
    return lax.ppermute(value, axis, [(i, (i + by) % 4) for i in range(4)])


def shards(values, keys, queries, gates, log_decay, level_mix, norm_gain, weight):
    y, a, b, c, x = (lax.axis_index(n) for n in ("y", "a", NEAR, "c", "x"))
    at = jnp.stack([c, b, a, y, x]).astype(jnp.int32)
    kept = lax.dynamic_slice_in_dim(weight, c * 512, 512, 1)
    theirs = swap(lax.dynamic_slice_in_dim(weight, (1 - c) * 512, 512, 1))
    both = jnp.concatenate(
        [jnp.where(c == 0, kept, theirs), jnp.where(c == 0, theirs, kept)]
    )
    perm = [(s * 4 + f, f * 4 + s) for s in range(4) for f in range(4)]
    mine = lax.ppermute(both, ("y", "x"), perm)
    mine, log_decay = lax.optimization_barrier((mine, log_decay))
    gathered = lax.all_gather(mine, ("a", "p", "q"))

    block = ((ROWS, 512), BF)
    keep, send = call(
        pack_body,
        [block, block],
        (at, keys, values, queries, gates, log_decay, level_mix),
        scratch=[
            pltpu.VMEM((8, 256), F32),
            pltpu.VMEM((8, 8, 256), F32),
            pltpu.SemaphoreType.DMA((10,)),
        ],
        hbm=range(1, 7),
        vmem=60,
    )
    got = swap(send)
    pay = ((4, 144, 128), BF)
    pay_b, first = call(ends_body, [pay, ((4, 128, 128), BF)], (at, keep, got))
    near = lax.all_to_all(pay_b, NEAR, 0, 0, tiled=True)
    pay_a, *near = call(near_body, [pay] + [((144, 256), BF)] * 4, (at, near))
    far = lax.all_to_all(pay_a, "a", 0, 0, tiled=True)
    near = near[:1] + [
        lax.ppermute(near[k], NEAR, [(i, i ^ k) for i in range(4)]) for k in (1, 2, 3)
    ]
    mixture, coef = call(
        own_body, [((512, 512), F32), ((512, 24), F32)], (at, keep, got, first)
    )
    pay_y, far, before = call(
        far_body,
        [pay, ((128, 256), BF), ((8, 128), F32)],
        (at, far),
        unread=near[1:],
    )
    rows = lax.all_to_all(pay_y, "y", 0, 0, tiled=True)
    (states,) = call(last_body, [((4, 128, 512), BF)], (at, rows, before, far))
    states = lax.all_to_all(states, NEAR, 0, 0, tiled=True)
    mixture, coef = call(
        mix_body,
        [((512, 512), F32), ((512, 16), F32)],
        (at, keep, got, mixture, coef, *near),
        scratch=[pltpu.VMEM((4, 144, 256), BF)],
    )
    _, gathered = lax.optimization_barrier((coef, gathered))
    rights = [gathered] + [shift(gathered, "y", 4 - k) for k in (1, 3, 2)]
    (normed,) = call(
        norm_body, [((512, 512), BF)], (at, keep, got, norm_gain[None], mixture, coef, states)
    )

    blocks = [normed] + [shift(normed, "x", j) for j in (1, 2, 3)]
    theirs = swap(project(at, blocks, rights, True))
    own = project(at, blocks, rights, False)
    return (own + theirs.astype(F32)).astype(BF)


def solution(mesh):
    fine = Mesh(mesh.devices.reshape(4, 4, 2, 2, 2, 4), SEQ + ("x",))
    return jax.shard_map(
        shards,
        mesh=fine,
        in_specs=(
            P(SEQ, "x"),
            P(SEQ, "x"),
            P(SEQ, "x"),
            P(SEQ, "x"),
            P("x", SEQ),
            P(None, "x", SEQ),
            P("x"),
            P(SEQ, "x"),
        ),
        out_specs=P(SEQ, "x"),
        check_vma=False,
    )
```

```python
import functools

import jax
import jax.numpy as jnp
from jax import lax
from jax.experimental import pallas as pl
from jax.experimental.pallas import tpu as pltpu
from jax.sharding import Mesh, PartitionSpec as P

BF = jnp.bfloat16
F32 = jnp.float32
SEQ = ("y", "a", "p", "q", "c")
NEAR = ("p", "q")
NT = (((1,), (1,)), ((), ()))
TN = (((0,), (0,)), ((), ()))
LOGS = 1024
ROWS = 1072


def swap(value):
    return lax.ppermute(value, "c", [(0, 1), (1, 0)])


def dot(left, right, dims=(((1,), (0,)), ((), ()))):
    return lax.dot_general(left, right, dims, preferred_element_type=F32)


def exact(left, right, dims):
    return lax.dot_general(
        left, right, dims, precision=lax.Precision.HIGHEST, preferred_element_type=F32
    )


def tail(log):
    high = log.astype(BF).astype(F32)
    middle = (log - high).astype(BF).astype(F32)
    low = log - high - middle
    row = lax.broadcasted_iota(jnp.int32, (16, 128), 0)
    return jnp.where(
        row == 0, high, jnp.where(row == 1, middle, jnp.where(row == 2, low, 0.0))
    ).astype(BF)


def untail(tile):
    return jnp.sum(tile.astype(F32), axis=0, keepdims=True)


def call(body, outs, args, unread=(), scratch=(), hbm=(), vmem=12):
    specs = [pl.BlockSpec(memory_space=pltpu.SMEM)]
    specs += [
        pl.BlockSpec(memory_space=pltpu.HBM if i in hbm else pltpu.VMEM)
        for i in range(1, len(args))
    ]
    specs += [pl.BlockSpec(memory_space=pl.ANY)] * len(unread)

    def run(*refs):
        body(*refs[: len(args)], *refs[len(args) + len(unread) :])

    return pl.pallas_call(
        run,
        out_shape=[jax.ShapeDtypeStruct(*o) for o in outs],
        in_specs=specs,
        out_specs=[pl.BlockSpec(memory_space=pltpu.VMEM)] * len(outs),
        scratch_shapes=list(scratch),
        compiler_params=pltpu.CompilerParams(vmem_limit_bytes=vmem * 2**20),
        cost_estimate=pl.CostEstimate(flops=10**6, bytes_accessed=10**6, transcendentals=0),
    )(*args, *unread)


def pack_body(
    at, keys, values, queries, gates, decay, mix, keep, send, small, levels, sems
):
    core = at[0]
    mine = pl.ds(pl.multiple_of(core * 512, 512), 512)
    theirs = pl.ds(pl.multiple_of((1 - core) * 512, 512), 512)
    copies = [
        pltpu.make_async_copy(decay, small, sems.at[0]),
        pltpu.make_async_copy(mix, levels, sems.at[1]),
    ]
    for i, ref in enumerate((keys, values, queries, gates)):
        rows = pl.ds(i * 256, 256)
        for out, cols, n in ((send, theirs, 2), (keep, mine, 6)):
            copies.append(pltpu.make_async_copy(ref.at[:, cols], out.at[rows, :], sems.at[n + i]))
    for copy in copies:
        copy.start()
    for copy in copies[:2]:
        copy.wait()
    for out, low in ((keep, core == 0), (send, core == 1)):
        logs = [jnp.where(low, small[0:4], small[4:8])]
        logs += [jnp.where(low, levels[l, 0:4], levels[l, 4:8]) for l in range(8)]
        logs = jnp.concatenate(logs + [jnp.zeros((12, 256), F32)], axis=0)
        high = logs.astype(BF)
        out[LOGS : LOGS + 48, 0:256] = high
        out[LOGS : LOGS + 48, 256:512] = (logs - high.astype(F32)).astype(BF)
    for copy in copies[2:]:
        copy.wait()


def logs_of(block):
    tile = block[LOGS : LOGS + 48, :].astype(F32)
    return tile[:, 0:256] + tile[:, 256:512]


def ends_body(at, keep, got, pay, first):
    core = at[0]
    logs = jnp.concatenate([logs_of(keep)[0:4], logs_of(got)[0:4]], axis=0)
    after = (
        lax.broadcasted_iota(jnp.int32, (256, 256), 1)
        > lax.broadcasted_iota(jnp.int32, (256, 256), 0)
    ).astype(F32)
    scale = jnp.exp(exact(after, logs, NT))
    total = jnp.sum(logs, axis=1, keepdims=True)
    for h in range(4):
        cols = slice(h * 128, h * 128 + 128)
        end = []
        for i, ref in enumerate((keep, got)):
            scaled = ref[0:256, cols].astype(F32) * scale[:, 4 * i + h : 4 * i + h + 1]
            end.append(dot(scaled.astype(BF), ref[256:512, cols], TN))
        own_log, got_log = total[h : h + 1], total[4 + h : 5 + h]
        own_later = jnp.exp(jnp.where(core == 0, got_log, 0.0))
        got_later = jnp.exp(jnp.where(core == 0, 0.0, own_log))
        pay[h, 0:128, :] = (end[0] * own_later + end[1] * got_later).astype(BF)
        pay[h, 128:144, :] = tail(own_log + got_log)
        first[h, :, :] = jnp.where(core == 0, end[0], end[1]).astype(BF)


def blocks_of(got):
    s = [got[i, 0:128, :].astype(F32) for i in range(4)]
    t = [untail(got[i, 128:144, :]) for i in range(4)]
    pair = s[0] * jnp.exp(t[1]) + s[1]
    return s, t, pair


def send_whole(s, t, pair, pay):
    state = (pair * jnp.exp(t[2] + t[3]) + s[2] * jnp.exp(t[3]) + s[3]).astype(BF)
    log = tail(t[0] + t[1] + t[2] + t[3])
    for i in range(4):
        pay[i, 0:128, :] = state
        pay[i, 128:144, :] = log


def lower_states(s, t, pair, at):
    odd, upper = at % 2 == 1, at >= 2
    one = jnp.where(odd, jnp.where(upper, s[2], s[0]), 0.0)
    step = jnp.where(odd, jnp.where(upper, t[2], t[0]), 0.0)
    two = jnp.where(upper, pair * jnp.exp(step), 0.0)
    before = sum(jnp.where(at > i, t[i], 0.0) for i in range(3))
    return one, two, before


def near_body(at, near, pay, *messages):
    s, t, pair = blocks_of(near)
    send_whole(s, t, pair, pay)
    for k, message in enumerate(messages):
        one, two, before = lower_states(s, t, pair, at[1] ^ k)
        message[0:128, 0:128] = one.astype(BF)
        message[0:128, 128:256] = two.astype(BF)
        message[128:144, 0:128] = tail(before)
        message[128:144, 128:256] = jnp.zeros((16, 128), BF)


def far_body(at, far, pay, states, before_out):
    s, t, pair = blocks_of(far)
    send_whole(s, t, pair, pay)
    one, two, before = lower_states(s, t, pair, at[2])
    states[:, 0:128] = one.astype(BF)
    states[:, 128:256] = two.astype(BF)
    before_out[...] = jnp.broadcast_to(before, (8, 128))


def last_body(at, rows, before, far, message):
    one, two, _ = lower_states(*blocks_of(rows), at[3])
    earlier = jnp.exp(before[0:1, :])
    one, two = (one * earlier).astype(BF), (two * earlier).astype(BF)
    for i in range(4):
        message[i, :, 0:256] = far[...]
        message[i, :, 256:384] = one
        message[i, :, 384:512] = two


def place(s, core):
    at = core if s == 0 else 1 - core
    return at, pl.ds(pl.multiple_of(at * 256, 256), 256)


def own_body(at, keep, got, first, mixture, coef):
    core = at[0]
    rows = lax.broadcasted_iota(jnp.int32, (256, 256), 0)
    cols = lax.broadcasted_iota(jnp.int32, (256, 256), 1)
    lower = rows >= cols
    upto = lower.astype(F32)
    both = (logs_of(keep), logs_of(got))
    for s, ref in enumerate((keep, got)):
        second, here = place(s, core)
        logs = both[s]
        at_row = exact(logs[0:8], upto, NT)
        at_col = exact(upto, logs[0:8], NT)
        level = logs.T
        first_log = jnp.sum(both[1 - s][0:4], axis=1, keepdims=True)
        first_log = jnp.where(second == 1, first_log, 0.0)
        for h in range(4):
            hc = slice(h * 128, h * 128 + 128)
            q, kb, v = ref[512:768, hc], ref[0:256, hc], ref[256:512, hc]
            local = at_col[:, h : h + 1]
            gap = jnp.where(lower, local - at_row[h : h + 1, :], -1e30)
            weights = (dot(q, kb, NT) * jnp.exp(gap)).astype(BF)
            m = [level[:, 4 + 4 * l + h : 5 + 4 * l + h] for l in range(8)]
            total = dot(weights, v) * m[0]
            start = jnp.exp(local)
            total += dot(q, first[h]) * jnp.where(second == 1, start * m[1], 0.0)
            mixture[here, hc] = total
            start = start * jnp.exp(first_log[h : h + 1])
            for l in range(2, 8):
                coef[here, 6 * h + l - 2 : 6 * h + l - 1] = start * m[l]


def mix_body(at, keep, got, mixture, coef, n0, n1, n2, n3, mixed, later, near):
    for k, n in enumerate((n0, n1, n2, n3)):
        near[at[1] ^ k] = n[...]
    for h in range(4):
        before = jnp.exp(untail(near[h, 128:144, 0:128])[:, 0:1])
        hc = slice(h * 128, h * 128 + 128)
        for s, ref in enumerate((keep, got)):
            _, here = place(s, at[0])
            read = dot(ref[512:768, hc], near[h, 0:128, :])
            total = mixture[here, hc] + read[:, 0:128] * coef[here, 6 * h : 6 * h + 1]
            mixed[here, hc] = total + read[:, 128:256] * coef[here, 6 * h + 1 : 6 * h + 2]
            later[here, 4 * h : 4 * h + 4] = coef[here, 6 * h + 2 : 6 * h + 6] * before


def norm_body(at, keep, got, gain, mixture, coef, states, normed):
    core = at[0]
    for h in range(4):
        mine = pl.ds(pl.multiple_of(core * 512 + h * 128, 128), 128)
        hc = slice(h * 128, h * 128 + 128)
        for s, ref in enumerate((keep, got)):
            _, here = place(s, core)
            z = ref[768:1024, hc].astype(F32)
            total = mixture[here, hc]
            for l in range(0, 4, 2):
                read = dot(ref[512:768, hc], states[h, :, l * 128 : l * 128 + 256])
                total += read[:, 0:128] * coef[here, 4 * h + l : 4 * h + l + 1]
                total += read[:, 128:256] * coef[here, 4 * h + l + 1 : 4 * h + l + 2]
            gated = total * (z / (1.0 + jnp.exp(-z)))
            size = lax.rsqrt(jnp.mean(gated * gated, axis=1, keepdims=True) + 1e-05)
            normed[here, hc] = (gated * size * gain[:, mine].astype(F32)).astype(BF)


def project_body(other, at, b0, b1, b2, b3, w0, w1, w2, w3, out, left, right, sems):
    row = (1 - at[0]) if other else at[0]
    rows = pl.ds(pl.multiple_of(row * 256, 256), 256)
    copies = [
        pltpu.make_async_copy(w, right.at[k], sems.at[k]) for k, w in enumerate((w0, w1, w2, w3))
    ]
    for copy in copies:
        copy.start()
    for j, block in enumerate((b0, b1, b2, b3)):
        left[(at[4] + 4 - j) % 4] = block[rows, :]
    total = 0.0
    for k, turn in enumerate((0, 1, 3, 2)):
        copies[k].wait()
        total += dot(left[(at[3] + turn) % 4], right[k].reshape(1024, 512), NT)
    out[...] = total.astype(out.dtype)


def project(at, blocks, rights, other):
    return call(
        functools.partial(project_body, other),
        [((256, 1024), BF if other else F32)],
        (at, *blocks, *rights),
        scratch=[
            pltpu.VMEM((4, 256, 512), BF),
            pltpu.VMEM((4, 16, 64, 512), BF),
            pltpu.SemaphoreType.DMA((4,)),
        ],
        hbm=range(5, 9),
        vmem=20,
    )[0]


def shift(value, axis, by):
    return lax.ppermute(value, axis, [(i, (i + by) % 4) for i in range(4)])


def shards(values, keys, queries, gates, log_decay, level_mix, norm_gain, weight):
    y, a, b, c, x = (lax.axis_index(n) for n in ("y", "a", NEAR, "c", "x"))
    at = jnp.stack([c, b, a, y, x]).astype(jnp.int32)
    turned = []
    for other in range(2):
        half = lax.dynamic_slice_in_dim(weight, (c ^ other) * 512, 512, 1)
        perm = [
            ((s * 2 + k) * 4 + f, (f * 2 + (k ^ other)) * 4 + s)
            for s in range(4)
            for f in range(4)
            for k in range(2)
        ]
        turned.append(lax.ppermute(half, ("y", "c", "x"), perm))
    block = ((ROWS, 512), BF)
    keep, send = call(
        pack_body,
        [block, block],
        (at, keys, values, queries, gates, log_decay, level_mix),
        scratch=[
            pltpu.VMEM((8, 256), F32),
            pltpu.VMEM((8, 8, 256), F32),
            pltpu.SemaphoreType.DMA((10,)),
        ],
        hbm=range(1, 7),
        vmem=60,
    )
    turned, send = lax.optimization_barrier((turned, send))
    mine = jnp.where(c == 0, jnp.concatenate(turned), jnp.concatenate(turned[::-1]))
    gathered = lax.all_gather(mine, ("a", "p", "q"))

    got = swap(send)
    pay = ((4, 144, 128), BF)
    pay_b, first = call(ends_body, [pay, ((4, 128, 128), BF)], (at, keep, got))
    near = lax.all_to_all(pay_b, NEAR, 0, 0, tiled=True)
    pay_a, *near = call(near_body, [pay] + [((144, 256), BF)] * 4, (at, near))
    far = lax.all_to_all(pay_a, "a", 0, 0, tiled=True)
    near = near[:1] + [
        lax.ppermute(near[k], NEAR, [(i, i ^ k) for i in range(4)]) for k in (1, 2, 3)
    ]
    mixture, coef = call(
        own_body, [((512, 512), F32), ((512, 24), F32)], (at, keep, got, first)
    )
    pay_y, far, before = call(
        far_body,
        [pay, ((128, 256), BF), ((8, 128), F32)],
        (at, far),
        unread=near[1:],
    )
    rows = lax.all_to_all(pay_y, "y", 0, 0, tiled=True)
    (states,) = call(last_body, [((4, 128, 512), BF)], (at, rows, before, far))
    states = lax.all_to_all(states, NEAR, 0, 0, tiled=True)
    mixture, coef = call(
        mix_body,
        [((512, 512), F32), ((512, 16), F32)],
        (at, keep, got, mixture, coef, *near),
        scratch=[pltpu.VMEM((4, 144, 256), BF)],
    )
    _, gathered = lax.optimization_barrier((coef, gathered))
    rights = [gathered] + [shift(gathered, "y", 4 - k) for k in (1, 3)]
    (normed,) = call(
        norm_body, [((512, 512), BF)], (at, keep, got, norm_gain[None], mixture, coef, states)
    )

    _, gathered = lax.optimization_barrier((normed, gathered))
    rights.append(shift(gathered, "y", 2))
    blocks = [normed] + [shift(normed, "x", j) for j in (1, 2, 3)]
    theirs = swap(project(at, blocks, rights, True))
    own = project(at, blocks, rights, False)
    return (own + theirs.astype(F32)).astype(BF)


def solution(mesh):
    fine = Mesh(mesh.devices.reshape(4, 4, 2, 2, 2, 4), SEQ + ("x",))
    return jax.shard_map(
        shards,
        mesh=fine,
        in_specs=(
            P(SEQ, "x"),
            P(SEQ, "x"),
            P(SEQ, "x"),
            P(SEQ, "x"),
            P("x", SEQ),
            P(None, "x", SEQ),
            P("x"),
            P(SEQ, "x"),
        ),
        out_specs=P(SEQ, "x"),
        check_vma=False,
    )
```

```python
import functools

import jax
import jax.numpy as jnp
from jax import lax
from jax.experimental import pallas as pl
from jax.experimental.pallas import tpu as pltpu
from jax.sharding import Mesh, PartitionSpec as P

BF = jnp.bfloat16
F32 = jnp.float32
SEQ = ("y", "a", "p", "q", "c")
NEAR = ("p", "q")
NT = (((1,), (1,)), ((), ()))
TN = (((0,), (0,)), ((), ()))
LOGS = 1024
ROWS = 1072


def swap(value):
    return lax.ppermute(value, "c", [(0, 1), (1, 0)])


def dot(left, right, dims=(((1,), (0,)), ((), ()))):
    return lax.dot_general(left, right, dims, preferred_element_type=F32)


def exact(left, right, dims):
    return lax.dot_general(
        left, right, dims, precision=lax.Precision.HIGHEST, preferred_element_type=F32
    )


def tail(log):
    high = log.astype(BF).astype(F32)
    middle = (log - high).astype(BF).astype(F32)
    low = log - high - middle
    row = lax.broadcasted_iota(jnp.int32, (16, 128), 0)
    return jnp.where(
        row == 0, high, jnp.where(row == 1, middle, jnp.where(row == 2, low, 0.0))
    ).astype(BF)


def untail(tile):
    return jnp.sum(tile.astype(F32), axis=0, keepdims=True)


def call(body, outs, args, unread=(), scratch=(), hbm=(), vmem=12):
    specs = [pl.BlockSpec(memory_space=pltpu.SMEM)]
    specs += [
        pl.BlockSpec(memory_space=pltpu.HBM if i in hbm else pltpu.VMEM)
        for i in range(1, len(args))
    ]
    specs += [pl.BlockSpec(memory_space=pl.ANY)] * len(unread)

    def run(*refs):
        body(*refs[: len(args)], *refs[len(args) + len(unread) :])

    return pl.pallas_call(
        run,
        out_shape=[jax.ShapeDtypeStruct(*o) for o in outs],
        in_specs=specs,
        out_specs=[pl.BlockSpec(memory_space=pltpu.VMEM)] * len(outs),
        scratch_shapes=list(scratch),
        compiler_params=pltpu.CompilerParams(vmem_limit_bytes=vmem * 2**20),
        cost_estimate=pl.CostEstimate(flops=10**6, bytes_accessed=10**6, transcendentals=0),
    )(*args, *unread)


def pack_body(
    at, keys, values, queries, gates, decay, mix, keep, send, small, levels, sems
):
    core = at[0]
    mine = pl.ds(pl.multiple_of(core * 512, 512), 512)
    theirs = pl.ds(pl.multiple_of((1 - core) * 512, 512), 512)
    copies = [
        pltpu.make_async_copy(decay, small, sems.at[0]),
        pltpu.make_async_copy(mix, levels, sems.at[1]),
    ]
    for i, ref in enumerate((keys, values, queries, gates)):
        rows = pl.ds(i * 256, 256)
        for out, cols, n in ((send, theirs, 2), (keep, mine, 6)):
            copies.append(pltpu.make_async_copy(ref.at[:, cols], out.at[rows, :], sems.at[n + i]))
    for copy in copies:
        copy.start()
    for copy in copies[:2]:
        copy.wait()
    for out, low in ((keep, core == 0), (send, core == 1)):
        logs = [jnp.where(low, small[0:4], small[4:8])]
        logs += [jnp.where(low, levels[l, 0:4], levels[l, 4:8]) for l in range(8)]
        logs = jnp.concatenate(logs + [jnp.zeros((12, 256), F32)], axis=0)
        high = logs.astype(BF)
        out[LOGS : LOGS + 48, 0:256] = high
        out[LOGS : LOGS + 48, 256:512] = (logs - high.astype(F32)).astype(BF)
    for copy in copies[2:]:
        copy.wait()


def logs_of(block):
    tile = block[LOGS : LOGS + 48, :].astype(F32)
    return tile[:, 0:256] + tile[:, 256:512]


def ends_body(at, keep, got, pay, first):
    core = at[0]
    logs = jnp.concatenate([logs_of(keep)[0:4], logs_of(got)[0:4]], axis=0)
    after = (
        lax.broadcasted_iota(jnp.int32, (256, 256), 1)
        > lax.broadcasted_iota(jnp.int32, (256, 256), 0)
    ).astype(F32)
    scale = jnp.exp(exact(after, logs, NT))
    total = jnp.sum(logs, axis=1, keepdims=True)
    for h in range(4):
        cols = slice(h * 128, h * 128 + 128)
        end = []
        for i, ref in enumerate((keep, got)):
            scaled = ref[0:256, cols].astype(F32) * scale[:, 4 * i + h : 4 * i + h + 1]
            end.append(dot(scaled.astype(BF), ref[256:512, cols], TN))
        own_log, got_log = total[h : h + 1], total[4 + h : 5 + h]
        own_later = jnp.exp(jnp.where(core == 0, got_log, 0.0))
        got_later = jnp.exp(jnp.where(core == 0, 0.0, own_log))
        pay[h, 0:128, :] = (end[0] * own_later + end[1] * got_later).astype(BF)
        pay[h, 128:144, :] = tail(own_log + got_log)
        first[h, :, :] = jnp.where(core == 0, end[0], end[1]).astype(BF)


def blocks_of(got):
    s = [got[i, 0:128, :].astype(F32) for i in range(4)]
    t = [untail(got[i, 128:144, :]) for i in range(4)]
    pair = s[0] * jnp.exp(t[1]) + s[1]
    return s, t, pair


def send_whole(s, t, pair, pay):
    state = (pair * jnp.exp(t[2] + t[3]) + s[2] * jnp.exp(t[3]) + s[3]).astype(BF)
    log = tail(t[0] + t[1] + t[2] + t[3])
    for i in range(4):
        pay[i, 0:128, :] = state
        pay[i, 128:144, :] = log


def lower_states(s, t, pair, at):
    odd, upper = at % 2 == 1, at >= 2
    one = jnp.where(odd, jnp.where(upper, s[2], s[0]), 0.0)
    step = jnp.where(odd, jnp.where(upper, t[2], t[0]), 0.0)
    two = jnp.where(upper, pair * jnp.exp(step), 0.0)
    before = sum(jnp.where(at > i, t[i], 0.0) for i in range(3))
    return one, two, before


def near_body(at, near, pay, *messages):
    s, t, pair = blocks_of(near)
    send_whole(s, t, pair, pay)
    for k, message in enumerate(messages):
        one, two, before = lower_states(s, t, pair, at[1] ^ k)
        message[0:128, 0:128] = one.astype(BF)
        message[0:128, 128:256] = two.astype(BF)
        message[128:144, 0:128] = tail(before)
        message[128:144, 128:256] = jnp.zeros((16, 128), BF)


def far_body(at, far, pay, states, before_out):
    s, t, pair = blocks_of(far)
    send_whole(s, t, pair, pay)
    one, two, before = lower_states(s, t, pair, at[2])
    states[:, 0:128] = one.astype(BF)
    states[:, 128:256] = two.astype(BF)
    before_out[...] = jnp.broadcast_to(before, (8, 128))


def last_body(at, rows, before, far, message):
    one, two, _ = lower_states(*blocks_of(rows), at[3])
    earlier = jnp.exp(before[0:1, :])
    one, two = (one * earlier).astype(BF), (two * earlier).astype(BF)
    for i in range(4):
        message[i, :, 0:256] = far[...]
        message[i, :, 256:384] = one
        message[i, :, 384:512] = two


def place(s, core):
    at = core if s == 0 else 1 - core
    return at, pl.ds(pl.multiple_of(at * 256, 256), 256)


def own_body(at, keep, got, first, mixture, coef):
    core = at[0]
    rows = lax.broadcasted_iota(jnp.int32, (256, 256), 0)
    cols = lax.broadcasted_iota(jnp.int32, (256, 256), 1)
    lower = rows >= cols
    upto = lower.astype(F32)
    both = (logs_of(keep), logs_of(got))
    for s, ref in enumerate((keep, got)):
        second, here = place(s, core)
        logs = both[s]
        at_row = exact(logs[0:8], upto, NT)
        at_col = exact(upto, logs[0:8], NT)
        level = logs.T
        first_log = jnp.sum(both[1 - s][0:4], axis=1, keepdims=True)
        first_log = jnp.where(second == 1, first_log, 0.0)
        for h in range(4):
            hc = slice(h * 128, h * 128 + 128)
            q, kb, v = ref[512:768, hc], ref[0:256, hc], ref[256:512, hc]
            local = at_col[:, h : h + 1]
            gap = jnp.where(lower, local - at_row[h : h + 1, :], -1e30)
            weights = (dot(q, kb, NT) * jnp.exp(gap)).astype(BF)
            m = [level[:, 4 + 4 * l + h : 5 + 4 * l + h] for l in range(8)]
            total = dot(weights, v) * m[0]
            start = jnp.exp(local)
            total += dot(q, first[h]) * jnp.where(second == 1, start * m[1], 0.0)
            mixture[here, hc] = total
            start = start * jnp.exp(first_log[h : h + 1])
            for l in range(2, 8):
                coef[here, 6 * h + l - 2 : 6 * h + l - 1] = start * m[l]


def mix_body(at, keep, got, mixture, coef, n0, n1, n2, n3, mixed, later, near):
    for k, n in enumerate((n0, n1, n2, n3)):
        near[at[1] ^ k] = n[...]
    for h in range(4):
        before = jnp.exp(untail(near[h, 128:144, 0:128])[:, 0:1])
        hc = slice(h * 128, h * 128 + 128)
        for s, ref in enumerate((keep, got)):
            _, here = place(s, at[0])
            read = dot(ref[512:768, hc], near[h, 0:128, :])
            total = mixture[here, hc] + read[:, 0:128] * coef[here, 6 * h : 6 * h + 1]
            mixed[here, hc] = total + read[:, 128:256] * coef[here, 6 * h + 1 : 6 * h + 2]
            later[here, 4 * h : 4 * h + 4] = coef[here, 6 * h + 2 : 6 * h + 6] * before


def norm_body(at, keep, got, gain, mixture, coef, states, normed):
    core = at[0]
    for h in range(4):
        mine = pl.ds(pl.multiple_of(core * 512 + h * 128, 128), 128)
        hc = slice(h * 128, h * 128 + 128)
        for s, ref in enumerate((keep, got)):
            _, here = place(s, core)
            z = ref[768:1024, hc].astype(F32)
            total = mixture[here, hc]
            for l in range(0, 4, 2):
                read = dot(ref[512:768, hc], states[h, :, l * 128 : l * 128 + 256])
                total += read[:, 0:128] * coef[here, 4 * h + l : 4 * h + l + 1]
                total += read[:, 128:256] * coef[here, 4 * h + l + 1 : 4 * h + l + 2]
            gated = total * (z / (1.0 + jnp.exp(-z)))
            size = lax.rsqrt(jnp.mean(gated * gated, axis=1, keepdims=True) + 1e-05)
            normed[here, hc] = (gated * size * gain[:, mine].astype(F32)).astype(BF)


def project_body(other, at, b0, b1, b2, b3, w0, w1, w2, w3, out, left, right, sems):
    row = (1 - at[0]) if other else at[0]
    rows = pl.ds(pl.multiple_of(row * 256, 256), 256)
    copies = []
    for j, block in enumerate((b0, b1, b2, b3)):
        spot = (at[4] + 4 - j) % 4
        copies.append(pltpu.make_async_copy(block.at[rows], left.at[spot], sems.at[0, j]))
    for k, w in enumerate((w0, w1, w2, w3)):
        copies.append(pltpu.make_async_copy(w, right.at[k], sems.at[1, k]))
    for copy in copies:
        copy.start()
    for copy in copies[:4]:
        copy.wait()
    total = 0.0
    for k, turn in enumerate((0, 1, 3, 2)):
        copies[4 + k].wait()
        total += dot(left[(at[3] + turn) % 4], right[k].reshape(1024, 512), NT)
    out[...] = total.astype(out.dtype)


def project(at, blocks, rights, other):
    return call(
        functools.partial(project_body, other),
        [((256, 1024), BF if other else F32)],
        (at, *blocks, *rights),
        scratch=[
            pltpu.VMEM((4, 256, 512), BF),
            pltpu.VMEM((4, 16, 64, 512), BF),
            pltpu.SemaphoreType.DMA((2, 4)),
        ],
        hbm=range(1, 9),
        vmem=20,
    )[0]


def shift(value, axis, by):
    return lax.ppermute(value, axis, [(i, (i + by) % 4) for i in range(4)])


def shards(values, keys, queries, gates, log_decay, level_mix, norm_gain, weight):
    y, a, b, c, x = (lax.axis_index(n) for n in ("y", "a", NEAR, "c", "x"))
    at = jnp.stack([c, b, a, y, x]).astype(jnp.int32)
    turned = []
    for other in range(2):
        half = lax.dynamic_slice_in_dim(weight, (c ^ other) * 512, 512, 1)
        perm = [
            ((s * 2 + k) * 4 + f, (f * 2 + (k ^ other)) * 4 + s)
            for s in range(4)
            for f in range(4)
            for k in range(2)
        ]
        turned.append(lax.ppermute(half, ("y", "c", "x"), perm))
    mine = jnp.where(c == 0, jnp.concatenate(turned), jnp.concatenate(turned[::-1]))
    block = ((ROWS, 512), BF)
    keep, send = call(
        pack_body,
        [block, block],
        (at, keys, values, queries, gates, log_decay, level_mix),
        scratch=[
            pltpu.VMEM((8, 256), F32),
            pltpu.VMEM((8, 8, 256), F32),
            pltpu.SemaphoreType.DMA((10,)),
        ],
        hbm=range(1, 7),
        vmem=60,
    )
    mine, send = lax.optimization_barrier((mine, send))
    gathered = lax.all_gather(mine, ("a", "p", "q"))

    got = swap(send)
    pay = ((4, 144, 128), BF)
    pay_b, first = call(ends_body, [pay, ((4, 128, 128), BF)], (at, keep, got))
    near = lax.all_to_all(pay_b, NEAR, 0, 0, tiled=True)
    pay_a, *near = call(near_body, [pay] + [((144, 256), BF)] * 4, (at, near))
    far = lax.all_to_all(pay_a, "a", 0, 0, tiled=True)
    near = near[:1] + [
        lax.ppermute(near[k], NEAR, [(i, i ^ k) for i in range(4)]) for k in (1, 2, 3)
    ]
    mixture, coef = call(
        own_body, [((512, 512), F32), ((512, 24), F32)], (at, keep, got, first)
    )
    pay_y, far, before = call(
        far_body,
        [pay, ((128, 256), BF), ((8, 128), F32)],
        (at, far),
        unread=near[1:],
    )
    rows = lax.all_to_all(pay_y, "y", 0, 0, tiled=True)
    (states,) = call(last_body, [((4, 128, 512), BF)], (at, rows, before, far))
    states = lax.all_to_all(states, NEAR, 0, 0, tiled=True)
    mixture, coef = call(
        mix_body,
        [((512, 512), F32), ((512, 16), F32)],
        (at, keep, got, mixture, coef, *near),
        scratch=[pltpu.VMEM((4, 144, 256), BF)],
    )
    _, gathered = lax.optimization_barrier((coef, gathered))
    rights = [gathered] + [shift(gathered, "y", 4 - k) for k in (1, 3, 2)]
    (normed,) = call(
        norm_body, [((512, 512), BF)], (at, keep, got, norm_gain[None], mixture, coef, states)
    )

    blocks = [normed] + [shift(normed, "x", j) for j in (1, 2, 3)]
    theirs = swap(project(at, blocks, rights, True))
    own = project(at, blocks, rights, False)
    return (own + theirs.astype(F32)).astype(BF)


def solution(mesh):
    fine = Mesh(mesh.devices.reshape(4, 4, 2, 2, 2, 4), SEQ + ("x",))
    return jax.shard_map(
        shards,
        mesh=fine,
        in_specs=(
            P(SEQ, "x"),
            P(SEQ, "x"),
            P(SEQ, "x"),
            P(SEQ, "x"),
            P("x", SEQ),
            P(None, "x", SEQ),
            P("x"),
            P(SEQ, "x"),
        ),
        out_specs=P(SEQ, "x"),
        check_vma=False,
    )
```

```python
import functools

import jax
import jax.numpy as jnp
from jax import lax
from jax.experimental import pallas as pl
from jax.experimental.pallas import tpu as pltpu
from jax.sharding import Mesh, PartitionSpec as P

BF = jnp.bfloat16
F32 = jnp.float32
SEQ = ("y", "a", "p", "q", "c")
NEAR = ("p", "q")
NT = (((1,), (1,)), ((), ()))
TN = (((0,), (0,)), ((), ()))
LOGS = 1024
ROWS = 1072


def swap(value):
    return lax.ppermute(value, "c", [(0, 1), (1, 0)])


def dot(left, right, dims=(((1,), (0,)), ((), ()))):
    return lax.dot_general(left, right, dims, preferred_element_type=F32)


def exact(left, right, dims):
    return lax.dot_general(
        left, right, dims, precision=lax.Precision.HIGHEST, preferred_element_type=F32
    )


def tail(log):
    high = log.astype(BF).astype(F32)
    middle = (log - high).astype(BF).astype(F32)
    low = log - high - middle
    row = lax.broadcasted_iota(jnp.int32, (16, 128), 0)
    return jnp.where(
        row == 0, high, jnp.where(row == 1, middle, jnp.where(row == 2, low, 0.0))
    ).astype(BF)


def untail(tile):
    return jnp.sum(tile.astype(F32), axis=0, keepdims=True)


def call(body, outs, args, unread=(), scratch=(), hbm=(), vmem=12):
    specs = [pl.BlockSpec(memory_space=pltpu.SMEM)]
    specs += [
        pl.BlockSpec(memory_space=pltpu.HBM if i in hbm else pltpu.VMEM)
        for i in range(1, len(args))
    ]
    specs += [pl.BlockSpec(memory_space=pl.ANY)] * len(unread)

    def run(*refs):
        body(*refs[: len(args)], *refs[len(args) + len(unread) :])

    return pl.pallas_call(
        run,
        out_shape=[jax.ShapeDtypeStruct(*o) for o in outs],
        in_specs=specs,
        out_specs=[pl.BlockSpec(memory_space=pltpu.VMEM)] * len(outs),
        scratch_shapes=list(scratch),
        compiler_params=pltpu.CompilerParams(vmem_limit_bytes=vmem * 2**20),
        cost_estimate=pl.CostEstimate(flops=10**6, bytes_accessed=10**6, transcendentals=0),
    )(*args, *unread)


def pack_body(
    at, keys, values, queries, gates, decay, mix, keep, send, small, levels, sems
):
    core = at[0]
    mine = pl.ds(pl.multiple_of(core * 512, 512), 512)
    theirs = pl.ds(pl.multiple_of((1 - core) * 512, 512), 512)
    copies = [
        pltpu.make_async_copy(decay, small, sems.at[0]),
        pltpu.make_async_copy(mix, levels, sems.at[1]),
    ]
    for i, ref in enumerate((keys, values, queries, gates)):
        rows = pl.ds(i * 256, 256)
        for out, cols, n in ((send, theirs, 2), (keep, mine, 6)):
            copies.append(pltpu.make_async_copy(ref.at[:, cols], out.at[rows, :], sems.at[n + i]))
    for copy in copies:
        copy.start()
    for copy in copies[:2]:
        copy.wait()
    for out, low in ((keep, core == 0), (send, core == 1)):
        logs = [jnp.where(low, small[0:4], small[4:8])]
        logs += [jnp.where(low, levels[l, 0:4], levels[l, 4:8]) for l in range(8)]
        logs = jnp.concatenate(logs + [jnp.zeros((12, 256), F32)], axis=0)
        high = logs.astype(BF)
        out[LOGS : LOGS + 48, 0:256] = high
        out[LOGS : LOGS + 48, 256:512] = (logs - high.astype(F32)).astype(BF)
    for copy in copies[2:]:
        copy.wait()


def logs_of(block):
    tile = block[LOGS : LOGS + 48, :].astype(F32)
    return tile[:, 0:256] + tile[:, 256:512]


def ends_body(at, keep, got, pay, first):
    core = at[0]
    logs = jnp.concatenate([logs_of(keep)[0:4], logs_of(got)[0:4]], axis=0)
    after = (
        lax.broadcasted_iota(jnp.int32, (256, 256), 1)
        > lax.broadcasted_iota(jnp.int32, (256, 256), 0)
    ).astype(F32)
    scale = jnp.exp(exact(after, logs, NT))
    total = jnp.sum(logs, axis=1, keepdims=True)
    for h in range(4):
        cols = slice(h * 128, h * 128 + 128)
        end = []
        for i, ref in enumerate((keep, got)):
            scaled = ref[0:256, cols].astype(F32) * scale[:, 4 * i + h : 4 * i + h + 1]
            end.append(dot(scaled.astype(BF), ref[256:512, cols], TN))
        own_log, got_log = total[h : h + 1], total[4 + h : 5 + h]
        own_later = jnp.exp(jnp.where(core == 0, got_log, 0.0))
        got_later = jnp.exp(jnp.where(core == 0, 0.0, own_log))
        pay[h, 0:128, :] = (end[0] * own_later + end[1] * got_later).astype(BF)
        pay[h, 128:144, :] = tail(own_log + got_log)
        first[h, :, :] = jnp.where(core == 0, end[0], end[1]).astype(BF)


def blocks_of(got):
    s = [got[i, 0:128, :].astype(F32) for i in range(4)]
    t = [untail(got[i, 128:144, :]) for i in range(4)]
    pair = s[0] * jnp.exp(t[1]) + s[1]
    return s, t, pair


def send_whole(s, t, pair, pay):
    state = (pair * jnp.exp(t[2] + t[3]) + s[2] * jnp.exp(t[3]) + s[3]).astype(BF)
    log = tail(t[0] + t[1] + t[2] + t[3])
    for i in range(4):
        pay[i, 0:128, :] = state
        pay[i, 128:144, :] = log


def lower_states(s, t, pair, at):
    odd, upper = at % 2 == 1, at >= 2
    one = jnp.where(odd, jnp.where(upper, s[2], s[0]), 0.0)
    step = jnp.where(odd, jnp.where(upper, t[2], t[0]), 0.0)
    two = jnp.where(upper, pair * jnp.exp(step), 0.0)
    before = sum(jnp.where(at > i, t[i], 0.0) for i in range(3))
    return one, two, before


def near_body(at, near, pay, *messages):
    s, t, pair = blocks_of(near)
    send_whole(s, t, pair, pay)
    for k, message in enumerate(messages):
        one, two, before = lower_states(s, t, pair, at[1] ^ k)
        message[0:128, 0:128] = one.astype(BF)
        message[0:128, 128:256] = two.astype(BF)
        message[128:144, 0:128] = tail(before)
        message[128:144, 128:256] = jnp.zeros((16, 128), BF)


def far_body(at, far, pay, states, before_out):
    s, t, pair = blocks_of(far)
    send_whole(s, t, pair, pay)
    one, two, before = lower_states(s, t, pair, at[2])
    states[:, 0:128] = one.astype(BF)
    states[:, 128:256] = two.astype(BF)
    before_out[...] = jnp.broadcast_to(before, (8, 128))


def last_body(at, rows, before, far, message):
    one, two, _ = lower_states(*blocks_of(rows), at[3])
    earlier = jnp.exp(before[0:1, :])
    one, two = (one * earlier).astype(BF), (two * earlier).astype(BF)
    for i in range(4):
        message[i, :, 0:256] = far[...]
        message[i, :, 256:384] = one
        message[i, :, 384:512] = two


def place(s, core):
    at = core if s == 0 else 1 - core
    return at, pl.ds(pl.multiple_of(at * 256, 256), 256)


def own_body(at, keep, got, first, mixture, coef):
    core = at[0]
    rows = lax.broadcasted_iota(jnp.int32, (256, 256), 0)
    cols = lax.broadcasted_iota(jnp.int32, (256, 256), 1)
    lower = rows >= cols
    upto = lower.astype(F32)
    both = (logs_of(keep), logs_of(got))
    for s, ref in enumerate((keep, got)):
        second, here = place(s, core)
        logs = both[s]
        at_row = exact(logs[0:8], upto, NT)
        at_col = exact(upto, logs[0:8], NT)
        level = logs.T
        first_log = jnp.sum(both[1 - s][0:4], axis=1, keepdims=True)
        first_log = jnp.where(second == 1, first_log, 0.0)
        for h in range(4):
            hc = slice(h * 128, h * 128 + 128)
            q, kb, v = ref[512:768, hc], ref[0:256, hc], ref[256:512, hc]
            local = at_col[:, h : h + 1]
            gap = jnp.where(lower, local - at_row[h : h + 1, :], -1e30)
            weights = (dot(q, kb, NT) * jnp.exp(gap)).astype(BF)
            m = [level[:, 4 + 4 * l + h : 5 + 4 * l + h] for l in range(8)]
            total = dot(weights, v) * m[0]
            start = jnp.exp(local)
            total += dot(q, first[h]) * jnp.where(second == 1, start * m[1], 0.0)
            mixture[here, hc] = total
            start = start * jnp.exp(first_log[h : h + 1])
            for l in range(2, 8):
                coef[here, 6 * h + l - 2 : 6 * h + l - 1] = start * m[l]


def mix_body(at, keep, got, mixture, coef, n0, n1, n2, n3, mixed, later, near):
    for k, n in enumerate((n0, n1, n2, n3)):
        near[at[1] ^ k] = n[...]
    for h in range(4):
        before = jnp.exp(untail(near[h, 128:144, 0:128])[:, 0:1])
        hc = slice(h * 128, h * 128 + 128)
        for s, ref in enumerate((keep, got)):
            _, here = place(s, at[0])
            read = dot(ref[512:768, hc], near[h, 0:128, :])
            total = mixture[here, hc] + read[:, 0:128] * coef[here, 6 * h : 6 * h + 1]
            mixed[here, hc] = total + read[:, 128:256] * coef[here, 6 * h + 1 : 6 * h + 2]
            later[here, 4 * h : 4 * h + 4] = coef[here, 6 * h + 2 : 6 * h + 6] * before


def norm_body(at, keep, got, gain, mixture, coef, states, normed):
    core = at[0]
    for h in range(4):
        mine = pl.ds(pl.multiple_of(core * 512 + h * 128, 128), 128)
        hc = slice(h * 128, h * 128 + 128)
        for s, ref in enumerate((keep, got)):
            _, here = place(s, core)
            z = ref[768:1024, hc].astype(F32)
            total = mixture[here, hc]
            for l in range(0, 4, 2):
                read = dot(ref[512:768, hc], states[h, :, l * 128 : l * 128 + 256])
                total += read[:, 0:128] * coef[here, 4 * h + l : 4 * h + l + 1]
                total += read[:, 128:256] * coef[here, 4 * h + l + 1 : 4 * h + l + 2]
            gated = total * (z / (1.0 + jnp.exp(-z)))
            size = lax.rsqrt(jnp.mean(gated * gated, axis=1, keepdims=True) + 1e-05)
            normed[here, hc] = (gated * size * gain[:, mine].astype(F32)).astype(BF)


def project_body(other, at, b0, b1, b2, b3, w0, w1, w2, w3, out, left, right, sems):
    row = (1 - at[0]) if other else at[0]
    rows = pl.ds(pl.multiple_of(row * 256, 256), 256)
    copies = []
    for j, block in enumerate((b0, b1, b2, b3)):
        spot = (at[4] + 4 - j) % 4
        copies.append(pltpu.make_async_copy(block.at[rows], left.at[spot], sems.at[0, j]))
    for k, w in enumerate((w0, w1, w2, w3)):
        copies.append(pltpu.make_async_copy(w, right.at[k], sems.at[1, k]))
    for copy in copies:
        copy.start()
    for copy in copies[:4]:
        copy.wait()
    total = 0.0
    for k, turn in enumerate((0, 1, 3, 2)):
        copies[4 + k].wait()
        total += dot(left[(at[3] + turn) % 4], right[k].reshape(1024, 512), NT)
    out[...] = total.astype(out.dtype)


def project(at, blocks, rights, other):
    return call(
        functools.partial(project_body, other),
        [((256, 1024), BF if other else F32)],
        (at, *blocks, *rights),
        scratch=[
            pltpu.VMEM((4, 256, 512), BF),
            pltpu.VMEM((4, 16, 64, 512), BF),
            pltpu.SemaphoreType.DMA((2, 4)),
        ],
        hbm=range(1, 9),
        vmem=20,
    )[0]


def shift(value, axis, by):
    return lax.ppermute(value, axis, [(i, (i + by) % 4) for i in range(4)])


def shards(values, keys, queries, gates, log_decay, level_mix, norm_gain, weight):
    y, a, b, q, c, x = (lax.axis_index(n) for n in ("y", "a", NEAR, "q", "c", "x"))
    at = jnp.stack([c, b, a, y, x]).astype(jnp.int32)
    turned = []
    for other in range(2):
        half = lax.dynamic_slice_in_dim(weight, (c ^ other) * 512, 512, 1)
        perm = [
            ((s * 2 + k) * 4 + f, (f * 2 + (k ^ other)) * 4 + s)
            for s in range(4)
            for f in range(4)
            for k in range(2)
        ]
        turned.append(lax.ppermute(half, ("y", "c", "x"), perm))
    mine = jnp.where(c == 0, jnp.concatenate(turned), jnp.concatenate(turned[::-1]))
    block = ((ROWS, 512), BF)
    keep, send = call(
        pack_body,
        [block, block],
        (at, keys, values, queries, gates, log_decay, level_mix),
        scratch=[
            pltpu.VMEM((8, 256), F32),
            pltpu.VMEM((8, 8, 256), F32),
            pltpu.SemaphoreType.DMA((10,)),
        ],
        hbm=range(1, 7),
        vmem=60,
    )
    mine, send = lax.optimization_barrier((mine, send))
    theirs = lax.ppermute(mine, "q", [(0, 1), (1, 0)])

    got = swap(send)
    pay = ((4, 144, 128), BF)
    pay_b, first = call(ends_body, [pay, ((4, 128, 128), BF)], (at, keep, got))
    theirs, pay_b = lax.optimization_barrier((theirs, pay_b))
    mine = jnp.stack([jnp.where(q == 0, mine, theirs), jnp.where(q == 0, theirs, mine)])
    gathered = lax.all_gather(mine, ("a", "p"), axis=0, tiled=True)

    near = lax.all_to_all(pay_b, NEAR, 0, 0, tiled=True)
    pay_a, *near = call(near_body, [pay] + [((144, 256), BF)] * 4, (at, near))
    far = lax.all_to_all(pay_a, "a", 0, 0, tiled=True)
    near = near[:1] + [
        lax.ppermute(near[k], NEAR, [(i, i ^ k) for i in range(4)]) for k in (1, 2, 3)
    ]
    mixture, coef = call(
        own_body, [((512, 512), F32), ((512, 24), F32)], (at, keep, got, first)
    )
    pay_y, far, before = call(
        far_body,
        [pay, ((128, 256), BF), ((8, 128), F32)],
        (at, far),
        unread=near[1:],
    )
    rows = lax.all_to_all(pay_y, "y", 0, 0, tiled=True)
    (states,) = call(last_body, [((4, 128, 512), BF)], (at, rows, before, far))
    states = lax.all_to_all(states, NEAR, 0, 0, tiled=True)
    mixture, coef = call(
        mix_body,
        [((512, 512), F32), ((512, 16), F32)],
        (at, keep, got, mixture, coef, *near),
        scratch=[pltpu.VMEM((4, 144, 256), BF)],
    )
    _, gathered = lax.optimization_barrier((coef, gathered))
    rights = [gathered] + [shift(gathered, "y", 4 - k) for k in (1, 3, 2)]
    (normed,) = call(
        norm_body, [((512, 512), BF)], (at, keep, got, norm_gain[None], mixture, coef, states)
    )

    blocks = [normed] + [shift(normed, "x", j) for j in (1, 2, 3)]
    theirs = swap(project(at, blocks, rights, True))
    own = project(at, blocks, rights, False)
    return (own + theirs.astype(F32)).astype(BF)


def solution(mesh):
    fine = Mesh(mesh.devices.reshape(4, 4, 2, 2, 2, 4), SEQ + ("x",))
    return jax.shard_map(
        shards,
        mesh=fine,
        in_specs=(
            P(SEQ, "x"),
            P(SEQ, "x"),
            P(SEQ, "x"),
            P(SEQ, "x"),
            P("x", SEQ),
            P(None, "x", SEQ),
            P("x"),
            P(SEQ, "x"),
        ),
        out_specs=P(SEQ, "x"),
        check_vma=False,
    )
```

```python
import functools

import jax
import jax.numpy as jnp
from jax import lax
from jax.experimental import pallas as pl
from jax.experimental.pallas import tpu as pltpu
from jax.sharding import Mesh, PartitionSpec as P

BF = jnp.bfloat16
F32 = jnp.float32
SEQ = ("y", "a", "p", "q", "c")
NEAR = ("p", "q")
NT = (((1,), (1,)), ((), ()))
TN = (((0,), (0,)), ((), ()))
LOGS = 1024
ROWS = 1072


def swap(value):
    return lax.ppermute(value, "c", [(0, 1), (1, 0)])


def dot(left, right, dims=(((1,), (0,)), ((), ()))):
    return lax.dot_general(left, right, dims, preferred_element_type=F32)


def exact(left, right, dims):
    return lax.dot_general(
        left, right, dims, precision=lax.Precision.HIGHEST, preferred_element_type=F32
    )


def tail(log):
    high = log.astype(BF).astype(F32)
    middle = (log - high).astype(BF).astype(F32)
    low = log - high - middle
    row = lax.broadcasted_iota(jnp.int32, (16, 128), 0)
    return jnp.where(
        row == 0, high, jnp.where(row == 1, middle, jnp.where(row == 2, low, 0.0))
    ).astype(BF)


def untail(tile):
    return jnp.sum(tile.astype(F32), axis=0, keepdims=True)


def call(body, outs, args, unread=(), scratch=(), hbm=(), vmem=12):
    specs = [pl.BlockSpec(memory_space=pltpu.SMEM)]
    specs += [
        pl.BlockSpec(memory_space=pltpu.HBM if i in hbm else pltpu.VMEM)
        for i in range(1, len(args))
    ]
    specs += [pl.BlockSpec(memory_space=pl.ANY)] * len(unread)

    def run(*refs):
        body(*refs[: len(args)], *refs[len(args) + len(unread) :])

    return pl.pallas_call(
        run,
        out_shape=[jax.ShapeDtypeStruct(*o) for o in outs],
        in_specs=specs,
        out_specs=[pl.BlockSpec(memory_space=pltpu.VMEM)] * len(outs),
        scratch_shapes=list(scratch),
        compiler_params=pltpu.CompilerParams(vmem_limit_bytes=vmem * 2**20),
        cost_estimate=pl.CostEstimate(flops=10**6, bytes_accessed=10**6, transcendentals=0),
    )(*args, *unread)


def pack_body(
    at, keys, values, queries, gates, decay, mix, keep, send, small, levels, sems
):
    core = at[0]
    mine = pl.ds(pl.multiple_of(core * 512, 512), 512)
    theirs = pl.ds(pl.multiple_of((1 - core) * 512, 512), 512)
    copies = [
        pltpu.make_async_copy(decay, small, sems.at[0]),
        pltpu.make_async_copy(mix, levels, sems.at[1]),
    ]
    for i, ref in enumerate((keys, values, queries, gates)):
        rows = pl.ds(i * 256, 256)
        for out, cols, n in ((send, theirs, 2), (keep, mine, 6)):
            copies.append(pltpu.make_async_copy(ref.at[:, cols], out.at[rows, :], sems.at[n + i]))
    for copy in copies:
        copy.start()
    for copy in copies[:2]:
        copy.wait()
    for out, low in ((keep, core == 0), (send, core == 1)):
        logs = [jnp.where(low, small[0:4], small[4:8])]
        logs += [jnp.where(low, levels[l, 0:4], levels[l, 4:8]) for l in range(8)]
        logs = jnp.concatenate(logs + [jnp.zeros((12, 256), F32)], axis=0)
        high = logs.astype(BF)
        out[LOGS : LOGS + 48, 0:256] = high
        out[LOGS : LOGS + 48, 256:512] = (logs - high.astype(F32)).astype(BF)
    for copy in copies[2:]:
        copy.wait()


def logs_of(block):
    tile = block[LOGS : LOGS + 48, :].astype(F32)
    return tile[:, 0:256] + tile[:, 256:512]


def ends_body(at, keep, got, pay, first):
    core = at[0]
    logs = jnp.concatenate([logs_of(keep)[0:4], logs_of(got)[0:4]], axis=0)
    after = (
        lax.broadcasted_iota(jnp.int32, (256, 256), 1)
        > lax.broadcasted_iota(jnp.int32, (256, 256), 0)
    ).astype(F32)
    scale = jnp.exp(exact(after, logs, NT))
    total = jnp.sum(logs, axis=1, keepdims=True)
    for h in range(4):
        cols = slice(h * 128, h * 128 + 128)
        end = []
        for i, ref in enumerate((keep, got)):
            scaled = ref[0:256, cols].astype(F32) * scale[:, 4 * i + h : 4 * i + h + 1]
            end.append(dot(scaled.astype(BF), ref[256:512, cols], TN))
        own_log, got_log = total[h : h + 1], total[4 + h : 5 + h]
        own_later = jnp.exp(jnp.where(core == 0, got_log, 0.0))
        got_later = jnp.exp(jnp.where(core == 0, 0.0, own_log))
        pay[h, 0:128, :] = (end[0] * own_later + end[1] * got_later).astype(BF)
        pay[h, 128:144, :] = tail(own_log + got_log)
        first[h, :, :] = jnp.where(core == 0, end[0], end[1]).astype(BF)


def blocks_of(got):
    s = [got[i, 0:128, :].astype(F32) for i in range(4)]
    t = [untail(got[i, 128:144, :]) for i in range(4)]
    pair = s[0] * jnp.exp(t[1]) + s[1]
    return s, t, pair


def send_whole(s, t, pair, pay):
    state = (pair * jnp.exp(t[2] + t[3]) + s[2] * jnp.exp(t[3]) + s[3]).astype(BF)
    log = tail(t[0] + t[1] + t[2] + t[3])
    for i in range(4):
        pay[i, 0:128, :] = state
        pay[i, 128:144, :] = log


def lower_states(s, t, pair, at):
    odd, upper = at % 2 == 1, at >= 2
    one = jnp.where(odd, jnp.where(upper, s[2], s[0]), 0.0)
    step = jnp.where(odd, jnp.where(upper, t[2], t[0]), 0.0)
    two = jnp.where(upper, pair * jnp.exp(step), 0.0)
    before = sum(jnp.where(at > i, t[i], 0.0) for i in range(3))
    return one, two, before


def near_body(at, near, pay, *messages):
    s, t, pair = blocks_of(near)
    send_whole(s, t, pair, pay)
    for k, message in enumerate(messages):
        one, two, before = lower_states(s, t, pair, at[1] ^ k)
        message[0:128, 0:128] = one.astype(BF)
        message[0:128, 128:256] = two.astype(BF)
        message[128:144, 0:128] = tail(before)
        message[128:144, 128:256] = jnp.zeros((16, 128), BF)


def far_body(at, far, pay, states, before_out):
    s, t, pair = blocks_of(far)
    send_whole(s, t, pair, pay)
    one, two, before = lower_states(s, t, pair, at[2])
    states[:, 0:128] = one.astype(BF)
    states[:, 128:256] = two.astype(BF)
    before_out[...] = jnp.broadcast_to(before, (8, 128))


def last_body(at, rows, before, far, message):
    one, two, _ = lower_states(*blocks_of(rows), at[3])
    earlier = jnp.exp(before[0:1, :])
    one, two = (one * earlier).astype(BF), (two * earlier).astype(BF)
    for i in range(4):
        message[i, :, 0:256] = far[...]
        message[i, :, 256:384] = one
        message[i, :, 384:512] = two


def place(s, core):
    at = core if s == 0 else 1 - core
    return at, pl.ds(pl.multiple_of(at * 256, 256), 256)


def own_body(at, keep, got, first, mixture, coef):
    core = at[0]
    rows = lax.broadcasted_iota(jnp.int32, (256, 256), 0)
    cols = lax.broadcasted_iota(jnp.int32, (256, 256), 1)
    lower = rows >= cols
    upto = lower.astype(F32)
    both = (logs_of(keep), logs_of(got))
    for s, ref in enumerate((keep, got)):
        second, here = place(s, core)
        logs = both[s]
        at_row = exact(logs[0:8], upto, NT)
        at_col = exact(upto, logs[0:8], NT)
        level = logs.T
        first_log = jnp.sum(both[1 - s][0:4], axis=1, keepdims=True)
        first_log = jnp.where(second == 1, first_log, 0.0)
        for h in range(4):
            hc = slice(h * 128, h * 128 + 128)
            q, kb, v = ref[512:768, hc], ref[0:256, hc], ref[256:512, hc]
            local = at_col[:, h : h + 1]
            gap = jnp.where(lower, local - at_row[h : h + 1, :], -1e30)
            weights = (dot(q, kb, NT) * jnp.exp(gap)).astype(BF)
            m = [level[:, 4 + 4 * l + h : 5 + 4 * l + h] for l in range(8)]
            total = dot(weights, v) * m[0]
            start = jnp.exp(local)
            total += dot(q, first[h]) * jnp.where(second == 1, start * m[1], 0.0)
            mixture[here, hc] = total
            start = start * jnp.exp(first_log[h : h + 1])
            for l in range(2, 8):
                coef[here, 6 * h + l - 2 : 6 * h + l - 1] = start * m[l]


def mix_body(at, keep, got, mixture, coef, n0, n1, n2, n3, mixed, later, near):
    for k, n in enumerate((n0, n1, n2, n3)):
        near[at[1] ^ k] = n[...]
    for h in range(4):
        before = jnp.exp(untail(near[h, 128:144, 0:128])[:, 0:1])
        hc = slice(h * 128, h * 128 + 128)
        for s, ref in enumerate((keep, got)):
            _, here = place(s, at[0])
            read = dot(ref[512:768, hc], near[h, 0:128, :])
            total = mixture[here, hc] + read[:, 0:128] * coef[here, 6 * h : 6 * h + 1]
            mixed[here, hc] = total + read[:, 128:256] * coef[here, 6 * h + 1 : 6 * h + 2]
            later[here, 4 * h : 4 * h + 4] = coef[here, 6 * h + 2 : 6 * h + 6] * before


def norm_body(at, keep, got, gain, mixture, coef, states, normed):
    core = at[0]
    for h in range(4):
        mine = pl.ds(pl.multiple_of(core * 512 + h * 128, 128), 128)
        hc = slice(h * 128, h * 128 + 128)
        for s, ref in enumerate((keep, got)):
            _, here = place(s, core)
            z = ref[768:1024, hc].astype(F32)
            total = mixture[here, hc]
            for l in range(0, 4, 2):
                read = dot(ref[512:768, hc], states[h, :, l * 128 : l * 128 + 256])
                total += read[:, 0:128] * coef[here, 4 * h + l : 4 * h + l + 1]
                total += read[:, 128:256] * coef[here, 4 * h + l + 1 : 4 * h + l + 2]
            gated = total * (z / (1.0 + jnp.exp(-z)))
            size = lax.rsqrt(jnp.mean(gated * gated, axis=1, keepdims=True) + 1e-05)
            normed[here, hc] = (gated * size * gain[:, mine].astype(F32)).astype(BF)


def project_body(other, at, b0, b1, b2, b3, w0, w1, w2, w3, out, left, right, sems):
    row = (1 - at[0]) if other else at[0]
    rows = pl.ds(pl.multiple_of(row * 256, 256), 256)
    copies = []
    for j, block in enumerate((b0, b1, b2, b3)):
        spot = (at[4] + 4 - j) % 4
        copies.append(pltpu.make_async_copy(block.at[rows], left.at[spot], sems.at[0, j]))
    for k, w in enumerate((w0, w1, w2, w3)):
        copies.append(pltpu.make_async_copy(w, right.at[k], sems.at[1, k]))
    for copy in copies:
        copy.start()
    for copy in copies[:4]:
        copy.wait()
    total = 0.0
    for k, turn in enumerate((0, 1, 3, 2)):
        copies[4 + k].wait()
        total += dot(left[(at[3] + turn) % 4], right[k].reshape(1024, 512), NT)
    out[...] = total.astype(out.dtype)


def project(at, blocks, rights, other):
    return call(
        functools.partial(project_body, other),
        [((256, 1024), BF if other else F32)],
        (at, *blocks, *rights),
        scratch=[
            pltpu.VMEM((4, 256, 512), BF),
            pltpu.VMEM((4, 16, 64, 512), BF),
            pltpu.SemaphoreType.DMA((2, 4)),
        ],
        hbm=range(1, 9),
        vmem=20,
    )[0]


def shift(value, axis, by):
    return lax.ppermute(value, axis, [(i, (i + by) % 4) for i in range(4)])


def shards(values, keys, queries, gates, log_decay, level_mix, norm_gain, weight):
    y, a, b, q, c, x = (lax.axis_index(n) for n in ("y", "a", NEAR, "q", "c", "x"))
    at = jnp.stack([c, b, a, y, x]).astype(jnp.int32)
    turned = []
    for other in range(2):
        half = lax.dynamic_slice_in_dim(weight, (c ^ other) * 512, 512, 1)
        perm = [
            ((s * 2 + k) * 4 + f, (f * 2 + (k ^ other)) * 4 + s)
            for s in range(4)
            for f in range(4)
            for k in range(2)
        ]
        turned.append(lax.ppermute(half, ("y", "c", "x"), perm))
    mine = jnp.where(c == 0, jnp.concatenate(turned), jnp.concatenate(turned[::-1]))
    block = ((ROWS, 512), BF)
    keep, send = call(
        pack_body,
        [block, block],
        (at, keys, values, queries, gates, log_decay, level_mix),
        scratch=[
            pltpu.VMEM((8, 256), F32),
            pltpu.VMEM((8, 8, 256), F32),
            pltpu.SemaphoreType.DMA((10,)),
        ],
        hbm=range(1, 7),
        vmem=60,
    )
    mine, send = lax.optimization_barrier((mine, send))
    theirs = lax.ppermute(mine, "q", [(0, 1), (1, 0)])

    got = swap(send)
    pay = ((4, 144, 128), BF)
    pay_b, first = call(ends_body, [pay, ((4, 128, 128), BF)], (at, keep, got))
    theirs, pay_b = lax.optimization_barrier((theirs, pay_b))
    mine = jnp.stack([jnp.where(q == 0, mine, theirs), jnp.where(q == 0, theirs, mine)])
    gathered = lax.all_gather(mine, ("a", "p"), axis=0, tiled=True)

    near = lax.all_to_all(pay_b, NEAR, 0, 0, tiled=True)
    pay_a, *near = call(near_body, [pay] + [((144, 256), BF)] * 4, (at, near))
    far = lax.all_to_all(pay_a, "a", 0, 0, tiled=True)
    near = near[:1] + [
        lax.ppermute(near[k], NEAR, [(i, i ^ k) for i in range(4)]) for k in (1, 2, 3)
    ]
    mixture, coef = call(
        own_body, [((512, 512), F32), ((512, 24), F32)], (at, keep, got, first)
    )
    pay_y, far, before = call(
        far_body,
        [pay, ((128, 256), BF), ((8, 128), F32)],
        (at, far),
        unread=near[1:],
    )
    rows = lax.all_to_all(pay_y, "y", 0, 0, tiled=True)
    (states,) = call(
        last_body, [((4, 128, 512), BF)], (at, rows, before, far), unread=(mixture,)
    )
    states = lax.all_to_all(states, NEAR, 0, 0, tiled=True)
    mixture, coef = call(
        mix_body,
        [((512, 512), F32), ((512, 16), F32)],
        (at, keep, got, mixture, coef, *near),
        scratch=[pltpu.VMEM((4, 144, 256), BF)],
    )
    _, gathered = lax.optimization_barrier((coef, gathered))
    rights = [gathered] + [shift(gathered, "y", 4 - k) for k in (1, 3, 2)]
    (normed,) = call(
        norm_body, [((512, 512), BF)], (at, keep, got, norm_gain[None], mixture, coef, states)
    )

    blocks = [normed] + [shift(normed, "x", j) for j in (1, 2, 3)]
    theirs = swap(project(at, blocks, rights, True))
    own = project(at, blocks, rights, False)
    return (own + theirs.astype(F32)).astype(BF)


def solution(mesh):
    fine = Mesh(mesh.devices.reshape(4, 4, 2, 2, 2, 4), SEQ + ("x",))
    return jax.shard_map(
        shards,
        mesh=fine,
        in_specs=(
            P(SEQ, "x"),
            P(SEQ, "x"),
            P(SEQ, "x"),
            P(SEQ, "x"),
            P("x", SEQ),
            P(None, "x", SEQ),
            P("x"),
            P(SEQ, "x"),
        ),
        out_specs=P(SEQ, "x"),
        check_vma=False,
    )
```

```python
import functools

import jax
import jax.numpy as jnp
from jax import lax
from jax.experimental import pallas as pl
from jax.experimental.pallas import tpu as pltpu
from jax.sharding import Mesh, PartitionSpec as P

BF = jnp.bfloat16
F32 = jnp.float32
SEQ = ("y", "a", "p", "q", "c")
NEAR = ("p", "q")
NT = (((1,), (1,)), ((), ()))
TN = (((0,), (0,)), ((), ()))
LOGS = 1024
ROWS = 1072


def swap(value):
    return lax.ppermute(value, "c", [(0, 1), (1, 0)])


def dot(left, right, dims=(((1,), (0,)), ((), ()))):
    return lax.dot_general(left, right, dims, preferred_element_type=F32)


def exact(left, right, dims):
    return lax.dot_general(
        left, right, dims, precision=lax.Precision.HIGHEST, preferred_element_type=F32
    )


def tail(log):
    high = log.astype(BF).astype(F32)
    middle = (log - high).astype(BF).astype(F32)
    low = log - high - middle
    row = lax.broadcasted_iota(jnp.int32, (16, 128), 0)
    return jnp.where(
        row == 0, high, jnp.where(row == 1, middle, jnp.where(row == 2, low, 0.0))
    ).astype(BF)


def untail(tile):
    return jnp.sum(tile.astype(F32), axis=0, keepdims=True)


def call(body, outs, args, unread=(), scratch=(), hbm=(), vmem=12):
    specs = [pl.BlockSpec(memory_space=pltpu.SMEM)]
    specs += [
        pl.BlockSpec(memory_space=pltpu.HBM if i in hbm else pltpu.VMEM)
        for i in range(1, len(args))
    ]
    specs += [pl.BlockSpec(memory_space=pl.ANY)] * len(unread)

    def run(*refs):
        body(*refs[: len(args)], *refs[len(args) + len(unread) :])

    return pl.pallas_call(
        run,
        out_shape=[jax.ShapeDtypeStruct(*o) for o in outs],
        in_specs=specs,
        out_specs=[pl.BlockSpec(memory_space=pltpu.VMEM)] * len(outs),
        scratch_shapes=list(scratch),
        compiler_params=pltpu.CompilerParams(vmem_limit_bytes=vmem * 2**20),
        cost_estimate=pl.CostEstimate(flops=10**6, bytes_accessed=10**6, transcendentals=0),
    )(*args, *unread)


def pack_body(
    at, keys, values, queries, gates, decay, mix, keep, send, small, levels, sems
):
    core = at[0]
    mine = pl.ds(pl.multiple_of(core * 512, 512), 512)
    theirs = pl.ds(pl.multiple_of((1 - core) * 512, 512), 512)
    copies = [
        pltpu.make_async_copy(decay, small, sems.at[0]),
        pltpu.make_async_copy(mix, levels, sems.at[1]),
    ]
    for i, ref in enumerate((keys, values, queries, gates)):
        rows = pl.ds(i * 256, 256)
        for out, cols, n in ((send, theirs, 2), (keep, mine, 6)):
            copies.append(pltpu.make_async_copy(ref.at[:, cols], out.at[rows, :], sems.at[n + i]))
    for copy in copies:
        copy.start()
    for copy in copies[:2]:
        copy.wait()
    for out, low in ((keep, core == 0), (send, core == 1)):
        logs = [jnp.where(low, small[0:4], small[4:8])]
        logs += [jnp.where(low, levels[l, 0:4], levels[l, 4:8]) for l in range(8)]
        logs = jnp.concatenate(logs + [jnp.zeros((12, 256), F32)], axis=0)
        high = logs.astype(BF)
        out[LOGS : LOGS + 48, 0:256] = high
        out[LOGS : LOGS + 48, 256:512] = (logs - high.astype(F32)).astype(BF)
    for copy in copies[2:]:
        copy.wait()


def logs_of(block):
    tile = block[LOGS : LOGS + 48, :].astype(F32)
    return tile[:, 0:256] + tile[:, 256:512]


def ends_body(at, keep, got, pay, first):
    core = at[0]
    logs = jnp.concatenate([logs_of(keep)[0:4], logs_of(got)[0:4]], axis=0)
    after = (
        lax.broadcasted_iota(jnp.int32, (256, 256), 1)
        > lax.broadcasted_iota(jnp.int32, (256, 256), 0)
    ).astype(F32)
    scale = jnp.exp(exact(after, logs, NT))
    total = jnp.sum(logs, axis=1, keepdims=True)
    for h in range(4):
        cols = slice(h * 128, h * 128 + 128)
        end = []
        for i, ref in enumerate((keep, got)):
            scaled = ref[0:256, cols].astype(F32) * scale[:, 4 * i + h : 4 * i + h + 1]
            end.append(dot(scaled.astype(BF), ref[256:512, cols], TN))
        own_log, got_log = total[h : h + 1], total[4 + h : 5 + h]
        own_later = jnp.exp(jnp.where(core == 0, got_log, 0.0))
        got_later = jnp.exp(jnp.where(core == 0, 0.0, own_log))
        pay[h, 0:128, :] = (end[0] * own_later + end[1] * got_later).astype(BF)
        pay[h, 128:144, :] = tail(own_log + got_log)
        first[h, :, :] = jnp.where(core == 0, end[0], end[1]).astype(BF)


def blocks_of(got):
    s = [got[i, 0:128, :].astype(F32) for i in range(4)]
    t = [untail(got[i, 128:144, :]) for i in range(4)]
    pair = s[0] * jnp.exp(t[1]) + s[1]
    return s, t, pair


def send_whole(s, t, pair, pay):
    state = (pair * jnp.exp(t[2] + t[3]) + s[2] * jnp.exp(t[3]) + s[3]).astype(BF)
    log = tail(t[0] + t[1] + t[2] + t[3])
    for i in range(4):
        pay[i, 0:128, :] = state
        pay[i, 128:144, :] = log


def lower_states(s, t, pair, at):
    odd, upper = at % 2 == 1, at >= 2
    one = jnp.where(odd, jnp.where(upper, s[2], s[0]), 0.0)
    step = jnp.where(odd, jnp.where(upper, t[2], t[0]), 0.0)
    two = jnp.where(upper, pair * jnp.exp(step), 0.0)
    before = sum(jnp.where(at > i, t[i], 0.0) for i in range(3))
    return one, two, before


def near_body(at, near, pay, *messages):
    s, t, pair = blocks_of(near)
    send_whole(s, t, pair, pay)
    for k, message in enumerate(messages):
        one, two, before = lower_states(s, t, pair, at[1] ^ k)
        message[0:128, 0:128] = one.astype(BF)
        message[0:128, 128:256] = two.astype(BF)
        message[128:144, 0:128] = tail(before)
        message[128:144, 128:256] = jnp.zeros((16, 128), BF)


def far_body(at, far, pay, states, before_out):
    s, t, pair = blocks_of(far)
    send_whole(s, t, pair, pay)
    one, two, before = lower_states(s, t, pair, at[2])
    states[:, 0:128] = one.astype(BF)
    states[:, 128:256] = two.astype(BF)
    before_out[...] = jnp.broadcast_to(before, (8, 128))


def last_body(at, rows, before, far, message):
    one, two, _ = lower_states(*blocks_of(rows), at[3])
    earlier = jnp.exp(before[0:1, :])
    one, two = (one * earlier).astype(BF), (two * earlier).astype(BF)
    for i in range(4):
        message[i, :, 0:256] = far[...]
        message[i, :, 256:384] = one
        message[i, :, 384:512] = two


def place(s, core):
    at = core if s == 0 else 1 - core
    return at, pl.ds(pl.multiple_of(at * 256, 256), 256)


def own_body(at, keep, got, first, mixture, coef):
    core = at[0]
    rows = lax.broadcasted_iota(jnp.int32, (256, 256), 0)
    cols = lax.broadcasted_iota(jnp.int32, (256, 256), 1)
    lower = rows >= cols
    upto = lower.astype(F32)
    both = (logs_of(keep), logs_of(got))
    for s, ref in enumerate((keep, got)):
        second, here = place(s, core)
        logs = both[s]
        at_row = exact(logs[0:8], upto, NT)
        at_col = exact(upto, logs[0:8], NT)
        level = logs.T
        first_log = jnp.sum(both[1 - s][0:4], axis=1, keepdims=True)
        first_log = jnp.where(second == 1, first_log, 0.0)
        for h in range(4):
            hc = slice(h * 128, h * 128 + 128)
            q, kb, v = ref[512:768, hc], ref[0:256, hc], ref[256:512, hc]
            local = at_col[:, h : h + 1]
            gap = jnp.where(lower, local - at_row[h : h + 1, :], -1e30)
            weights = (dot(q, kb, NT) * jnp.exp(gap)).astype(BF)
            m = [level[:, 4 + 4 * l + h : 5 + 4 * l + h] for l in range(8)]
            total = dot(weights, v) * m[0]
            start = jnp.exp(local)
            total += dot(q, first[h]) * jnp.where(second == 1, start * m[1], 0.0)
            mixture[here, hc] = total
            start = start * jnp.exp(first_log[h : h + 1])
            for l in range(2, 8):
                coef[here, 6 * h + l - 2 : 6 * h + l - 1] = start * m[l]


def mix_body(at, keep, got, mixture, coef, n0, n1, n2, n3, mixed, later, near):
    for k, n in enumerate((n0, n1, n2, n3)):
        near[at[1] ^ k] = n[...]
    for h in range(4):
        before = jnp.exp(untail(near[h, 128:144, 0:128])[:, 0:1])
        hc = slice(h * 128, h * 128 + 128)
        for s, ref in enumerate((keep, got)):
            _, here = place(s, at[0])
            read = dot(ref[512:768, hc], near[h, 0:128, :])
            total = mixture[here, hc] + read[:, 0:128] * coef[here, 6 * h : 6 * h + 1]
            mixed[here, hc] = total + read[:, 128:256] * coef[here, 6 * h + 1 : 6 * h + 2]
            later[here, 4 * h : 4 * h + 4] = coef[here, 6 * h + 2 : 6 * h + 6] * before


def norm_body(at, keep, got, gain, mixture, coef, states, normed):
    core = at[0]
    for h in range(4):
        mine = pl.ds(pl.multiple_of(core * 512 + h * 128, 128), 128)
        hc = slice(h * 128, h * 128 + 128)
        for s, ref in enumerate((keep, got)):
            _, here = place(s, core)
            z = ref[768:1024, hc].astype(F32)
            total = mixture[here, hc]
            for l in range(0, 4, 2):
                read = dot(ref[512:768, hc], states[h, :, l * 128 : l * 128 + 256])
                total += read[:, 0:128] * coef[here, 4 * h + l : 4 * h + l + 1]
                total += read[:, 128:256] * coef[here, 4 * h + l + 1 : 4 * h + l + 2]
            gated = total * (z / (1.0 + jnp.exp(-z)))
            size = lax.rsqrt(jnp.mean(gated * gated, axis=1, keepdims=True) + 1e-05)
            normed[here, hc] = (gated * size * gain[:, mine].astype(F32)).astype(BF)


def project_body(other, at, b0, b1, b2, b3, w0, w1, w2, w3, out, left, right, sems):
    row = (1 - at[0]) if other else at[0]
    rows = pl.ds(pl.multiple_of(row * 256, 256), 256)
    copies = [
        pltpu.make_async_copy(w, right.at[k], sems.at[k]) for k, w in enumerate((w0, w1, w2, w3))
    ]
    for copy in copies:
        copy.start()
    for j, block in enumerate((b0, b1, b2, b3)):
        left[(at[4] + 4 - j) % 4] = block[rows, :]
    total = 0.0
    for k, turn in enumerate((0, 1, 3, 2)):
        copies[k].wait()
        total += dot(left[(at[3] + turn) % 4], right[k].reshape(1024, 512), NT)
    out[...] = total.astype(out.dtype)


def project(at, blocks, rights, other):
    return call(
        functools.partial(project_body, other),
        [((256, 1024), BF if other else F32)],
        (at, *blocks, *rights),
        scratch=[
            pltpu.VMEM((4, 256, 512), BF),
            pltpu.VMEM((4, 16, 64, 512), BF),
            pltpu.SemaphoreType.DMA((4,)),
        ],
        hbm=range(5, 9),
        vmem=20,
    )[0]


def shift(value, axis, by):
    return lax.ppermute(value, axis, [(i, (i + by) % 4) for i in range(4)])


def shards(values, keys, queries, gates, log_decay, level_mix, norm_gain, weight):
    y, a, b, c, x = (lax.axis_index(n) for n in ("y", "a", NEAR, "c", "x"))
    at = jnp.stack([c, b, a, y, x]).astype(jnp.int32)
    turned = []
    for other in range(2):
        half = lax.dynamic_slice_in_dim(weight, (c ^ other) * 512, 512, 1)
        perm = [
            ((s * 2 + k) * 4 + f, (f * 2 + (k ^ other)) * 4 + s)
            for s in range(4)
            for f in range(4)
            for k in range(2)
        ]
        turned.append(lax.ppermute(half, ("y", "c", "x"), perm))
    mine = jnp.where(c == 0, jnp.concatenate(turned), jnp.concatenate(turned[::-1]))
    block = ((ROWS, 512), BF)
    keep, send = call(
        pack_body,
        [block, block],
        (at, keys, values, queries, gates, log_decay, level_mix),
        scratch=[
            pltpu.VMEM((8, 256), F32),
            pltpu.VMEM((8, 8, 256), F32),
            pltpu.SemaphoreType.DMA((10,)),
        ],
        hbm=range(1, 7),
        vmem=60,
    )
    mine, send = lax.optimization_barrier((mine, send))
    gathered = lax.all_gather(mine, ("a", "p", "q"))

    got = swap(send)
    pay = ((4, 144, 128), BF)
    pay_b, first = call(ends_body, [pay, ((4, 128, 128), BF)], (at, keep, got))
    near = lax.all_to_all(pay_b, NEAR, 0, 0, tiled=True)
    pay_a, *near = call(near_body, [pay] + [((144, 256), BF)] * 4, (at, near))
    far = lax.all_to_all(pay_a, "a", 0, 0, tiled=True)
    near = near[:1] + [
        lax.ppermute(near[k], NEAR, [(i, i ^ k) for i in range(4)]) for k in (1, 2, 3)
    ]
    mixture, coef = call(
        own_body, [((512, 512), F32), ((512, 24), F32)], (at, keep, got, first)
    )
    pay_y, far, before = call(
        far_body,
        [pay, ((128, 256), BF), ((8, 128), F32)],
        (at, far),
        unread=near[1:],
    )
    rows = lax.all_to_all(pay_y, "y", 0, 0, tiled=True)
    (states,) = call(
        last_body, [((4, 128, 512), BF)], (at, rows, before, far), unread=(mixture,)
    )
    states = lax.all_to_all(states, NEAR, 0, 0, tiled=True)
    mixture, coef = call(
        mix_body,
        [((512, 512), F32), ((512, 16), F32)],
        (at, keep, got, mixture, coef, *near),
        scratch=[pltpu.VMEM((4, 144, 256), BF)],
    )
    _, gathered = lax.optimization_barrier((coef, gathered))
    rights = [gathered] + [shift(gathered, "y", 4 - k) for k in (1, 3, 2)]
    (normed,) = call(
        norm_body, [((512, 512), BF)], (at, keep, got, norm_gain[None], mixture, coef, states)
    )

    blocks = [normed] + [shift(normed, "x", j) for j in (1, 2, 3)]
    theirs = swap(project(at, blocks, rights, True))
    own = project(at, blocks, rights, False)
    return (own + theirs.astype(F32)).astype(BF)


def solution(mesh):
    fine = Mesh(mesh.devices.reshape(4, 4, 2, 2, 2, 4), SEQ + ("x",))
    return jax.shard_map(
        shards,
        mesh=fine,
        in_specs=(
            P(SEQ, "x"),
            P(SEQ, "x"),
            P(SEQ, "x"),
            P(SEQ, "x"),
            P("x", SEQ),
            P(None, "x", SEQ),
            P("x"),
            P(SEQ, "x"),
        ),
        out_specs=P(SEQ, "x"),
        check_vma=False,
    )
```

```python
import functools

import jax
import jax.numpy as jnp
from jax import lax
from jax.experimental import pallas as pl
from jax.experimental.pallas import tpu as pltpu
from jax.sharding import Mesh, PartitionSpec as P

BF = jnp.bfloat16
F32 = jnp.float32
SEQ = ("y", "a", "p", "q", "c")
NEAR = ("p", "q")
NT = (((1,), (1,)), ((), ()))
TN = (((0,), (0,)), ((), ()))
LOGS = 512
ROWS = 560


def swap(value):
    return lax.ppermute(value, "c", [(0, 1), (1, 0)])


def dot(left, right, dims=(((1,), (0,)), ((), ()))):
    return lax.dot_general(left, right, dims, preferred_element_type=F32)


def exact(left, right, dims):
    return lax.dot_general(
        left, right, dims, precision=lax.Precision.HIGHEST, preferred_element_type=F32
    )


def tail(log):
    high = log.astype(BF).astype(F32)
    middle = (log - high).astype(BF).astype(F32)
    low = log - high - middle
    row = lax.broadcasted_iota(jnp.int32, (16, 128), 0)
    return jnp.where(
        row == 0, high, jnp.where(row == 1, middle, jnp.where(row == 2, low, 0.0))
    ).astype(BF)


def untail(tile):
    return jnp.sum(tile.astype(F32), axis=0, keepdims=True)


def call(body, outs, args, unread=(), scratch=(), hbm=(), vmem=12):
    specs = [pl.BlockSpec(memory_space=pltpu.SMEM)]
    specs += [
        pl.BlockSpec(memory_space=pltpu.HBM if i in hbm else pltpu.VMEM)
        for i in range(1, len(args))
    ]
    specs += [pl.BlockSpec(memory_space=pl.ANY)] * len(unread)

    def run(*refs):
        body(*refs[: len(args)], *refs[len(args) + len(unread) :])

    return pl.pallas_call(
        run,
        out_shape=[jax.ShapeDtypeStruct(*o) for o in outs],
        in_specs=specs,
        out_specs=[pl.BlockSpec(memory_space=pltpu.VMEM)] * len(outs),
        scratch_shapes=list(scratch),
        compiler_params=pltpu.CompilerParams(vmem_limit_bytes=vmem * 2**20),
        cost_estimate=pl.CostEstimate(flops=10**6, bytes_accessed=10**6, transcendentals=0),
    )(*args, *unread)


def pack_body(
    at, keys, values, decay, mix, keep, send, small, levels, sems
):
    core = at[0]
    mine = pl.ds(pl.multiple_of(core * 512, 512), 512)
    theirs = pl.ds(pl.multiple_of((1 - core) * 512, 512), 512)
    copies = [
        pltpu.make_async_copy(decay, small, sems.at[0]),
        pltpu.make_async_copy(mix, levels, sems.at[1]),
    ]
    for i, ref in enumerate((keys, values)):
        rows = pl.ds(i * 256, 256)
        for out, cols, n in ((send, theirs, 2), (keep, mine, 4)):
            copies.append(pltpu.make_async_copy(ref.at[:, cols], out.at[rows, :], sems.at[n + i]))
    for copy in copies:
        copy.start()
    for copy in copies[:2]:
        copy.wait()
    for out, low in ((keep, core == 0), (send, core == 1)):
        logs = [jnp.where(low, small[0:4], small[4:8])]
        logs += [jnp.where(low, levels[l, 0:4], levels[l, 4:8]) for l in range(8)]
        logs = jnp.concatenate(logs + [jnp.zeros((12, 256), F32)], axis=0)
        high = logs.astype(BF)
        out[LOGS : LOGS + 48, 0:256] = high
        out[LOGS : LOGS + 48, 256:512] = (logs - high.astype(F32)).astype(BF)
    for copy in copies[2:]:
        copy.wait()


def late_body(at, queries, gates, keep, send, sems):
    core = at[0]
    copies = []
    for i, ref in enumerate((queries, gates)):
        for n, (out, half) in enumerate(((send, 1 - core), (keep, core))):
            cols = pl.ds(pl.multiple_of(half * 512, 512), 512)
            rows = pl.ds(i * 256, 256)
            copies.append(pltpu.make_async_copy(ref.at[:, cols], out.at[rows, :], sems.at[i, n]))
    for copy in copies:
        copy.start()
    for copy in copies:
        copy.wait()


def logs_of(block):
    tile = block[LOGS : LOGS + 48, :].astype(F32)
    return tile[:, 0:256] + tile[:, 256:512]


def ends_body(at, keep, got, pay, first):
    core = at[0]
    logs = jnp.concatenate([logs_of(keep)[0:4], logs_of(got)[0:4]], axis=0)
    after = (
        lax.broadcasted_iota(jnp.int32, (256, 256), 1)
        > lax.broadcasted_iota(jnp.int32, (256, 256), 0)
    ).astype(F32)
    scale = jnp.exp(exact(after, logs, NT))
    total = jnp.sum(logs, axis=1, keepdims=True)
    for h in range(4):
        cols = slice(h * 128, h * 128 + 128)
        end = []
        for i, ref in enumerate((keep, got)):
            scaled = ref[0:256, cols].astype(F32) * scale[:, 4 * i + h : 4 * i + h + 1]
            end.append(dot(scaled.astype(BF), ref[256:512, cols], TN))
        own_log, got_log = total[h : h + 1], total[4 + h : 5 + h]
        own_later = jnp.exp(jnp.where(core == 0, got_log, 0.0))
        got_later = jnp.exp(jnp.where(core == 0, 0.0, own_log))
        pay[h, 0:128, :] = (end[0] * own_later + end[1] * got_later).astype(BF)
        pay[h, 128:144, :] = tail(own_log + got_log)
        first[h, :, :] = jnp.where(core == 0, end[0], end[1]).astype(BF)


def blocks_of(got):
    s = [got[i, 0:128, :].astype(F32) for i in range(4)]
    t = [untail(got[i, 128:144, :]) for i in range(4)]
    pair = s[0] * jnp.exp(t[1]) + s[1]
    return s, t, pair


def send_whole(s, t, pair, pay):
    state = (pair * jnp.exp(t[2] + t[3]) + s[2] * jnp.exp(t[3]) + s[3]).astype(BF)
    log = tail(t[0] + t[1] + t[2] + t[3])
    for i in range(4):
        pay[i, 0:128, :] = state
        pay[i, 128:144, :] = log


def lower_states(s, t, pair, at):
    odd, upper = at % 2 == 1, at >= 2
    one = jnp.where(odd, jnp.where(upper, s[2], s[0]), 0.0)
    step = jnp.where(odd, jnp.where(upper, t[2], t[0]), 0.0)
    two = jnp.where(upper, pair * jnp.exp(step), 0.0)
    before = sum(jnp.where(at > i, t[i], 0.0) for i in range(3))
    return one, two, before


def near_body(at, near, pay, *messages):
    s, t, pair = blocks_of(near)
    send_whole(s, t, pair, pay)
    for k, message in enumerate(messages):
        one, two, before = lower_states(s, t, pair, at[1] ^ k)
        message[0:128, 0:128] = one.astype(BF)
        message[0:128, 128:256] = two.astype(BF)
        message[128:144, 0:128] = tail(before)
        message[128:144, 128:256] = jnp.zeros((16, 128), BF)


def far_body(at, far, pay, states, before_out):
    s, t, pair = blocks_of(far)
    send_whole(s, t, pair, pay)
    one, two, before = lower_states(s, t, pair, at[2])
    states[:, 0:128] = one.astype(BF)
    states[:, 128:256] = two.astype(BF)
    before_out[...] = jnp.broadcast_to(before, (8, 128))


def last_body(at, rows, before, far, message):
    one, two, _ = lower_states(*blocks_of(rows), at[3])
    earlier = jnp.exp(before[0:1, :])
    one, two = (one * earlier).astype(BF), (two * earlier).astype(BF)
    for i in range(4):
        message[i, :, 0:256] = far[...]
        message[i, :, 256:384] = one
        message[i, :, 384:512] = two


def place(s, core):
    at = core if s == 0 else 1 - core
    return at, pl.ds(pl.multiple_of(at * 256, 256), 256)


def own_body(at, keep, got, keep_q, got_q, first, mixture, coef):
    core = at[0]
    rows = lax.broadcasted_iota(jnp.int32, (256, 256), 0)
    cols = lax.broadcasted_iota(jnp.int32, (256, 256), 1)
    lower = rows >= cols
    upto = lower.astype(F32)
    both = (logs_of(keep), logs_of(got))
    for s, ref in enumerate((keep, got)):
        second, here = place(s, core)
        logs = both[s]
        at_row = exact(logs[0:8], upto, NT)
        at_col = exact(upto, logs[0:8], NT)
        level = logs.T
        first_log = jnp.sum(both[1 - s][0:4], axis=1, keepdims=True)
        first_log = jnp.where(second == 1, first_log, 0.0)
        for h in range(4):
            hc = slice(h * 128, h * 128 + 128)
            q, kb, v = (keep_q, got_q)[s][0:256, hc], ref[0:256, hc], ref[256:512, hc]
            local = at_col[:, h : h + 1]
            gap = jnp.where(lower, local - at_row[h : h + 1, :], -1e30)
            weights = (dot(q, kb, NT) * jnp.exp(gap)).astype(BF)
            m = [level[:, 4 + 4 * l + h : 5 + 4 * l + h] for l in range(8)]
            total = dot(weights, v) * m[0]
            start = jnp.exp(local)
            total += dot(q, first[h]) * jnp.where(second == 1, start * m[1], 0.0)
            mixture[here, hc] = total
            start = start * jnp.exp(first_log[h : h + 1])
            for l in range(2, 8):
                coef[here, 6 * h + l - 2 : 6 * h + l - 1] = start * m[l]


def mix_body(at, keep, got, mixture, coef, n0, n1, n2, n3, mixed, later, near):
    for k, n in enumerate((n0, n1, n2, n3)):
        near[at[1] ^ k] = n[...]
    for h in range(4):
        before = jnp.exp(untail(near[h, 128:144, 0:128])[:, 0:1])
        hc = slice(h * 128, h * 128 + 128)
        for s, ref in enumerate((keep, got)):
            _, here = place(s, at[0])
            read = dot(ref[0:256, hc], near[h, 0:128, :])
            total = mixture[here, hc] + read[:, 0:128] * coef[here, 6 * h : 6 * h + 1]
            mixed[here, hc] = total + read[:, 128:256] * coef[here, 6 * h + 1 : 6 * h + 2]
            later[here, 4 * h : 4 * h + 4] = coef[here, 6 * h + 2 : 6 * h + 6] * before


def norm_body(at, keep, got, gain, mixture, coef, states, normed):
    core = at[0]
    for h in range(4):
        mine = pl.ds(pl.multiple_of(core * 512 + h * 128, 128), 128)
        hc = slice(h * 128, h * 128 + 128)
        for s, ref in enumerate((keep, got)):
            _, here = place(s, core)
            z = ref[256:512, hc].astype(F32)
            total = mixture[here, hc]
            for l in range(0, 4, 2):
                read = dot(ref[0:256, hc], states[h, :, l * 128 : l * 128 + 256])
                total += read[:, 0:128] * coef[here, 4 * h + l : 4 * h + l + 1]
                total += read[:, 128:256] * coef[here, 4 * h + l + 1 : 4 * h + l + 2]
            gated = total * (z / (1.0 + jnp.exp(-z)))
            size = lax.rsqrt(jnp.mean(gated * gated, axis=1, keepdims=True) + 1e-05)
            normed[here, hc] = (gated * size * gain[:, mine].astype(F32)).astype(BF)


def project_body(other, at, b0, b1, b2, b3, w0, w1, w2, w3, out, left, right, sems):
    row = (1 - at[0]) if other else at[0]
    rows = pl.ds(pl.multiple_of(row * 256, 256), 256)
    copies = [
        pltpu.make_async_copy(w, right.at[k], sems.at[k]) for k, w in enumerate((w0, w1, w2, w3))
    ]
    for copy in copies:
        copy.start()
    for j, block in enumerate((b0, b1, b2, b3)):
        left[(at[4] + 4 - j) % 4] = block[rows, :]
    total = 0.0
    for k, turn in enumerate((0, 1, 3, 2)):
        copies[k].wait()
        total += dot(left[(at[3] + turn) % 4], right[k].reshape(1024, 512), NT)
    out[...] = total.astype(out.dtype)


def project(at, blocks, rights, other):
    return call(
        functools.partial(project_body, other),
        [((256, 1024), BF if other else F32)],
        (at, *blocks, *rights),
        scratch=[
            pltpu.VMEM((4, 256, 512), BF),
            pltpu.VMEM((4, 16, 64, 512), BF),
            pltpu.SemaphoreType.DMA((4,)),
        ],
        hbm=range(5, 9),
        vmem=20,
    )[0]


def shift(value, axis, by):
    return lax.ppermute(value, axis, [(i, (i + by) % 4) for i in range(4)])


def shards(values, keys, queries, gates, log_decay, level_mix, norm_gain, weight):
    y, a, b, c, x = (lax.axis_index(n) for n in ("y", "a", NEAR, "c", "x"))
    at = jnp.stack([c, b, a, y, x]).astype(jnp.int32)
    turned = []
    for other in range(2):
        half = lax.dynamic_slice_in_dim(weight, (c ^ other) * 512, 512, 1)
        perm = [
            ((s * 2 + k) * 4 + f, (f * 2 + (k ^ other)) * 4 + s)
            for s in range(4)
            for f in range(4)
            for k in range(2)
        ]
        turned.append(lax.ppermute(half, ("y", "c", "x"), perm))
    mine = jnp.where(c == 0, jnp.concatenate(turned), jnp.concatenate(turned[::-1]))
    block = ((ROWS, 512), BF)
    keep, send = call(
        pack_body,
        [block, block],
        (at, keys, values, log_decay, level_mix),
        scratch=[
            pltpu.VMEM((8, 256), F32),
            pltpu.VMEM((8, 8, 256), F32),
            pltpu.SemaphoreType.DMA((6,)),
        ],
        hbm=range(1, 5),
        vmem=60,
    )
    mine, send = lax.optimization_barrier((mine, send))
    gathered = lax.all_gather(mine, ("a", "p", "q"))

    got = swap(send)
    pay = ((4, 144, 128), BF)
    pay_b, first = call(ends_body, [pay, ((4, 128, 128), BF)], (at, keep, got))
    queries, pay_b = lax.optimization_barrier((queries, pay_b))
    keep_q, send_q = call(
        late_body,
        [((512, 512), BF)] * 2,
        (at, queries, gates),
        scratch=[pltpu.SemaphoreType.DMA((2, 2))],
        hbm=(1, 2),
        vmem=60,
    )
    got_q = swap(send_q)
    near = lax.all_to_all(pay_b, NEAR, 0, 0, tiled=True)
    pay_a, *near = call(near_body, [pay] + [((144, 256), BF)] * 4, (at, near))
    far = lax.all_to_all(pay_a, "a", 0, 0, tiled=True)
    near = near[:1] + [
        lax.ppermute(near[k], NEAR, [(i, i ^ k) for i in range(4)]) for k in (1, 2, 3)
    ]
    mixture, coef = call(
        own_body, [((512, 512), F32), ((512, 24), F32)], (at, keep, got, keep_q, got_q, first)
    )
    pay_y, far, before = call(
        far_body,
        [pay, ((128, 256), BF), ((8, 128), F32)],
        (at, far),
        unread=near[1:],
    )
    rows = lax.all_to_all(pay_y, "y", 0, 0, tiled=True)
    (states,) = call(
        last_body, [((4, 128, 512), BF)], (at, rows, before, far), unread=(mixture,)
    )
    states = lax.all_to_all(states, NEAR, 0, 0, tiled=True)
    mixture, coef = call(
        mix_body,
        [((512, 512), F32), ((512, 16), F32)],
        (at, keep_q, got_q, mixture, coef, *near),
        scratch=[pltpu.VMEM((4, 144, 256), BF)],
    )
    _, gathered = lax.optimization_barrier((coef, gathered))
    rights = [gathered] + [shift(gathered, "y", 4 - k) for k in (1, 3, 2)]
    (normed,) = call(
        norm_body, [((512, 512), BF)], (at, keep_q, got_q, norm_gain[None], mixture, coef, states)
    )

    blocks = [normed] + [shift(normed, "x", j) for j in (1, 2, 3)]
    theirs = swap(project(at, blocks, rights, True))
    own = project(at, blocks, rights, False)
    return (own + theirs.astype(F32)).astype(BF)


def solution(mesh):
    fine = Mesh(mesh.devices.reshape(4, 4, 2, 2, 2, 4), SEQ + ("x",))
    return jax.shard_map(
        shards,
        mesh=fine,
        in_specs=(
            P(SEQ, "x"),
            P(SEQ, "x"),
            P(SEQ, "x"),
            P(SEQ, "x"),
            P("x", SEQ),
            P(None, "x", SEQ),
            P("x"),
            P(SEQ, "x"),
        ),
        out_specs=P(SEQ, "x"),
        check_vma=False,
    )
```
